32 devices in a mesh: dp: 8 (over z, y), rep: 4 (over x, core).
Axes of the slice: x: 2, y: 2, z: 4, core: 2. Of those that a mesh axis runs over, the one named last changes fastest.
Arguments:
- inputs: bfloat16 [512, 14, 14, 1024], P(('dp', 'rep')), may hold values from -6 to 6
- cotangent: bfloat16 [512, 7, 7, 2048], P(('dp', 'rep')), may hold values from -6 to 6
- image_group: int32 [512], P(('dp', 'rep')), may hold values from 0 to 2, as said below
- group_side: int32 [3], replicated, may hold values from 10 to 14, as said below
- group_width: int32 [3], replicated, may hold values from 2 to 4, as said below
- group_depth: int32 [3], replicated, may hold values from 0 to 1, as said below
- entry_reduce: bfloat16 [1024, 512], P('dp'), may hold values from -0.1875 to 0.1875
- entry_spatial: bfloat16 [9, 512, 512], P(None, 'dp'), may hold values from -0.09375 to 0.09375
- entry_expand: bfloat16 [512, 2048], P('dp'), may hold values from -0.25 to 0.25
- entry_project: bfloat16 [1024, 2048], P('dp'), may hold values from -0.1875 to 0.1875
- entry_norm_reduce: bfloat16 [2, 3, 512], P(None, None, 'dp'), may hold values from 0.099609375 to 1.8984375
- entry_norm_spatial: bfloat16 [2, 3, 512], P(None, None, 'dp'), may hold values from 0.099609375 to 1.8984375
- entry_norm_expand: bfloat16 [2, 3, 2048], P(None, None, 'dp'), may hold values from 0.099609375 to 1.8984375
- entry_norm_project: bfloat16 [2, 3, 2048], P(None, None, 'dp'), may hold values from 0.099609375 to 1.8984375
- inner_reduce: bfloat16 [2048, 512], P('dp'), may hold values from -0.125 to 0.125
- inner_spatial: bfloat16 [9, 512, 512], P(None, 'dp'), may hold values from -0.09375 to 0.09375
- inner_expand: bfloat16 [512, 2048], P('dp'), may hold values from -0.25 to 0.25
- inner_norm_reduce: bfloat16 [2, 3, 512], P(None, None, 'dp'), may hold values from 0.099609375 to 1.8984375
- inner_norm_spatial: bfloat16 [2, 3, 512], P(None, None, 'dp'), may hold values from 0.099609375 to 1.8984375
- inner_norm_expand: bfloat16 [2, 3, 2048], P(None, None, 'dp'), may hold values from 0.099609375 to 1.8984375
Outputs:
- result: bfloat16 [512, 7, 7, 2048], P(('dp', 'rep'))
- input_grad: float32 [512, 14, 14, 1024], P(('dp', 'rep'))
- entry_reduce_grad: float32 [1024, 512], P('dp')
- entry_spatial_grad: float32 [9, 512, 512], P(None, 'dp')
- entry_expand_grad: float32 [512, 2048], P('dp')
- entry_project_grad: float32 [1024, 2048], P('dp')
- entry_norm_reduce_grad: float32 [2, 3, 512], P(None, None, 'dp')
- entry_norm_spatial_grad: float32 [2, 3, 512], P(None, None, 'dp')
- entry_norm_expand_grad: float32 [2, 3, 2048], P(None, None, 'dp')
- entry_norm_project_grad: float32 [2, 3, 2048], P(None, None, 'dp')
- inner_reduce_grad: float32 [2048, 512], P('dp')
- inner_spatial_grad: float32 [9, 512, 512], P(None, 'dp')
- inner_expand_grad: float32 [512, 2048], P('dp')
- inner_norm_reduce_grad: float32 [2, 3, 512], P(None, None, 'dp')
- inner_norm_spatial_grad: float32 [2, 3, 512], P(None, None, 'dp')
- inner_norm_expand_grad: float32 [2, 3, 2048], P(None, None, 'dp')
The draws below stay inside these ranges and needn't reach their ends.
Inputs may be any that keep to these rules, and one draw needn't show every extreme that they name: `image_group`: the group of each image; every group has images. `group_side`: even sides, distinct between groups, one of them 14; a group's images fill the upper left side x side pixels and the rest of the map is padding. `group_width`: a group uses the first width * 128 inner channels; the groups' values are distinct. `group_depth`: 1 where a group's images pass the second block, 0 where they skip it; exactly one group skips.
All inputs are finite; a program needn't handle non-finite values.
Results may differ from the reference program's by a relative error of at most 0.02.
Values may be sent and summed in bfloat16 or wider, within the bound.
No kernel may reach another device: no remote copies, remote signals or barrier semaphores. Data moves between devices by JAX's collectives and lax.ppermute only.
A program may use at most 256 MiB of HBM per device.

```python
import jax
import jax.numpy as jnp
from jax import lax

CIN = 1024
MID = 512
COUT = 2048
SIDE = 14
GROUPS = 3
IMAGES = 512


def draw_image_group(key, part):
    key = jax.random.fold_in(key, 11)
    order_key, lower_key, upper_key = jax.random.split(key, 3)
    shuffled = jax.random.permutation(order_key, IMAGES).astype(jnp.int32)
    quarter = max(IMAGES // 4, 1)
    half = max(IMAGES // 2, quarter + 1)
    lower_cut = jax.random.randint(lower_key, (), 1, quarter + 1, dtype=jnp.int32)
    upper_cut = lower_cut + jax.random.randint(upper_key, (), quarter, half + 1, dtype=jnp.int32)
    return (shuffled >= lower_cut).astype(jnp.int32) + (shuffled >= upper_cut).astype(jnp.int32)


def draw_group_side(key, part):
    key = jax.random.fold_in(key, 12)
    shuffled = jax.random.permutation(key, GROUPS).astype(jnp.int32)
    return (SIDE - 2 * shuffled).astype(jnp.int32)


def draw_group_width(key, part):
    key = jax.random.fold_in(key, 13)
    shuffled = jax.random.permutation(key, GROUPS).astype(jnp.int32)
    return (4 - shuffled).astype(jnp.int32)


def draw_group_depth(key, part):
    key = jax.random.fold_in(key, 14)
    shuffled = jax.random.permutation(key, GROUPS).astype(jnp.int32)
    return (shuffled > 0).astype(jnp.int32)


def level_of(rng, dims, pieces, low, largest):
    factor_of = 1.0
    for axis_at, parts in pieces:
        draws = jax.random.uniform(jax.random.fold_in(jax.random.fold_in(rng, 6), axis_at), (parts,), jnp.float32, low / len(pieces), largest / len(pieces))
        factor_of = factor_of * jnp.repeat(jnp.exp(draws), dims[axis_at] // parts).reshape((-1,) + (1,) * (len(dims) - 1 - axis_at))
    return factor_of


def gaussian(rng, shape, scale, bound, pieces=(), kind=jnp.bfloat16):
    values = scale * jax.random.normal(rng, shape, jnp.float32)
    if pieces:
        values = values * level_of(rng, shape, pieces, -0.22, 0.18)
    return jnp.clip(values, -bound, bound).astype(kind)


def setup_inputs(seed: int = 0) -> dict:
    key_list = jax.random.split(jax.random.key(seed), 21)
    return {
        "inputs": gaussian(key_list[0], (IMAGES, SIDE, SIDE, CIN), 1.0, 6.0, ((0, 32),)),
        "cotangent": gaussian(key_list[1], (IMAGES, SIDE // 2, SIDE // 2, COUT), 1.0, 6.0, ((0, 32),)),
        "image_group": draw_image_group(jax.random.fold_in(key_list[20], 71), 0),
        "group_side": draw_group_side(jax.random.fold_in(key_list[20], 71), 0),
        "group_width": draw_group_width(jax.random.fold_in(key_list[20], 71), 0),
        "group_depth": draw_group_depth(jax.random.fold_in(key_list[20], 71), 0),
        "entry_reduce": gaussian(key_list[6], (CIN, MID), CIN ** -0.5, 0.1875, ((0, 8),)),
        "entry_spatial": gaussian(key_list[7], (9, MID, MID), (9 * MID) ** -0.5, 0.09375, ((1, 8),)),
        "entry_expand": gaussian(key_list[8], (MID, COUT), MID ** -0.5, 0.25, ((0, 8),)),
        "entry_project": gaussian(key_list[9], (CIN, COUT), CIN ** -0.5, 0.1875, ((0, 8),)),
        "entry_norm_reduce": jnp.clip(1.0 + 0.18 * jax.random.normal(key_list[10], (2, GROUPS, MID), jnp.float32), 0.099609375, 1.8984375).astype(jnp.bfloat16),
        "entry_norm_spatial": jnp.clip(1.0 + 0.18 * jax.random.normal(key_list[11], (2, GROUPS, MID), jnp.float32), 0.099609375, 1.8984375).astype(jnp.bfloat16),
        "entry_norm_expand": jnp.clip(1.0 + 0.18 * jax.random.normal(key_list[12], (2, GROUPS, COUT), jnp.float32), 0.099609375, 1.8984375).astype(jnp.bfloat16),
        "entry_norm_project": jnp.clip(1.0 + 0.18 * jax.random.normal(key_list[13], (2, GROUPS, COUT), jnp.float32), 0.099609375, 1.8984375).astype(jnp.bfloat16),
        "inner_reduce": gaussian(key_list[14], (COUT, MID), COUT ** -0.5, 0.125, ((0, 8),)),
        "inner_spatial": gaussian(key_list[15], (9, MID, MID), (9 * MID) ** -0.5, 0.09375, ((1, 8),)),
        "inner_expand": gaussian(key_list[16], (MID, COUT), MID ** -0.5, 0.25, ((0, 8),)),
        "inner_norm_reduce": jnp.clip(1.0 + 0.18 * jax.random.normal(key_list[17], (2, GROUPS, MID), jnp.float32), 0.099609375, 1.8984375).astype(jnp.bfloat16),
        "inner_norm_spatial": jnp.clip(1.0 + 0.18 * jax.random.normal(key_list[18], (2, GROUPS, MID), jnp.float32), 0.099609375, 1.8984375).astype(jnp.bfloat16),
        "inner_norm_expand": jnp.clip(1.0 + 0.18 * jax.random.normal(key_list[19], (2, GROUPS, COUT), jnp.float32), 0.099609375, 1.8984375).astype(jnp.bfloat16),
    }


@jax.custom_vjp
def low(v):
    return lax.optimization_barrier(v.astype(jnp.bfloat16)).astype(jnp.float32)

@jax.custom_vjp
def low_back(v):
    return v

def low_keep(v):
    return (low(v), None)

def low_pass(kept, grad):
    return (grad,)

def back_keep(v):
    return (v, None)

def back_low(kept, grad):
    return (low(grad),)
low.defvjp(low_keep, low_pass)
low_back.defvjp(back_keep, back_low)
EPSILON = 1e-05
HIGHEST = lax.Precision.HIGHEST

def pixel_mask(limits, extent):
    across = jnp.arange(extent, dtype=jnp.int32)
    inside = (across[None, :, None] < limits[:, None, None]) & (across[None, None, :] < limits[:, None, None])
    return inside.astype(jnp.float32)

def group_sums(values, onehot):
    per_image = lax.optimization_barrier(jnp.sum(values, axis=(1, 2)))
    return jnp.dot(onehot.T, per_image, precision=HIGHEST)

def spread_rows(group_table, onehot):
    return jnp.dot(onehot, group_table, precision=HIGHEST)[:, None, None, :]

def conv_single(source, weights):
    return jnp.einsum('nhwc,ck->nhwk', source, weights, precision=HIGHEST)

def conv_three(source, weights, stride):
    padded = jnp.pad(source, ((0, 0), (1, 1), (1, 1), (0, 0)))
    out_side = source.shape[1] // stride
    extent = stride * (out_side - 1) + 1
    accumulated = 0.0
    for offset in range(9):
        vertical = offset // 3
        lateral = offset % 3
        window = padded[:, vertical:vertical + extent:stride, lateral:lateral + extent:stride, :]
        accumulated = accumulated + jnp.einsum('nhwc,ck->nhwk', window, weights[offset], precision=HIGHEST)
    return accumulated

def normalize(values, affine, onehot, valid, counts):
    masked = values * valid[..., None]
    first_sum = group_sums(masked, onehot)
    second_sum = group_sums(masked * values, onehot)
    center = first_sum / counts[:, None]
    inverse = lax.rsqrt(second_sum / counts[:, None] - center * center + EPSILON)
    scale_table = affine[0] * inverse
    shift_table = affine[1] - center * scale_table
    return values * spread_rows(scale_table, onehot) + spread_rows(shift_table, onehot)

def reference(inputs, cotangent, image_group, group_side, group_width, group_depth, entry_reduce, entry_spatial, entry_expand, entry_project, entry_norm_reduce, entry_norm_spatial, entry_norm_expand, entry_norm_project, inner_reduce, inner_spatial, inner_expand, inner_norm_reduce, inner_norm_spatial, inner_norm_expand):
    onehot = (image_group[:, None] == jnp.arange(GROUPS, dtype=jnp.int32)[None, :]).astype(jnp.float32)
    totals = lax.optimization_barrier(jnp.sum(onehot, axis=0))
    side_real = group_side.astype(jnp.float32)
    half_real = (group_side // 2).astype(jnp.float32)
    counts_in = totals * side_real * side_real
    counts_out = totals * half_real * half_real
    own_side = group_side[image_group]
    own_width = group_width[image_group]
    own_gate = group_depth[image_group].astype(jnp.float32)[:, None, None, None]
    valid_in = pixel_mask(own_side, SIDE)
    valid_out = pixel_mask(own_side // 2, SIDE // 2)
    channel_keep = (jnp.arange(MID, dtype=jnp.int32)[None, :] < (own_width * MID // 4)[:, None]).astype(jnp.float32)
    mask_in = valid_in[..., None] * channel_keep[:, None, None, :]
    mask_out = valid_out[..., None] * channel_keep[:, None, None, :]
    edge_out = valid_out[..., None]

    def forward(source, entry_parts, inner_parts):
        reduced = low_back(conv_single(source, entry_parts[0]))
        first_act = low(jax.nn.gelu(normalize(reduced, entry_parts[4], onehot, valid_in, counts_in)) * mask_in)
        spatial = low_back(conv_three(first_act, entry_parts[1], 2))
        second_act = low(jax.nn.gelu(normalize(spatial, entry_parts[5], onehot, valid_out, counts_out)) * mask_out)
        expanded = low_back(conv_single(second_act, entry_parts[2]))
        projected = low_back(conv_single(source[:, ::2, ::2, :], entry_parts[3]))
        summed = normalize(expanded, entry_parts[6], onehot, valid_out, counts_out) + normalize(projected, entry_parts[7], onehot, valid_out, counts_out)
        middle = jax.nn.gelu(summed) * edge_out
        inner_reduced = low_back(conv_single(low(middle), inner_parts[0]))
        third_act = low(jax.nn.gelu(normalize(inner_reduced, inner_parts[3], onehot, valid_out, counts_out)) * mask_out)
        inner_mixed = low_back(conv_three(third_act, inner_parts[1], 1))
        fourth_act = low(jax.nn.gelu(normalize(inner_mixed, inner_parts[4], onehot, valid_out, counts_out)) * mask_out)
        inner_expanded = low_back(conv_single(fourth_act, inner_parts[2]))
        closed_value = jax.nn.gelu(normalize(inner_expanded, inner_parts[5], onehot, valid_out, counts_out) + middle) * edge_out
        return middle + own_gate * (closed_value - middle)
    source = inputs.astype(jnp.float32)
    entry_parts = (entry_reduce.astype(jnp.float32), entry_spatial.astype(jnp.float32), entry_expand.astype(jnp.float32), entry_project.astype(jnp.float32), entry_norm_reduce.astype(jnp.float32), entry_norm_spatial.astype(jnp.float32), entry_norm_expand.astype(jnp.float32), entry_norm_project.astype(jnp.float32))
    inner_parts = (inner_reduce.astype(jnp.float32), inner_spatial.astype(jnp.float32), inner_expand.astype(jnp.float32), inner_norm_reduce.astype(jnp.float32), inner_norm_spatial.astype(jnp.float32), inner_norm_expand.astype(jnp.float32))
    final_value, pullback = jax.vjp(forward, source, entry_parts, inner_parts)
    grad_source, grad_entry, grad_inner = pullback(cotangent.astype(jnp.float32))
    return (final_value.astype(jnp.bfloat16), grad_source, grad_entry[0], grad_entry[1], grad_entry[2], grad_entry[3], grad_entry[4], grad_entry[5], grad_entry[6], grad_entry[7], grad_inner[0], grad_inner[1], grad_inner[2], grad_inner[3], grad_inner[4], grad_inner[5])
```

```python
import functools

import jax
import jax.numpy as jnp
from jax import lax
from jax.experimental import pallas as pl
from jax.experimental.pallas import tpu as pltpu
from jax.sharding import PartitionSpec as P

EPSILON = 1e-05
AXES = ("dp", "rep")
BF = jnp.bfloat16
F32 = jnp.float32
GROUPS = 3
LANES = 512
VMEM = 56 * 1024 * 1024


def xor_swap(value, distance):
    count = lax.axis_size("dp") * lax.axis_size("rep")
    return lax.ppermute(value, AXES, [(d, d ^ distance) for d in range(count)])


def sum_everywhere(value):
    count = lax.axis_size("dp") * lax.axis_size("rep")
    bits = [1 << b for b in range(count.bit_length() - 1)]
    stages = [bits[:1]] + [bits[i : i + 2] for i in range(1, len(bits), 2)]
    for stage in stages:
        distances = [0]
        for bit in stage:
            distances = distances + [d | bit for d in distances]
        parts = [xor_swap(value, d) for d in distances[1:]]
        for part in parts:
            value = value + part
    return value


def gelu_parts(u):
    k = 0.7978845608028654
    square = u * u
    t = jnp.tanh(k * u * (1.0 + 0.044715 * square))
    half = 0.5 * (1.0 + t)
    slope = half + 0.5 * u * (1.0 - t * t) * (k + (3 * 0.044715 * k) * square)
    return u * half, slope


def dot(a, b):
    return lax.dot_general(a, b, (((1,), (0,)), ((), ())), preferred_element_type=F32)


def dot_nt(a, b):
    return lax.dot_general(a, b, (((1,), (1,)), ((), ())), preferred_element_type=F32)


def dot_tn(a, b):
    return lax.dot_general(a, b, (((0,), (0,)), ((), ())), preferred_element_type=F32)


def flat(field):
    return field.reshape(-1, field.shape[-1])


def whole(shape):
    return pl.BlockSpec(shape, lambda *_: (0,) * len(shape))


def along(shape, axis):
    return pl.BlockSpec(shape, lambda s: tuple(s if a == axis else 0 for a in range(len(shape))))


def call(kernel, name, steps, ins, outs, scratch=(), flops=0):
    arrays = [a for a, _ in ins]
    size = sum(a.size * a.dtype.itemsize for a in arrays)
    return pl.pallas_call(
        kernel,
        name=name,
        grid=(steps,),
        in_specs=[s for _, s in ins],
        out_specs=[s for _, _, s in outs],
        out_shape=[jax.ShapeDtypeStruct(shape, dtype) for shape, dtype, _ in outs],
        scratch_shapes=list(scratch),
        compiler_params=pltpu.CompilerParams(
            vmem_limit_bytes=VMEM, dimension_semantics=("arbitrary",)
        ),
        cost_estimate=pl.CostEstimate(flops=flops, bytes_accessed=size, transcendentals=0),
    )(*arrays)


def rows3(ref, first):
    return [ref[first + g : first + g + 1, :] for g in range(GROUPS)]


def spread(onehot, rows):
    total = onehot[0] * rows[0]
    for g in range(1, GROUPS):
        total = total + onehot[g] * rows[g]
    return total


def group_rows(onehot, *sums):
    rows = [
        jnp.sum(onehot[g] * image, axis=0, keepdims=True) for image in sums for g in range(GROUPS)
    ]
    return rows


def put_rows(ref, rows):
    for r, row in enumerate(rows):
        ref[r : r + 1, :] = row
    if len(rows) < ref.shape[0]:
        ref[len(rows) :, :] = jnp.zeros((ref.shape[0] - len(rows), ref.shape[1]), F32)


def moments(sums, counts):
    first, second, count = rows3(sums, 0), rows3(sums, GROUPS), rows3(counts, 0)
    center = [a / c for a, c in zip(first, count)]
    inverse = [lax.rsqrt(b / c - m * m + EPSILON) for b, c, m in zip(second, count, center)]
    return center, inverse


def forward_coefs(sums, table, counts, onehot):
    center, inverse = moments(sums, counts)
    scale = [a * i for a, i in zip(rows3(table, 0), inverse)]
    shift = [b - m * s for b, m, s in zip(rows3(table, GROUPS), center, scale)]
    return spread(onehot, scale), spread(onehot, shift)


def backward_coefs(sums, back, table, counts, onehot, gain_at=0):
    center, inverse = moments(sums, counts)
    count = rows3(counts, 0)
    factor = [a * i for a, i in zip(rows3(table, 0), inverse)]
    gain = [g / c for g, c in zip(rows3(back, gain_at), count)]
    bias = [b / c for b, c in zip(rows3(back, GROUPS), count)]
    on_z = [-f * i * g for f, i, g in zip(factor, inverse, gain)]
    on_one = [f * (m * i * g - b) for f, m, i, g, b in zip(factor, center, inverse, gain, bias)]
    return spread(onehot, factor), spread(onehot, on_z), spread(onehot, on_one)


def gain_rows(sums, counts, onehot, with_z, plain):
    center, inverse = moments(sums, counts)
    raw_z, raw = group_rows(onehot, with_z), group_rows(onehot, plain)
    return [i * (e - m * d) for i, e, m, d in zip(inverse, raw_z, center, raw)]


def inside(limits, row, count, step=1, start=0):
    column = lax.broadcasted_iota(jnp.int32, (count,) + limits.shape, 0) * step + start
    return (column < limits[None]) & (row < limits)[None]


def add_stats(values, mask, first, second):
    kept = jnp.where(mask, values, 0.0)
    return first + jnp.sum(kept, axis=0), second + jnp.sum(kept * values, axis=0)


def k_first(x, w, limits, onehot, count_row, z, sums, acc):
    step = pl.program_id(0)

    @pl.when(step == 0)
    def _():
        acc[...] = jnp.zeros_like(acc)

    rows, cols = x.shape[0], x.shape[1]
    values = dot(flat(x[...]), w[...]).reshape(rows, cols, x.shape[2], w.shape[1])
    z[...] = values.astype(BF)
    first, second = acc[0], acc[1]
    for r in range(rows):
        mask = inside(limits[...], step * rows + r, cols)
        first, second = add_stats(values[r], mask, first, second)
    acc[0] = first
    acc[1] = second

    @pl.when(step == pl.num_programs(0) - 1)
    def _():
        put_rows(sums, group_rows(onehot, first, second) + [count_row[0:1, :]])


def stats_of(field, limits, onehot, z, sums):
    side = field.shape[0]
    shape = field.shape[2:]

    def row(i, carry):
        values = field[i]
        z[i] = values.astype(BF)
        return add_stats(values, inside(limits[...], i, side), *carry)

    first, second = lax.fori_loop(
        0, side, row, (jnp.zeros(shape, F32), jnp.zeros(shape, F32))
    )
    put_rows(sums, group_rows(onehot, first, second))


def k_strided(x, w, limits, onehot, z, sums, acc):
    side = z.shape[0]
    acc[...] = dot(flat(x[:, 0, :, 0]), w[0]).reshape(acc.shape)
    stats_of(acc, limits, onehot, z, sums)


def k_entry_spatial(
    z1, in_sums, table, counts, counts_out, limits, limits_out, onehot, w,
    planes, slope, z2, sums, acc,
):
    step = pl.program_id(0)
    side = z2.shape[0]

    @pl.when(step == 0)
    def _():
        planes[1, :, 0] = jnp.zeros(planes.shape[1:2] + planes.shape[3:], BF)
        planes[:, 1, :, 0] = jnp.zeros(planes.shape[:1] + planes.shape[2:3] + planes.shape[4:], BF)

    scale, shift = forward_coefs(in_sums, table, counts, onehot)
    for a in range(2):
        for b in range(2):
            u = z1[0, a, :, b].astype(F32) * scale + shift
            act, grad = gelu_parts(u)
            mask = inside(limits[...], 2 * step + a, side, 2, b)
            planes[a, b, step + a, b : b + side] = jnp.where(mask, act, 0.0).astype(BF)
            slope[0, a, :, b] = jnp.where(mask, grad, 0.0).astype(BF)

    @pl.when(step == pl.num_programs(0) - 1)
    def _():
        for t in range(9):
            v, h = t // 3, t % 3
            rows = planes[(v + 1) % 2, (h + 1) % 2, v // 2 : v // 2 + side, h // 2 : h // 2 + side]
            part = dot(flat(rows), w[t]).reshape(acc.shape)
            if t == 0:
                acc[...] = part
            else:
                acc[...] += part
        stats_of(acc, limits_out, onehot, z2, sums)


def activate(z, coefs, limits, store):
    scale, shift = coefs
    side = z.shape[0]

    def row(i, carry):
        act, grad = gelu_parts(z[i].astype(F32) * scale + shift)
        mask = inside(limits[...], i, side)
        store(i, jnp.where(mask, act, 0.0).astype(BF), jnp.where(mask, grad, 0.0).astype(BF))
        return carry

    lax.fori_loop(0, side, row, 0)


def k_expand(z, in_sums, table, counts, keeps, limits, onehot, w, a, slope, z_out, sums, acc):
    @pl.when(pl.program_id(0) == 0)
    def _():
        def store(i, act, grad):
            a[i] = act
            slope[i] = grad

        activate(z, forward_coefs(in_sums, table, counts, onehot), keeps, store)

    acc[...] = dot(flat(a[...]), w[0]).reshape(acc.shape)
    stats_of(acc, limits, onehot, z_out, sums)


def k_middle(
    z3, zs, sums3, sums_s, table3, table_s, counts, limits, onehot, w,
    middle, slope, z4, sums, acc,
):
    step = pl.program_id(0)
    side = z3.shape[0]
    scale, shift = forward_coefs(sums3, table3, counts, onehot)
    scale_s, shift_s = forward_coefs(sums_s, table_s, counts, onehot)
    shift = shift + shift_s

    def row(i, carry):
        act, grad = gelu_parts(z3[i].astype(F32) * scale + zs[i].astype(F32) * scale_s + shift)
        mask = inside(limits[...], i, side)
        middle[i] = jnp.where(mask, act, 0.0).astype(BF)
        slope[i] = jnp.where(mask, grad, 0.0).astype(BF)
        return carry

    lax.fori_loop(0, side, row, 0)
    part = dot(flat(middle[...]), w[...]).reshape(acc.shape)

    @pl.when(step == 0)
    def _():
        acc[...] = part

    @pl.when(step > 0)
    def _():
        acc[...] += part

    @pl.when(step == pl.num_programs(0) - 1)
    def _():
        stats_of(acc, limits, onehot, z4, sums)


def clear_edges(padded):
    edge = jnp.zeros(padded.shape[1:], BF)
    last = padded.shape[0] - 1
    padded[0] = edge
    padded[last] = edge
    for i in range(1, last):
        padded[i, 0] = edge[0]
        padded[i, last] = edge[0]


def k_inner_spatial(z4, in_sums, table, counts, keeps, limits, onehot, w, padded, slope, z5, sums, acc):
    side = z4.shape[0]
    clear_edges(padded)

    def store(i, act, grad):
        padded[i + 1, 1 : 1 + side] = act
        slope[i] = grad

    activate(z4, forward_coefs(in_sums, table, counts, onehot), keeps, store)
    for t in range(9):
        v, h = t // 3, t % 3
        part = dot(flat(padded[v : v + side, h : h + side]), w[t]).reshape(acc.shape)
        if t == 0:
            acc[...] = part
        else:
            acc[...] += part
    stats_of(acc, limits, onehot, z5, sums)


def k_close(z6, in_sums, table, counts, limits, onehot, gate, middle, cot, result, du6, sums):
    side = z6.shape[0]
    scale, shift = forward_coefs(in_sums, table, counts, onehot)
    opened = gate[...]
    zero = jnp.zeros(opened.shape, F32)

    def row(i, carry):
        plain, with_z = carry
        z = z6[i].astype(F32)
        mid = middle[i].astype(F32)
        act, grad = gelu_parts(z * scale + shift + mid)
        mask = inside(limits[...], i, side)
        closed = jnp.where(mask, act, 0.0)
        result[i] = (mid + opened * (closed - mid)).astype(BF)
        du = jnp.where(mask, grad, 0.0) * opened * cot[i].astype(F32)
        du6[i] = du.astype(BF)
        return plain + jnp.sum(du, axis=0), with_z + jnp.sum(du * z, axis=0)

    plain, with_z = lax.fori_loop(0, side, row, (zero, zero))
    put_rows(
        sums,
        gain_rows(in_sums, counts, onehot, with_z, plain) + group_rows(onehot, plain),
    )


def finish_back(acc, slope, z, in_sums, counts, onehot, du_out, sums):
    zero = jnp.zeros(slope.shape[2:], F32)

    def row(i, carry):
        plain, with_z = carry
        du = acc[i] * slope[i].astype(F32)
        du_out[i] = du.astype(du_out.dtype)
        return plain + jnp.sum(du, axis=0), with_z + jnp.sum(du * z[i].astype(F32), axis=0)

    plain, with_z = lax.fori_loop(0, slope.shape[0], row, (zero, zero))
    put_rows(
        sums,
        gain_rows(in_sums, counts, onehot, with_z, plain) + group_rows(onehot, plain),
    )


def norm_back(du, z, coefs, limits, store):
    factor, on_z, on_one = coefs
    side = z.shape[0]

    def row(i, carry):
        dz = du[i].astype(F32) * factor + z[i].astype(F32) * on_z + on_one
        store(i, jnp.where(inside(limits[...], i, side), dz, 0.0).astype(BF))
        return carry

    lax.fori_loop(0, side, row, 0)


def k_back_expand(
    du6, z6, sums6, back6, table6, counts, limits, onehot, w, slope, z5, sums5,
    dz6, du5, sums, acc,
):
    step = pl.program_id(0)

    def store(i, dz):
        dz6[i] = dz

    norm_back(du6, z6, backward_coefs(sums6, back6, table6, counts, onehot), limits, store)
    part = dot_nt(flat(dz6[...]), w[0]).reshape(acc.shape)

    @pl.when(step == 0)
    def _():
        acc[...] = part

    @pl.when(step > 0)
    def _():
        acc[...] += part

    @pl.when(step == pl.num_programs(0) - 1)
    def _():
        finish_back(acc, slope, z5, sums5, counts, onehot, du5, sums)


def k_back_inner_spatial(
    du5, z5, sums5, back5, table5, counts, limits, onehot, w, slope, z4, sums4,
    dz5, du4, sums, padded, acc,
):
    side = z5.shape[0]
    clear_edges(padded)

    def store(i, dz):
        dz5[i] = dz
        padded[i + 1, 1 : 1 + side] = dz

    norm_back(du5, z5, backward_coefs(sums5, back5, table5, counts, onehot), limits, store)
    for t in range(9):
        v, h = t // 3, t % 3
        rows = padded[2 - v : 2 - v + side, 2 - h : 2 - h + side]
        part = dot_nt(flat(rows), w[t]).reshape(acc.shape)
        if t == 0:
            acc[...] = part
        else:
            acc[...] += part
    finish_back(acc, slope, z4, sums4, counts, onehot, du4, sums)


def k_back_middle(
    du4, z4, sums4, back4, table4, counts, limits, onehot, w, gate, cot, du6, slope3,
    z3, zs, sums3, sums_s, dz4, du3, sums, acc,
):
    side = z4.shape[0]

    @pl.when(pl.program_id(0) == 0)
    def _():
        def store(i, dz):
            dz4[i] = dz

        norm_back(du4, z4, backward_coefs(sums4, back4, table4, counts, onehot), limits, store)

    acc[...] = dot_nt(flat(dz4[...]), w[...]).reshape(acc.shape)
    shut = 1.0 - gate[...]
    zero = jnp.zeros(shut.shape, F32)

    def row(i, carry):
        plain, with_z3, with_zs = carry
        grad = shut * cot[i].astype(F32) + du6[i].astype(F32) + acc[i]
        du = grad * slope3[i].astype(F32)
        du3[i] = du.astype(BF)
        return (
            plain + jnp.sum(du, axis=0),
            with_z3 + jnp.sum(du * z3[i].astype(F32), axis=0),
            with_zs + jnp.sum(du * zs[i].astype(F32), axis=0),
        )

    plain, with_z3, with_zs = lax.fori_loop(0, side, row, (zero, zero, zero))
    put_rows(
        sums,
        gain_rows(sums3, counts, onehot, with_z3, plain)
        + group_rows(onehot, plain)
        + gain_rows(sums_s, counts, onehot, with_zs, plain),
    )


def k_back_entry_expand(
    du3, z3, zs, sums3, sums_s, back3, table3, table_s, counts, limits, onehot, w,
    slope, z2, sums2, dz3, dzs, du2, sums, acc,
):
    step = pl.program_id(0)
    side = z3.shape[0]
    factor, on_z, on_one = backward_coefs(sums3, back3, table3, counts, onehot)
    factor_s, on_zs, on_one_s = backward_coefs(
        sums_s, back3, table_s, counts, onehot, 2 * GROUPS
    )

    def row(i, carry):
        du = du3[i].astype(F32)
        mask = inside(limits[...], i, side)
        dz = du * factor + z3[i].astype(F32) * on_z + on_one
        dz3[i] = jnp.where(mask, dz, 0.0).astype(BF)
        dz = du * factor_s + zs[i].astype(F32) * on_zs + on_one_s
        dzs[i] = jnp.where(mask, dz, 0.0).astype(BF)
        return carry

    lax.fori_loop(0, side, row, 0)
    part = dot_nt(flat(dz3[...]), w[0]).reshape(acc.shape)

    @pl.when(step == 0)
    def _():
        acc[...] = part

    @pl.when(step > 0)
    def _():
        acc[...] += part

    @pl.when(step == pl.num_programs(0) - 1)
    def _():
        finish_back(acc, slope, z2, sums2, counts, onehot, du2, sums)


def k_back_strided(dzs, w, out):
    part = dot_nt(flat(dzs[...]), w[0]).reshape(out.shape)

    @pl.when(pl.program_id(0) == 0)
    def _():
        out[...] = part

    @pl.when(pl.program_id(0) > 0)
    def _():
        out[...] += part


def k_back_entry_spatial(
    du2, z2, sums2, back2, table2, counts, counts_in, limits, onehot, w, slope, z1, sums1,
    dz2, du1, sums, padded, total, acc,
):
    step = pl.program_id(0)
    side = z2.shape[0]

    @pl.when(step == 0)
    def _():
        total[...] = jnp.zeros_like(total)
        padded[...] = jnp.zeros_like(padded)

        def store(i, dz):
            dz2[i] = dz
            padded[i, 0:side] = dz

        norm_back(du2, z2, backward_coefs(sums2, back2, table2, counts, onehot), limits, store)

    steps = {0: [(1, 0)], 1: [(2, 0), (0, 1)]}
    for a in range(2):
        for b in range(2):

            @pl.when(step == 2 * a + b)
            def _():
                started = False
                for v, down in steps[a]:
                    for h, right in steps[b]:
                        rows = padded[down : down + side, right : right + side]
                        part = dot_nt(flat(rows), w[3 * v + h]).reshape(acc.shape)
                        if started:
                            acc[...] += part
                        else:
                            acc[...] = part
                        started = True

    def row(i, carry):
        plain, with_z = carry
        du = acc[i] * slope[i, 0, :, 0].astype(F32)
        du1[i, 0, :, 0] = du.astype(BF)
        z = z1[i, 0, :, 0].astype(F32)
        return plain + jnp.sum(du, axis=0), with_z + jnp.sum(du * z, axis=0)

    plain, with_z = lax.fori_loop(0, side, row, (total[0], total[1]))
    total[0] = plain
    total[1] = with_z

    @pl.when(step == pl.num_programs(0) - 1)
    def _():
        put_rows(
            sums,
            gain_rows(sums1, counts_in, onehot, with_z, plain) + group_rows(onehot, plain),
        )


def k_back_first(du1, z1, sums1, back1, table1, counts, limits, onehot, w, strided, dz1, dx):
    step = pl.program_id(0)
    rows, cols = du1.shape[0], du1.shape[1]
    factor, on_z, on_one = backward_coefs(sums1, back1, table1, counts, onehot)
    for r in range(rows):
        dz = du1[r].astype(F32) * factor + z1[r].astype(F32) * on_z + on_one
        mask = inside(limits[...], rows * step + r, cols)
        dz1[r] = jnp.where(mask, dz, 0.0).astype(BF)
    for r in range(rows):
        part = dot_nt(flat(dz1[r]), w[...]).reshape(dx.shape[1:])
        dx[r] = part
    for j in range(cols // 2):
        dx[0, 2 * j] += strided[0, j]


def k_taps(field, dz, out):
    t = pl.program_id(0)
    v, h = t // 3, t % 3
    side = dz.shape[0]
    rows = field[pl.ds(v, side), pl.ds(h, side)]
    out[0] = dot_tn(flat(rows), flat(dz[...])).astype(BF)


def k_taps_strided(planes, dz, out):
    t = pl.program_id(0)
    v, h = t // 3, t % 3
    side = dz.shape[0]
    rows = planes[(v + 1) % 2, (h + 1) % 2, pl.ds(v // 2, side), pl.ds(h // 2, side)]
    out[0] = dot_tn(flat(rows), flat(dz[...])).astype(BF)


def body(
    inputs,
    cotangent,
    image_group,
    group_side,
    group_width,
    group_depth,
    entry_reduce,
    entry_spatial,
    entry_expand,
    entry_project,
    entry_norm_reduce,
    entry_norm_spatial,
    entry_norm_expand,
    entry_norm_project,
    inner_reduce,
    inner_spatial,
    inner_expand,
    inner_norm_reduce,
    inner_norm_spatial,
    inner_norm_expand,
):
    images, full, _, wide = inputs.shape
    half = full // 2
    mid, out = entry_reduce.shape[1], entry_expand.shape[1]
    blocks = out // LANES
    shards, copies = lax.axis_size("dp"), lax.axis_size("rep")
    devices = shards * copies
    position, copy = lax.axis_index("dp"), lax.axis_index("rep")

    onehot_int = (image_group[None, :] == jnp.arange(GROUPS, dtype=jnp.int32)[:, None]).astype(
        jnp.int32
    )
    own_side = jnp.sum(onehot_int * group_side[:, None], axis=0)
    own_width = jnp.sum(onehot_int * group_width[:, None], axis=0)
    own_gate = jnp.sum(onehot_int * group_depth[:, None], axis=0)

    def lanes(vector):
        return jnp.broadcast_to(vector[:, None], (images, LANES))

    onehot = jnp.broadcast_to(
        onehot_int.astype(F32)[:, :, None], (GROUPS, images, LANES)
    )
    gate = lanes(own_gate).astype(F32)
    limits_in, limits_out = lanes(own_side), lanes(own_side // 2)
    kept = jnp.arange(mid, dtype=jnp.int32)[None, :] < (own_width * mid // 4)[:, None]
    keeps_in = jnp.where(kept, limits_in, 0)
    keeps_out = jnp.where(kept, limits_out, 0)

    def quarter(weights):
        rows = weights.shape[-2] // copies
        part = lax.dynamic_slice_in_dim(weights, copy * rows, rows, weights.ndim - 2)
        part = part.reshape((-1,) + part.shape[-2:])
        return jnp.concatenate(
            [part[..., i : i + LANES] for i in range(0, part.shape[-1], LANES)], axis=0
        )

    def gather_weights(weights):
        parts = [quarter(w) for w in weights]
        rows = jnp.concatenate([flat(p) for p in parts], axis=0)
        gathered = lax.all_gather(rows, AXES, axis=0, tiled=False)
        result, at = [], 0
        for p in parts:
            size = p.shape[0] * p.shape[1]
            field = gathered[:, at : at + size].reshape((devices,) + p.shape)
            result.append(field.transpose(1, 0, 2, 3).reshape(p.shape[0], -1, LANES))
            at += size
        return result

    def scatter_grads(grads, shapes):
        parts = []
        for g in grads:
            q = g.shape[1] // devices
            field = g.reshape(g.shape[0], devices, q, LANES).transpose(1, 0, 2, 3)
            parts.append(field.reshape(devices, -1, LANES))
        rows = jnp.concatenate(parts, axis=1).reshape(-1, LANES)
        own = lax.psum_scatter(rows, AXES, scatter_dimension=0, tiled=True)
        gathered = lax.all_gather(own, "rep", axis=0, tiled=False)
        result, at = [], 0
        for g, shape in zip(grads, shapes):
            t, q = g.shape[0], g.shape[1] // devices
            field = gathered[:, at : at + t * q].reshape(copies, t, q, LANES)
            if len(shape) == 3:
                field = field.transpose(1, 0, 2, 3)
            else:
                field = field.transpose(0, 2, 1, 3)
            result.append(field.reshape(shape).astype(F32))
            at += t * q
        return result

    tables_all = (
        entry_norm_reduce,
        entry_norm_spatial,
        entry_norm_expand,
        entry_norm_project,
        inner_norm_reduce,
        inner_norm_spatial,
        inner_norm_expand,
    )
    w_reduce = lax.all_gather(entry_reduce, "dp", axis=0, tiled=True)
    tables_flat = jnp.concatenate([t.reshape(2 * GROUPS, -1) for t in tables_all], axis=1)
    tables_flat = lax.all_gather(tables_flat, "dp", axis=0, tiled=False)
    tables, at = [], 0
    for t in tables_all:
        width = t.shape[2]
        field = tables_flat[:, :, at : at + width].transpose(1, 0, 2)
        tables.append(field.reshape(2 * GROUPS, shards * width).astype(F32))
        at += width
    w_spatial, w_expand, w_project, w_ireduce, w_ispatial, w_iexpand = gather_weights(
        [entry_spatial, entry_expand, entry_project, inner_reduce, inner_spatial, inner_expand]
    )
    w_ireduce = w_ireduce[0]

    x = inputs.transpose(1, 2, 0, 3)
    x_split = x.reshape(half, 2, half, 2, images, wide)
    cot = cotangent.transpose(1, 2, 0, 3)

    small = (half, half, images, LANES)
    large = (half, half, images, out)
    split = (half, 2, half, 2, images, LANES)
    rows_out, rows_in = half * half * images, full * full * images
    six = (2 * GROUPS, LANES)
    sums_block = (8, LANES)

    def fixed(array):
        return (array, whole(array.shape))

    def column(array):
        return (array, along(array.shape[:-1] + (LANES,), array.ndim - 1))

    def tap(array):
        return (array, along((1,) + array.shape[1:], 0))

    small_out = (small, BF, whole(small))
    large_out = (large, BF, along(small, 3))
    sums_out = ((8, LANES), F32, whole((8, LANES)))
    sums_wide = ((8, out), F32, along((8, LANES), 1))
    acc = pltpu.VMEM(small, F32)

    count_row = jnp.concatenate(
        [
            jnp.broadcast_to(jnp.sum(onehot_int[g]).astype(F32), (1, 128))
            for g in range(GROUPS)
        ]
        + [jnp.zeros((1, LANES - 128 * GROUPS), F32)],
        axis=1,
    )
    z1, sums1 = call(
        k_first, "first", half,
        [(x, along((2, full, images, wide), 0)), fixed(w_reduce), fixed(limits_in), fixed(onehot),
         fixed(count_row)],
        [((full, full, images, mid), BF, along((2, full, images, mid), 0)), sums_out],
        [pltpu.VMEM((2, images, mid), F32)], flops=2 * rows_in * wide * mid,
    )
    sums1 = sum_everywhere(sums1)
    totals = sums1[2 * GROUPS, 0 : 128 * GROUPS : 128]
    side_real = group_side.astype(F32)
    half_real = (group_side // 2).astype(F32)
    counts_in = jnp.broadcast_to((totals * side_real * side_real)[:, None], (GROUPS, LANES))
    counts = jnp.broadcast_to((totals * half_real * half_real)[:, None], (GROUPS, LANES))
    counts_in, counts = fixed(counts_in), fixed(counts)
    onehot, gate = fixed(onehot), fixed(gate)
    limits_in, limits_out = fixed(limits_in), fixed(limits_out)
    keeps_in, keeps_out = fixed(keeps_in), fixed(keeps_out)

    zs, sums_s = call(
        k_strided, "strided", blocks,
        [(x_split, whole((half, 1, half, 1, images, wide))), tap(w_project), limits_out, onehot],
        [large_out, sums_wide], [acc], flops=2 * rows_out * wide * out,
    )
    z1_split = z1.reshape(split)
    row_split = (1, 2, half, 2, images, LANES)
    planes_shape = (2, 2, half + 1, half + 1, images, mid)
    planes, slope1, z2, sums2 = call(
        k_entry_spatial, "entry_spatial", half,
        [(z1_split, along(row_split, 0)), fixed(sums1), fixed(tables[0]), counts_in, counts,
         keeps_in, limits_out, onehot, fixed(w_spatial)],
        [(planes_shape, BF, whole(planes_shape)), (split, BF, along(row_split, 0)), small_out,
         sums_out],
        [acc], flops=18 * rows_out * mid * mid,
    )
    sums2 = sum_everywhere(sums2)
    a2, slope2, z3, sums3 = call(
        k_expand, "expand", blocks,
        [fixed(z2), fixed(sums2), fixed(tables[1]), counts, keeps_out, limits_out, onehot,
         tap(w_expand)],
        [small_out, small_out, large_out, sums_wide], [acc], flops=2 * rows_out * mid * out,
    )
    joined = sum_everywhere(jnp.concatenate([sums3, sums_s], axis=1))
    sums3, sums_s = joined[:, :out], joined[:, out:]
    w_rows = (w_ireduce, along((LANES, mid), 0))
    middle, slope3, z4, sums4 = call(
        k_middle, "middle", blocks,
        [column(z3), column(zs), column(sums3), column(sums_s), column(tables[2]),
         column(tables[3]), counts, limits_out, onehot, w_rows],
        [large_out, large_out, small_out, sums_out], [acc], flops=2 * rows_out * mid * out,
    )
    sums4 = sum_everywhere(sums4)
    padded_shape = (half + 2, half + 2, images, mid)
    padded4, slope4, z5, sums5 = call(
        k_inner_spatial, "inner_spatial", 1,
        [fixed(z4), fixed(sums4), fixed(tables[4]), counts, keeps_out, limits_out, onehot,
         fixed(w_ispatial)],
        [(padded_shape, BF, whole(padded_shape)), small_out, small_out, sums_out], [acc],
        flops=18 * rows_out * mid * mid,
    )
    sums5 = sum_everywhere(sums5)
    a5, slope5, z6, sums6 = call(
        k_expand, "inner_expand", blocks,
        [fixed(z5), fixed(sums5), fixed(tables[5]), counts, keeps_out, limits_out, onehot,
         tap(w_iexpand)],
        [small_out, small_out, large_out, sums_wide], [acc], flops=2 * rows_out * mid * out,
    )
    sums6 = sum_everywhere(sums6)
    result, du6, back6 = call(
        k_close, "close", blocks,
        [column(z6), column(sums6), column(tables[6]), counts, limits_out, onehot, gate,
         column(middle), column(cot)],
        [large_out, large_out, sums_wide],
    )
    back6 = sum_everywhere(back6)
    dz6, du5, back5 = call(
        k_back_expand, "back_inner_expand", blocks,
        [column(du6), column(z6), column(sums6), column(back6), column(tables[6]), counts,
         limits_out, onehot, tap(w_iexpand), fixed(slope5), fixed(z5), fixed(sums5)],
        [large_out, (small, F32, whole(small)), sums_out], [acc],
        flops=2 * rows_out * mid * out,
    )
    back5 = sum_everywhere(back5)
    g_iexpand = weight_blocks(a5, dz6)
    dz5, du4, back4 = call(
        k_back_inner_spatial, "back_inner_spatial", 1,
        [fixed(du5), fixed(z5), fixed(sums5), fixed(back5), fixed(tables[5]), counts, limits_out,
         onehot, fixed(w_ispatial), fixed(slope4), fixed(z4), fixed(sums4)],
        [small_out, (small, F32, whole(small)), sums_out],
        [pltpu.VMEM(padded_shape, BF), acc], flops=18 * rows_out * mid * mid,
    )
    back4 = sum_everywhere(back4)
    taps_out = ((9, mid, mid), BF, along((1, mid, mid), 0))
    (g_ispatial,) = call(
        k_taps, "inner_spatial_grad", 9, [fixed(padded4), fixed(dz5)], [taps_out],
        flops=18 * rows_out * mid * mid,
    )
    dz4, du3, back3 = call(
        k_back_middle, "back_middle", blocks,
        [fixed(du4), fixed(z4), fixed(sums4), fixed(back4), fixed(tables[4]), counts, limits_out,
         onehot, w_rows, gate, column(cot), column(du6), column(slope3), column(z3), column(zs),
         column(sums3), column(sums_s)],
        [small_out, large_out, ((16, out), F32, along((16, LANES), 1))], [acc],
        flops=2 * rows_out * mid * out,
    )
    back3 = sum_everywhere(back3)
    g_ireduce = dot_tn(flat(middle), flat(dz4)).astype(BF)[None]
    inner_grads = scatter_grads(
        (g_ireduce, g_ispatial, g_iexpand),
        (inner_reduce.shape, inner_spatial.shape, inner_expand.shape),
    )
    dz3, dzs, du2, back2 = call(
        k_back_entry_expand, "back_entry_expand", blocks,
        [column(du3), column(z3), column(zs), column(sums3), column(sums_s), column(back3),
         column(tables[2]), column(tables[3]), counts, limits_out, onehot, tap(w_expand),
         fixed(slope2), fixed(z2), fixed(sums2)],
        [large_out, large_out, (small, F32, whole(small)), sums_out], [acc],
        flops=2 * rows_out * mid * out,
    )
    back2 = sum_everywhere(back2)
    strided_shape = (half, half, images, wide)
    (d_strided,) = call(
        k_back_strided, "back_strided", blocks, [column(dzs), tap(w_project)],
        [(strided_shape, F32, whole(strided_shape))], flops=2 * rows_out * wide * out,
    )
    g_expand = weight_blocks(a2, dz3)
    g_project = weight_blocks(x_split[:, 0, :, 0], dzs)
    plane = (half, 1, half, 1, images, LANES)

    def parity(array):
        return (array, pl.BlockSpec(plane, lambda s: (0, s // 2, 0, s % 2, 0, 0)))

    dz2, du1, back1 = call(
        k_back_entry_spatial, "back_entry_spatial", 4,
        [fixed(du2), fixed(z2), fixed(sums2), fixed(back2), fixed(tables[1]), counts, counts_in,
         limits_out, onehot, fixed(w_spatial), parity(slope1), parity(z1_split), fixed(sums1)],
        [small_out, (split, BF, parity(z1_split)[1]), sums_out],
        [pltpu.VMEM((half + 1, half + 1, images, mid), BF), pltpu.VMEM((2, images, mid), F32), acc],
        flops=18 * rows_out * mid * mid,
    )
    back1 = sum_everywhere(back1)
    (g_spatial,) = call(
        k_taps_strided, "entry_spatial_grad", 9, [fixed(planes), fixed(dz2)], [taps_out],
        flops=18 * rows_out * mid * mid,
    )
    two = (2, full, images, mid)
    dz1, d_inputs = call(
        k_back_first, "back_first", half,
        [(du1.reshape(z1.shape), along(two, 0)), (z1, along(two, 0)), fixed(sums1), fixed(back1),
         fixed(tables[0]), counts_in, limits_in, onehot, fixed(w_reduce),
         (d_strided, along((1, half, images, wide), 0))],
        [(z1.shape, BF, along(two, 0)),
         ((full, full, images, wide), F32, along((2, full, images, wide), 0))],
        flops=2 * rows_in * wide * mid,
    )
    g_reduce = dot_tn(flat(x), flat(dz1)).astype(BF)[None]
    entry_grads = scatter_grads(
        (g_reduce, g_spatial, g_expand, g_project),
        (entry_reduce.shape, entry_spatial.shape, entry_expand.shape, entry_project.shape),
    )

    def own_share(back, gain_at=0):
        width = back.shape[1] // shards
        own = lax.dynamic_slice_in_dim(back, position * width, width, 1)
        return jnp.stack([own[gain_at : gain_at + GROUPS], own[GROUPS : 2 * GROUPS]])

    return (
        result.transpose(2, 0, 1, 3),
        d_inputs.transpose(2, 0, 1, 3),
        *entry_grads,
        own_share(back1),
        own_share(back2),
        own_share(back3),
        own_share(back3, 2 * GROUPS),
        *inner_grads,
        own_share(back4),
        own_share(back5),
        own_share(back6),
    )


def weight_blocks(source, dz):
    grad = dot_tn(flat(source), flat(dz)).astype(BF)
    return jnp.stack([grad[:, i : i + LANES] for i in range(0, grad.shape[1], LANES)])


def solution(mesh):
    images = P(("dp", "rep"), None, None, None)
    rows = P("dp", None)
    taps = P(None, "dp", None)
    table = P(None, None, "dp")
    entry = (rows, taps, rows, rows, table, table, table, table)
    inner = (rows, taps, rows, table, table, table)
    return jax.shard_map(
        body,
        mesh=mesh,
        in_specs=(images, images, P(("dp", "rep")), P(), P(), P(), *entry, *inner),
        out_specs=(images, images, *entry, *inner),
        check_vma=False,
    )
```

```python
import functools

import jax
import jax.numpy as jnp
from jax import lax
from jax.experimental import pallas as pl
from jax.experimental.pallas import tpu as pltpu
from jax.sharding import PartitionSpec as P

EPSILON = 1e-05
AXES = ("dp", "rep")
BF = jnp.bfloat16
F32 = jnp.float32
GROUPS = 3
LANES = 512
VMEM = 22 * 1024 * 1024


def xor_swap(value, distance):
    count = lax.axis_size("dp") * lax.axis_size("rep")
    return lax.ppermute(value, AXES, [(d, d ^ distance) for d in range(count)])


def own_bit(bit):
    me = lax.axis_index("dp") * lax.axis_size("rep") + lax.axis_index("rep")
    return lax.shift_right_logical(me, bit) & 1


def index_bits():
    count = lax.axis_size("dp") * lax.axis_size("rep")
    return count.bit_length() - 1


def sum_stages(value, bits):
    for stage in [bits[i : i + 2] for i in range(0, len(bits), 2)]:
        distances = [0]
        for bit in stage:
            distances = distances + [d | (1 << bit) for d in distances]
        for part in [xor_swap(value, d) for d in distances[1:]]:
            value = value + part
    return value


def sum_near(value):
    if value.size <= 8192:
        return sum_stages(value + xor_swap(value, 1), [1, 2])
    width = value.shape[1] // 2
    own = own_bit(0)
    kept = lax.dynamic_slice_in_dim(value, own * width, width, 1)
    sent = lax.dynamic_slice_in_dim(value, (1 - own) * width, width, 1)
    return sum_stages(kept + xor_swap(sent, 1), [1, 2])


def sum_far(value, columns):
    value = sum_stages(value, list(range(3, index_bits())))
    if value.shape[1] == columns:
        return value
    return pair(value, xor_swap(value, 1), 0, 1)


def sum_everywhere(value):
    return sum_far(sum_near(value), value.shape[1])


def after(*values):
    return lax.optimization_barrier(values)


def pair(value, other, bit, axis):
    own = own_bit(bit)
    return jnp.concatenate(
        [jnp.where(own == 0, value, other), jnp.where(own == 0, other, value)], axis=axis
    )


def gather_bit(value, bit, axis):
    return pair(value, xor_swap(value, 1 << bit), bit, axis)


def gather_rows(part, others):
    count = index_bits()
    value = part.reshape((1,) * count + part.shape)
    for bit in list(range(3, count)) + [2, 1, 0]:
        value = gather_bit(value, bit, count - 1 - bit)
        if bit == 3:
            value, *others = after(value, *others)
    return value.reshape((-1,) + part.shape), others


def split_rows(value):
    total = value.shape[-2]
    cut = total // 32 * 16 or total // 2
    return value[..., :cut, :], value[..., cut:, :]


def is_line():
    return lax.axis_size("dp") == 8 and lax.axis_size("rep") == 4


def line_place():
    return lax.axis_index("dp") // 2


def line_shift(value, step, among=range(4)):
    pairs = [
        (p * 8 + i, (p + step) * 8 + i) for p in among for i in range(8) if 0 <= p + step < 4
    ]
    return lax.ppermute(value, AXES, pairs)


def line_gather_start(part):
    if not is_line():
        return (part,)
    return part, line_shift(part, 1), line_shift(part, -1)


def line_gather_end(parts):
    part = parts[0]
    if not is_line():
        count = index_bits()
        value = part.reshape((1,) * count + part.shape)
        for bit in range(3, count):
            value = gather_bit(value, bit, count - 1 - bit)
        return value.reshape((-1, 1, 1, 1) + part.shape)
    right, left = [parts[1]], [parts[2]]
    for _ in range(2):
        right.append(line_shift(right[-1], 1))
        left.append(line_shift(left[-1], -1))
    row = jnp.stack(right[::-1] + [part] + left)
    row = lax.dynamic_slice_in_dim(row, 3 - line_place(), 4, 0)
    return row.reshape((4, 1, 1, 1) + part.shape)


def added(parts):
    total = parts[0].astype(F32)
    for part in parts[1:]:
        total = total + part.astype(F32)
    return total


def halves(segments, bit, axis, other):
    index = own_bit(bit) ^ other
    return [[lax.dynamic_slice_in_dim(p, index, 1, axis) for p in s] for s in segments]


def halve_sent(segments, bit, axis):
    sent = [added(parts).astype(BF) for parts in halves(segments, bit, axis, 1)]
    return sent[0] if len(sent) == 1 else jnp.concatenate(sent, axis=-2)


def halve_end(segments, sent, bit, axis):
    got = xor_swap(sent, 1 << bit)
    result, at = [], 0
    for parts in halves(segments, bit, axis, 0):
        count = parts[0].shape[-2]
        result.append(parts + [lax.slice_in_dim(got, at, at + count, axis=got.ndim - 2)])
        at += count
    return result


def halve_bit(segments, bit, axis):
    return halve_end(segments, halve_sent(segments, bit, axis), bit, axis)


def cut_rows(segments):
    total = sum(s[0].shape[-2] for s in segments)
    cut = total // 32 * 16 or total // 2
    low, high, at = [], [], 0
    for s in segments:
        count = s[0].shape[-2]
        here = min(max(cut - at, 0), count)
        if here:
            low.append([p[..., :here, :] for p in s])
        if here < count:
            high.append([p[..., here:, :] for p in s])
        at += count
    return low, high


def flat_after(*values):
    leaves, tree = jax.tree.flatten(values)
    return jax.tree.unflatten(tree, lax.optimization_barrier(leaves))


def near_shape(value):
    return value.reshape((-1, 2, 2, 2) + value.shape[1:])


class LineScatter:
    def __init__(self, segments):
        self.segments = segments
        self.right = self.left = None

    def block(self, index):
        index = jnp.clip(index, 0, 3)
        parts = [
            added([lax.dynamic_index_in_dim(p, index, 0, keepdims=False) for p in s])
            for s in self.segments
        ]
        return jnp.concatenate(parts, axis=-2) if len(parts) > 1 else parts[0]

    def step(self, number):
        if not is_line():
            return
        place = line_place()
        to_right, to_left = self.block(4 - number + place), self.block(number - 4 + place)
        if self.right is not None:
            to_right, to_left = added([to_right, self.right]), added([to_left, self.left])
        self.right = line_shift(to_right.astype(BF), 1, range(number))
        self.left = line_shift(to_left.astype(BF), -1, range(4 - number, 4))

    def end(self):
        shape = self.segments[0][0].shape
        if is_line():
            result = added([self.block(line_place()), self.right, self.left])
            return result.reshape((-1, shape[-1])).astype(BF)
        count = index_bits() - 3
        values = [[p.reshape((2,) * count + p.shape[-2:]) for p in s] for s in self.segments]
        for step in range(count):
            values = halve_bit(values, step + 3, count - 1 - step)
        values = [added(s).reshape((-1, shape[-1])).astype(BF) for s in values]
        return jnp.concatenate(values, axis=0)

    def state(self):
        return [self.segments, self.right, self.left]

    def put(self, state):
        self.segments, self.right, self.left = state


def gather_copy(value, bit):
    return gather_bit(value, bit, 1 - bit)


def gelu_parts(u):
    k = 0.7978845608028654
    square = u * u
    half = 0.5 + 0.5 * jnp.tanh(u * (k + (0.044715 * k) * square))
    slope = half * (1.0 + u * (1.0 - half) * (2 * k + (6 * 0.044715 * k) * square))
    return u * half, slope


def dot(a, b):
    return lax.dot_general(a, b, (((1,), (0,)), ((), ())), preferred_element_type=F32)


def dot_nt(a, b):
    return lax.dot_general(a, b, (((1,), (1,)), ((), ())), preferred_element_type=F32)


def dot_tn(a, b):
    return lax.dot_general(a, b, (((0,), (0,)), ((), ())), preferred_element_type=F32)


def flat(field):
    return field.reshape(-1, field.shape[-1])


def whole(shape):
    return pl.BlockSpec(shape, lambda *_: (0,) * len(shape), pipeline_mode=pl.Buffered(1))


def along(shape, axis):
    return pl.BlockSpec(shape, lambda s: tuple(s if a == axis else 0 for a in range(len(shape))))


class Weight:
    def __init__(self, gathered, at, taps, q):
        if q % 16 == 0:
            self.array, self.at, self.taps, self.q = gathered, at, taps, q
        else:
            devices = gathered.shape[0]
            field = gathered[:, at : at + taps * q].reshape(devices, taps, q, LANES)
            field = field.transpose(1, 0, 2, 3).reshape(1, taps * devices * q, LANES)
            self.array, self.at, self.taps, self.q = field, 0, taps, devices * q

    def held(self):
        return pltpu.with_memory_space_constraint(self.array, pltpu.HBM)

    def spec(self, rows, index, mode=None):
        return pl.BlockSpec((self.array.shape[0], rows, LANES), index, pipeline_mode=mode)

    def chunk(self, at, count):
        rows = count * self.q
        place = at // rows
        return (self.held(), self.spec(rows, lambda *_: (0, place, 0), pl.Buffered(1)))

    def every(self):
        chunks, left, at = [], self.taps, self.at
        while left:
            count = left
            while at % (count * self.q):
                count -= 1
            chunks.append(self.chunk(at, count))
            at += count * self.q
            left -= count
        return chunks

    def moving(self):
        first = self.at // self.q
        return (self.held(), self.spec(self.q, lambda s: (0, first + s, 0)))

    def moving_all(self):
        return self.chunk(self.at, self.taps)

    def moving_rows(self, steps):
        devices = self.array.shape[0]
        if devices > 1:
            place = self.at // self.q
            return (
                self.held(),
                pl.BlockSpec((devices // steps, self.q, LANES), lambda s: (s, place, 0)),
            )
        return (self.held(), pl.BlockSpec((1, self.q // steps, LANES), lambda s: (0, s, 0)))


class Taps:
    def __init__(self, refs, total):
        self.refs = refs
        self.q = sum(r.shape[1] for r in refs) // total

    def __getitem__(self, t):
        row = t * self.q
        for ref in self.refs:
            if row < ref.shape[1]:
                return flat(ref[:, row : row + self.q])
            row -= ref.shape[1]


def call(kernel, name, steps, ins, outs, scratch=(), flops=0, into=None):
    groups = [i if isinstance(i, list) else [i] for i in ins]
    arrays = [a for g in groups for a, _ in g]
    size = sum(a.size * a.dtype.itemsize for a in arrays)

    def body(*refs):
        params, at = [], 0
        for i, g in zip(ins, groups):
            some = refs[at : at + len(g)]
            params.append(Taps(some, 9) if isinstance(i, list) else some[0])
            at += len(g)
        kernel(*params, *refs[at + (into is not None) :])

    given = [] if into is None else [into]

    return pl.pallas_call(
        body,
        name=name,
        grid=(steps,),
        in_specs=[s for g in groups for _, s in g] + [pl.BlockSpec(memory_space=pl.ANY)] * len(given),
        input_output_aliases={len(arrays): 0} if given else {},
        out_specs=[s for _, _, s in outs],
        out_shape=[jax.ShapeDtypeStruct(shape, dtype) for shape, dtype, _ in outs],
        scratch_shapes=list(scratch),
        compiler_params=pltpu.CompilerParams(
            vmem_limit_bytes=VMEM, dimension_semantics=("arbitrary",)
        ),
        cost_estimate=pl.CostEstimate(flops=flops, bytes_accessed=size, transcendentals=0),
    )(*arrays, *given)


def rows3(ref, first):
    return [ref[first + g : first + g + 1, :] for g in range(GROUPS)]


def spread(onehot, rows):
    total = onehot[0] * rows[0]
    for g in range(1, GROUPS):
        total = total + onehot[g] * rows[g]
    return total


def group_rows(onehot, *sums):
    rows = [
        jnp.sum(onehot[g] * image, axis=0, keepdims=True) for image in sums for g in range(GROUPS)
    ]
    return rows


def put_rows(ref, rows):
    for r, row in enumerate(rows):
        ref[r : r + 1, :] = row
    if len(rows) < ref.shape[0]:
        ref[len(rows) :, :] = jnp.zeros((ref.shape[0] - len(rows), ref.shape[1]), F32)


def moments(sums, counts):
    first, second, count = rows3(sums, 0), rows3(sums, GROUPS), rows3(counts, 0)
    center = [a / c for a, c in zip(first, count)]
    inverse = [lax.rsqrt(b / c - m * m + EPSILON) for b, c, m in zip(second, count, center)]
    return center, inverse


def forward_coefs(sums, table, counts, onehot):
    center, inverse = moments(sums, counts)
    scale = [a * i for a, i in zip(rows3(table, 0), inverse)]
    shift = [b - m * s for b, m, s in zip(rows3(table, GROUPS), center, scale)]
    return spread(onehot, scale), spread(onehot, shift)


def backward_coefs(sums, back, table, counts, onehot, gain_at=0):
    center, inverse = moments(sums, counts)
    count = rows3(counts, 0)
    factor = [a * i for a, i in zip(rows3(table, 0), inverse)]
    gain = [g / c for g, c in zip(rows3(back, gain_at), count)]
    bias = [b / c for b, c in zip(rows3(back, GROUPS), count)]
    on_z = [-f * i * g for f, i, g in zip(factor, inverse, gain)]
    on_one = [f * (m * i * g - b) for f, m, i, g, b in zip(factor, center, inverse, gain, bias)]
    return spread(onehot, factor), spread(onehot, on_z), spread(onehot, on_one)


def gain_rows(sums, counts, onehot, with_z, plain):
    center, inverse = moments(sums, counts)
    raw_z, raw = group_rows(onehot, with_z), group_rows(onehot, plain)
    return [i * (e - m * d) for i, e, m, d in zip(inverse, raw_z, center, raw)]


def inside(limits, row, count, step=1, start=0):
    column = lax.broadcasted_iota(jnp.int32, (count,) + limits.shape, 0) * step + start
    return (column < limits[None]) & (row < limits)[None]


def add_stats(values, mask, first, second):
    kept = jnp.where(mask, values, 0.0)
    return first + jnp.sum(kept, axis=0), second + jnp.sum(kept * values, axis=0)


def k_first(x, w, limits, onehot, count_row, z, sums, acc):
    step = pl.program_id(0)

    @pl.when(step == 0)
    def _():
        acc[...] = jnp.zeros_like(acc)

    rows, cols = x.shape[0], x.shape[1]
    values = dot(flat(x[...]), flat(w[...])).reshape(rows, cols, x.shape[2], LANES)
    z[...] = values.astype(BF)
    first, second = acc[0], acc[1]
    for r in range(rows):
        mask = inside(limits[...], step * rows + r, cols)
        first, second = add_stats(values[r], mask, first, second)
    acc[0] = first
    acc[1] = second

    @pl.when(step == pl.num_programs(0) - 1)
    def _():
        put_rows(sums, group_rows(onehot, first, second) + [count_row[0:1, :]])


def stats_of(field, limits, onehot, z, sums):
    side = field.shape[0]
    shape = field.shape[2:]

    def row(i, carry):
        values = field[i]
        z[i] = values.astype(BF)
        if limits is None:
            return carry[0] + jnp.sum(values, axis=0), carry[1] + jnp.sum(values * values, axis=0)
        return add_stats(values, inside(limits[...], i, side), *carry)

    first, second = lax.fori_loop(
        0, side, row, (jnp.zeros(shape, F32), jnp.zeros(shape, F32)), unroll=True
    )
    put_rows(sums, group_rows(onehot, first, second))


def k_strided(x, w, limits, onehot, z, sums, acc):
    side = z.shape[0]
    acc[...] = dot(flat(x[:, 0, :, 0]), flat(w[...])).reshape(acc.shape)
    stats_of(acc, limits, onehot, z, sums)


def k_entry_spatial(
    z1, in_sums, table, counts, counts_out, limits, limits_out, onehot, w,
    planes, slope, z2, sums, acc,
):
    step = pl.program_id(0)
    side = z2.shape[0]

    @pl.when(step == 0)
    def _():
        planes[1, :, 0] = jnp.zeros(planes.shape[1:2] + planes.shape[3:], BF)
        planes[:, 1, :, 0] = jnp.zeros(planes.shape[:1] + planes.shape[2:3] + planes.shape[4:], BF)

    scale, shift = forward_coefs(in_sums, table, counts, onehot)
    for a in range(2):
        for b in range(2):
            u = z1[0, a, :, b].astype(F32) * scale + shift
            act, grad = gelu_parts(u)
            mask = inside(limits[...], 2 * step + a, side, 2, b)
            planes[a, b, step + a, b : b + side] = jnp.where(mask, act, 0.0).astype(BF)
            slope[0, a, :, b] = jnp.where(mask, grad, 0.0).astype(BF)

    @pl.when(step == pl.num_programs(0) - 1)
    def _():
        for t in range(9):
            v, h = t // 3, t % 3
            rows = planes[(v + 1) % 2, (h + 1) % 2, v // 2 : v // 2 + side, h // 2 : h // 2 + side]
            part = dot(flat(rows), w[t]).reshape(acc.shape)
            if t == 0:
                acc[...] = part
            else:
                acc[...] += part
        stats_of(acc, limits_out, onehot, z2, sums)


def activate(z, coefs, limits, store):
    scale, shift = coefs
    side = z.shape[0]

    def row(i, carry):
        act, grad = gelu_parts(z[i].astype(F32) * scale + shift)
        mask = inside(limits[...], i, side)
        store(i, jnp.where(mask, act, 0.0).astype(BF), jnp.where(mask, grad, 0.0).astype(BF))
        return carry

    lax.fori_loop(0, side, row, 0, unroll=True)


def k_expand(z, in_sums, table, counts, keeps, onehot, w, a, slope, z_out, sums, acc):
    @pl.when(pl.program_id(0) == 0)
    def _():
        def store(i, act, grad):
            a[i] = act
            slope[i] = grad

        activate(z, forward_coefs(in_sums, table, counts, onehot), keeps, store)

    acc[...] = dot(flat(a[...]), flat(w[...])).reshape(acc.shape)
    stats_of(acc, None, onehot, z_out, sums)


def k_middle(
    z3, zs, sums3, sums_s, table3, table_s, counts, limits, onehot, w,
    middle, slope, z4, sums, acc,
):
    step = pl.program_id(0)
    side = z3.shape[0]
    scale, shift = forward_coefs(sums3, table3, counts, onehot)
    scale_s, shift_s = forward_coefs(sums_s, table_s, counts, onehot)
    shift = shift + shift_s

    def row(i, carry):
        act, grad = gelu_parts(z3[i].astype(F32) * scale + zs[i].astype(F32) * scale_s + shift)
        mask = inside(limits[...], i, side)
        middle[i] = jnp.where(mask, act, 0.0).astype(BF)
        slope[i] = jnp.where(mask, grad, 0.0).astype(BF)
        return carry

    lax.fori_loop(0, side, row, 0, unroll=True)
    part = dot(flat(middle[...]), flat(w[...])).reshape(acc.shape)

    @pl.when(step == 0)
    def _():
        acc[...] = part

    @pl.when(step > 0)
    def _():
        acc[...] += part

    @pl.when(step == pl.num_programs(0) - 1)
    def _():
        stats_of(acc, None, onehot, z4, sums)


def clear_edges(padded):
    edge = jnp.zeros(padded.shape[1:], BF)
    last = padded.shape[0] - 1
    padded[0] = edge
    padded[last] = edge
    for i in range(1, last):
        padded[i, 0] = edge[0]
        padded[i, last] = edge[0]


def k_inner_spatial(z4, in_sums, table, counts, keeps, limits, onehot, w, padded, slope, z5, sums, acc):
    side = z4.shape[0]
    clear_edges(padded)

    def store(i, act, grad):
        padded[i + 1, 1 : 1 + side] = act
        slope[i] = grad

    activate(z4, forward_coefs(in_sums, table, counts, onehot), keeps, store)
    for t in range(9):
        v, h = t // 3, t % 3
        part = dot(flat(padded[v : v + side, h : h + side]), w[t]).reshape(acc.shape)
        if t == 0:
            acc[...] = part
        else:
            acc[...] += part
    stats_of(acc, limits, onehot, z5, sums)


def k_close(z6, in_sums, table, counts, limits, onehot, gate, middle, cot, result, du6, sums):
    side = z6.shape[0]
    scale, shift = forward_coefs(in_sums, table, counts, onehot)
    opened = gate[...]
    zero = jnp.zeros(opened.shape, F32)

    def row(i, carry):
        plain, with_z = carry
        z = z6[i].astype(F32)
        mid = middle[i].astype(F32)
        act, grad = gelu_parts(z * scale + shift + mid)
        mask = inside(limits[...], i, side)
        closed = jnp.where(mask, act, 0.0)
        result[i] = (mid + opened * (closed - mid)).astype(BF)
        du = jnp.where(mask, grad, 0.0) * opened * cot[i].astype(F32)
        du6[i] = du.astype(BF)
        return plain + jnp.sum(du, axis=0), with_z + jnp.sum(du * z, axis=0)

    plain, with_z = lax.fori_loop(0, side, row, (zero, zero), unroll=True)
    put_rows(
        sums,
        gain_rows(in_sums, counts, onehot, with_z, plain) + group_rows(onehot, plain),
    )


def finish_back(acc, slope, z, in_sums, counts, onehot, du_out, sums):
    zero = jnp.zeros(slope.shape[2:], F32)

    def row(i, carry):
        plain, with_z = carry
        du = acc[i] * slope[i].astype(F32)
        du_out[i] = du.astype(du_out.dtype)
        return plain + jnp.sum(du, axis=0), with_z + jnp.sum(du * z[i].astype(F32), axis=0)

    plain, with_z = lax.fori_loop(0, slope.shape[0], row, (zero, zero), unroll=True)
    put_rows(
        sums,
        gain_rows(in_sums, counts, onehot, with_z, plain) + group_rows(onehot, plain),
    )


def norm_back(du, z, coefs, limits, store):
    factor, on_z, on_one = coefs
    side = z.shape[0]

    def row(i, carry):
        dz = du[i].astype(F32) * factor + z[i].astype(F32) * on_z + on_one
        store(i, jnp.where(inside(limits[...], i, side), dz, 0.0).astype(BF))
        return carry

    lax.fori_loop(0, side, row, 0, unroll=True)


def k_back_expand(
    du6, z6, sums6, back6, table6, counts, limits, onehot, w, slope, z5, sums5,
    dz6, du5, sums, acc,
):
    step = pl.program_id(0)

    def store(i, dz):
        dz6[i] = dz

    norm_back(du6, z6, backward_coefs(sums6, back6, table6, counts, onehot), limits, store)
    part = dot_nt(flat(dz6[...]), flat(w[...])).reshape(acc.shape)

    @pl.when(step == 0)
    def _():
        acc[...] = part

    @pl.when(step > 0)
    def _():
        acc[...] += part

    @pl.when(step == pl.num_programs(0) - 1)
    def _():
        finish_back(acc, slope, z5, sums5, counts, onehot, du5, sums)


def k_back_inner_spatial(
    du5, z5, sums5, back5, table5, counts, limits, onehot, w, slope, z4, sums4,
    dz5, du4, sums, padded, acc,
):
    side = z5.shape[0]
    clear_edges(padded)

    def store(i, dz):
        dz5[i] = dz
        padded[i + 1, 1 : 1 + side] = dz

    norm_back(du5, z5, backward_coefs(sums5, back5, table5, counts, onehot), limits, store)
    for t in range(9):
        v, h = t // 3, t % 3
        rows = padded[2 - v : 2 - v + side, 2 - h : 2 - h + side]
        part = dot_nt(flat(rows), w[t]).reshape(acc.shape)
        if t == 0:
            acc[...] = part
        else:
            acc[...] += part
    finish_back(acc, slope, z4, sums4, counts, onehot, du4, sums)


def k_back_middle(
    du4, z4, sums4, back4, table4, counts, limits, onehot, w, gate, cot, du6, slope3,
    z3, zs, sums3, sums_s, dz4, du3, sums, acc,
):
    side = z4.shape[0]

    @pl.when(pl.program_id(0) == 0)
    def _():
        def store(i, dz):
            dz4[i] = dz

        norm_back(du4, z4, backward_coefs(sums4, back4, table4, counts, onehot), limits, store)

    acc[...] = dot_nt(flat(dz4[...]), flat(w[...])).reshape(acc.shape)
    shut = 1.0 - gate[...]
    zero = jnp.zeros(shut.shape, F32)

    def row(i, carry):
        plain, with_z3, with_zs = carry
        grad = shut * cot[i].astype(F32) + du6[i].astype(F32) + acc[i]
        du = grad * slope3[i].astype(F32)
        du3[i] = du.astype(BF)
        return (
            plain + jnp.sum(du, axis=0),
            with_z3 + jnp.sum(du * z3[i].astype(F32), axis=0),
            with_zs + jnp.sum(du * zs[i].astype(F32), axis=0),
        )

    plain, with_z3, with_zs = lax.fori_loop(0, side, row, (zero, zero, zero), unroll=True)
    put_rows(
        sums,
        gain_rows(sums3, counts, onehot, with_z3, plain)
        + group_rows(onehot, plain)
        + gain_rows(sums_s, counts, onehot, with_zs, plain),
    )


def k_back_entry_expand(
    du3, z3, zs, sums3, sums_s, back3, table3, table_s, counts, limits, onehot, w,
    slope, z2, sums2, dz3, dzs, du2, sums, acc,
):
    step = pl.program_id(0)
    side = z3.shape[0]
    factor, on_z, on_one = backward_coefs(sums3, back3, table3, counts, onehot)
    factor_s, on_zs, on_one_s = backward_coefs(
        sums_s, back3, table_s, counts, onehot, 2 * GROUPS
    )

    def row(i, carry):
        du = du3[i].astype(F32)
        mask = inside(limits[...], i, side)
        dz = du * factor + z3[i].astype(F32) * on_z + on_one
        dz3[i] = jnp.where(mask, dz, 0.0).astype(BF)
        dz = du * factor_s + zs[i].astype(F32) * on_zs + on_one_s
        dzs[i] = jnp.where(mask, dz, 0.0).astype(BF)
        return carry

    lax.fori_loop(0, side, row, 0, unroll=True)
    part = dot_nt(flat(dz3[...]), flat(w[...])).reshape(acc.shape)

    @pl.when(step == 0)
    def _():
        acc[...] = part

    @pl.when(step > 0)
    def _():
        acc[...] += part

    @pl.when(step == pl.num_programs(0) - 1)
    def _():
        finish_back(acc, slope, z2, sums2, counts, onehot, du2, sums)


def k_back_strided(dzs, w, out):
    part = dot_nt(flat(dzs[...]), flat(w[...])).reshape(out.shape)

    @pl.when(pl.program_id(0) == 0)
    def _():
        out[...] = part

    @pl.when(pl.program_id(0) > 0)
    def _():
        out[...] += part


def k_back_entry_spatial(
    du2, z2, sums2, back2, table2, counts, counts_in, limits, onehot, w, slope, z1, sums1,
    dz2, du1, sums, padded, total, acc,
):
    step = pl.program_id(0)
    side = z2.shape[0]

    @pl.when(step == 0)
    def _():
        total[...] = jnp.zeros_like(total)
        padded[...] = jnp.zeros_like(padded)

        def store(i, dz):
            dz2[i] = dz
            padded[i, 0:side] = dz

        norm_back(du2, z2, backward_coefs(sums2, back2, table2, counts, onehot), limits, store)

    steps = {0: [(1, 0)], 1: [(2, 0), (0, 1)]}
    for a in range(2):
        for b in range(2):

            @pl.when(step == 2 * a + b)
            def _():
                started = False
                for v, down in steps[a]:
                    for h, right in steps[b]:
                        rows = padded[down : down + side, right : right + side]
                        part = dot_nt(flat(rows), w[3 * v + h]).reshape(acc.shape)
                        if started:
                            acc[...] += part
                        else:
                            acc[...] = part
                        started = True

    def row(i, carry):
        plain, with_z = carry
        du = acc[i] * slope[i, 0, :, 0].astype(F32)
        du1[i, 0, :, 0] = du.astype(BF)
        z = z1[i, 0, :, 0].astype(F32)
        return plain + jnp.sum(du, axis=0), with_z + jnp.sum(du * z, axis=0)

    plain, with_z = lax.fori_loop(0, side, row, (total[0], total[1]), unroll=True)
    total[0] = plain
    total[1] = with_z

    @pl.when(step == pl.num_programs(0) - 1)
    def _():
        put_rows(
            sums,
            gain_rows(sums1, counts_in, onehot, with_z, plain) + group_rows(onehot, plain),
        )


def k_back_first(du1, z1, sums1, back1, table1, counts, limits, onehot, x, dz1, grad, acc):
    step = pl.program_id(0)
    rows, cols = du1.shape[0], du1.shape[1]
    factor, on_z, on_one = backward_coefs(sums1, back1, table1, counts, onehot)
    for r in range(rows):
        dz = du1[r].astype(F32) * factor + z1[r].astype(F32) * on_z + on_one
        mask = inside(limits[...], rows * step + r, cols)
        dz1[r] = jnp.where(mask, dz, 0.0).astype(BF)
    part = dot_tn(flat(x[...]), flat(dz1[...]))

    @pl.when(step == 0)
    def _():
        acc[...] = part

    @pl.when(step > 0)
    def _():
        acc[...] += part

    @pl.when(step == pl.num_programs(0) - 1)
    def _():
        grad[...] = acc[...].astype(BF).reshape(grad.shape)


def k_input_grad(dz1, w, strided, dx):
    rows, cols = dz1.shape[0], dz1.shape[1]
    weights = flat(w[...])
    for r in range(rows):
        dx[r] = dot_nt(flat(dz1[r]), weights).reshape(dx.shape[1:])
    for j in range(cols // 2):
        dx[0, 2 * j] += strided[0, j]


def k_grad(source, dz, out):
    out[...] = dot_tn(flat(source[...]), flat(dz[...])).astype(BF).reshape(out.shape)


def k_grad_columns(source, dz, out, turned):
    @pl.when(pl.program_id(0) == 0)
    def _():
        turned[...] = flat(source[...]).T

    out[...] = dot(turned[...], flat(dz[...])).astype(BF).reshape(out.shape)


def k_grad_strided(x, dz, out, turned):
    k_grad_columns(x.at[:, 0, :, 0], dz, out, turned)


def k_taps(field, dz, out):
    t = pl.program_id(0)
    v, h = t // 3, t % 3
    side = dz.shape[0]
    rows = field[pl.ds(v, side), pl.ds(h, side)]
    out[...] = dot_tn(flat(rows), flat(dz[...])).astype(BF).reshape(out.shape)


def k_taps_strided(planes, dz, out):
    t = pl.program_id(0)
    v, h = t // 3, t % 3
    side = dz.shape[0]
    rows = planes[(v + 1) % 2, (h + 1) % 2, pl.ds(v // 2, side), pl.ds(h // 2, side)]
    out[...] = dot_tn(flat(rows), flat(dz[...])).astype(BF).reshape(out.shape)


def body(
    inputs,
    cotangent,
    image_group,
    group_side,
    group_width,
    group_depth,
    entry_reduce,
    entry_spatial,
    entry_expand,
    entry_project,
    entry_norm_reduce,
    entry_norm_spatial,
    entry_norm_expand,
    entry_norm_project,
    inner_reduce,
    inner_spatial,
    inner_expand,
    inner_norm_reduce,
    inner_norm_spatial,
    inner_norm_expand,
):
    images, full, _, wide = inputs.shape
    half = full // 2
    mid, out = entry_reduce.shape[1], entry_expand.shape[1]
    blocks = out // LANES
    shards, copies = lax.axis_size("dp"), lax.axis_size("rep")
    devices = shards * copies
    position, copy = lax.axis_index("dp"), lax.axis_index("rep")

    onehot_int = (image_group[None, :] == jnp.arange(GROUPS, dtype=jnp.int32)[:, None]).astype(
        jnp.int32
    )
    own_side = jnp.sum(onehot_int * group_side[:, None], axis=0)
    own_width = jnp.sum(onehot_int * group_width[:, None], axis=0)
    own_gate = jnp.sum(onehot_int * group_depth[:, None], axis=0)

    def lanes(vector):
        return jnp.broadcast_to(vector[:, None], (images, LANES))

    onehot = jnp.broadcast_to(
        onehot_int.astype(F32)[:, :, None], (GROUPS, images, LANES)
    )
    gate = lanes(own_gate).astype(F32)
    limits_in, limits_out = lanes(own_side), lanes(own_side // 2)
    kept = jnp.arange(mid, dtype=jnp.int32)[None, :] < (own_width * mid // 4)[:, None]
    keeps_in = jnp.where(kept, limits_in, 0)
    keeps_out = jnp.where(kept, limits_out, 0)

    def quarter(weights):
        rows = weights.shape[-2] // copies
        part = lax.dynamic_slice_in_dim(weights, copy * rows, rows, weights.ndim - 2)
        part = part.reshape((-1,) + part.shape[-2:])
        return flat(
            jnp.concatenate(
                [part[..., i : i + LANES] for i in range(0, part.shape[-1], LANES)], axis=0
            )
        )

    def layout(weights):
        taps = weights.shape[0] if weights.ndim == 3 else weights.shape[1] // LANES
        return taps, weights.shape[-2] // copies

    def joined(weights):
        parts = [quarter(w) for w in weights]
        return parts[0] if len(parts) == 1 else jnp.concatenate(parts, axis=0)

    def views(gathered, weights):
        result, at = [], 0
        for w in weights:
            taps, q = layout(w)
            result.append(Weight(gathered, at, taps, q))
            at += taps * q
        return result

    def everywhere(weights):
        return views(lax.all_gather(joined(weights), AXES, axis=0, tiled=False), weights)

    def shares(own, weights):
        gathered = own.reshape((copies,) + own.shape[-2:])
        result, at = [], 0
        for w in weights:
            taps, q = layout(w)
            field = gathered[:, at : at + taps * q].reshape(copies, taps, q, LANES)
            if w.ndim == 3:
                field = field.transpose(1, 0, 2, 3)
            else:
                field = field.transpose(0, 2, 1, 3)
            result.append(field.reshape(w.shape).astype(F32))
            at += taps * q
        return result

    def packs(weights):
        return all(layout(w)[1] % 16 == 0 for w in weights)

    def grad_out(weights, steps, at=0, total=None):
        taps, q = layout(weights)
        if q % 16:
            shape = (taps * devices * q, LANES)
            return (shape, BF, pl.BlockSpec((shape[0] // steps, LANES), lambda s: (s, 0)))
        shape = (devices, total or taps * q, LANES)
        first = at // q
        if taps > 1:
            return (shape, BF, pl.BlockSpec((devices, q, LANES), lambda s: (0, first + s, 0)))
        return (shape, BF, pl.BlockSpec((devices // steps, q, LANES), lambda s: (s, first, 0)))

    def grad_rows(grad, weights):
        taps, q = layout(weights)
        if q % 16 == 0:
            return grad
        field = grad.reshape(taps, devices, q, LANES).transpose(1, 0, 2, 3)
        return field.reshape(devices, taps * q, LANES)

    def grads_into(weights):
        total = sum(layout(w)[0] * layout(w)[1] for w in weights)
        results = {}

        def run(index, kernel, name, steps, ins, flops, scratch=()):
            w = weights[index]
            at = sum(layout(v)[0] * layout(v)[1] for v in weights[:index])
            if packs(weights):
                (results["all"],) = call(
                    kernel, name, steps, ins, [grad_out(w, steps, at, total)], scratch, flops,
                    into=results.get("all"),
                )
            else:
                (results[index],) = call(kernel, name, steps, ins, [grad_out(w, steps)], scratch, flops)

        def whole_rows():
            if "all" in results:
                return results["all"]
            return jnp.concatenate(
                [grad_rows(results[i], w) for i, w in enumerate(weights)], axis=1
            )

        return run, whole_rows

    tables_all = (
        entry_norm_reduce,
        entry_norm_spatial,
        entry_norm_expand,
        entry_norm_project,
        inner_norm_reduce,
        inner_norm_spatial,
        inner_norm_expand,
    )
    w_spatial, w_expand = everywhere([entry_spatial, entry_expand])
    table_cells = jnp.concatenate([t.reshape(2 * GROUPS, -1) for t in tables_all], axis=1)
    table_rows = -(-table_cells.size // (copies * LANES))
    table_part = jnp.pad(
        table_cells.reshape(-1), (0, copies * table_rows * LANES - table_cells.size)
    ).reshape(copies, table_rows, LANES)
    table_part = lax.dynamic_index_in_dim(table_part, copy, 0, keepdims=False)
    middle_weights = [entry_project, inner_reduce]
    last_weights = [inner_spatial, inner_expand]
    first_array, others = gather_rows(
        jnp.concatenate([quarter(entry_reduce), table_part], axis=0), middle_weights + last_weights
    )
    w_ispatial, w_iexpand = everywhere(others[2:])
    first_array, part = after(first_array, joined(others[:2]))
    (w_reduce,) = views(first_array, [entry_reduce])
    line = line_gather_start(part)
    tables_flat = first_array[:, -table_rows:].reshape(shards, -1)[:, : table_cells.size]
    tables_flat = tables_flat.reshape((shards,) + table_cells.shape)
    tables, at = [], 0
    for t in tables_all:
        width = t.shape[2]
        field = tables_flat[:, :, at : at + width].transpose(1, 0, 2)
        tables.append(field.reshape(2 * GROUPS, shards * width).astype(F32))
        at += width

    x = inputs.transpose(1, 2, 0, 3)
    x_split = x.reshape(half, 2, half, 2, images, wide)
    cot = cotangent.transpose(1, 2, 0, 3)

    small = (half, half, images, LANES)
    large = (half, half, images, out)
    split = (half, 2, half, 2, images, LANES)
    rows_out, rows_in = half * half * images, full * full * images
    six = (2 * GROUPS, LANES)
    sums_block = (8, LANES)

    def fixed(array):
        return (array, whole(array.shape))

    def column(array):
        return (array, along(array.shape[:-1] + (LANES,), array.ndim - 1))

    small_out = (small, BF, whole(small))
    large_out = (large, BF, along(small, 3))
    sums_out = ((8, LANES), F32, whole((8, LANES)))
    sums_wide = ((8, out), F32, along((8, LANES), 1))
    acc = pltpu.VMEM(small, F32)

    count_row = jnp.concatenate(
        [
            jnp.broadcast_to(jnp.sum(onehot_int[g]).astype(F32), (1, 128))
            for g in range(GROUPS)
        ]
        + [jnp.zeros((1, LANES - 128 * GROUPS), F32)],
        axis=1,
    )
    z1, sums1 = call(
        k_first, "first", half,
        [(x, along((2, full, images, wide), 0)), w_reduce.moving_all(), fixed(limits_in), fixed(onehot),
         fixed(count_row)],
        [((full, full, images, mid), BF, along((2, full, images, mid), 0)), sums_out],
        [pltpu.VMEM((2, images, mid), F32)], flops=2 * rows_in * wide * mid,
    )
    sums1, z1, *line = after(sums1, z1, *line)
    sums1, *line = after(sum_everywhere(sums1), *line)
    low, high = split_rows(line_gather_end(line))
    low, high = gather_bit(low, 2, 1), gather_bit(high, 1, 2)
    low, high, w_spatial.array, z1 = after(low, high, w_spatial.array, z1)
    w_expand.array = w_spatial.array if w_expand.at else w_expand.array
    low, high = gather_bit(low, 1, 2), gather_bit(high, 2, 1)
    totals = sums1[2 * GROUPS, 0 : 128 * GROUPS : 128]
    side_real = group_side.astype(F32)
    half_real = (group_side // 2).astype(F32)
    counts_in = jnp.broadcast_to((totals * side_real * side_real)[:, None], (GROUPS, LANES))
    counts = jnp.broadcast_to((totals * half_real * half_real)[:, None], (GROUPS, LANES))
    counts_in, counts = fixed(counts_in), fixed(counts)
    onehot, gate = fixed(onehot), fixed(gate)
    limits_in, limits_out = fixed(limits_in), fixed(limits_out)
    keeps_in, keeps_out = fixed(keeps_in), fixed(keeps_out)

    z1_split = z1.reshape(split)
    row_split = (1, 2, half, 2, images, LANES)
    planes_shape = (2, 2, half + 1, half + 1, images, mid)
    planes, slope1, z2, sums2 = call(
        k_entry_spatial, "entry_spatial", half,
        [(z1_split, along(row_split, 0)), fixed(sums1), fixed(tables[0]), counts_in, counts,
         keeps_in, limits_out, onehot, w_spatial.every()],
        [(planes_shape, BF, whole(planes_shape)), (split, BF, along(row_split, 0)), small_out,
         sums_out],
        [acc], flops=18 * rows_out * mid * mid,
    )
    sums2, low, high = after(sums2, low, high)
    values = [gather_bit(v, 0, 3) for v in (low, high)]
    gathered = jnp.concatenate(values, axis=4).reshape(devices, -1, LANES)
    w_project, w_ireduce = views(gathered, middle_weights)
    sums2 = sum_everywhere(sums2)
    zs, sums_s = call(
        k_strided, "strided", blocks,
        [(x_split, whole((half, 1, half, 1, images, wide))), w_project.moving(), limits_out, onehot],
        [large_out, sums_wide], [acc], flops=2 * rows_out * wide * out,
    )
    a2, slope2, z3, sums3 = call(
        k_expand, "expand", blocks,
        [fixed(z2), fixed(sums2), fixed(tables[1]), counts, keeps_out, onehot,
         w_expand.moving()],
        [small_out, small_out, large_out, sums_wide], [acc], flops=2 * rows_out * mid * out,
    )
    joined = sum_everywhere(jnp.concatenate([sums3, sums_s], axis=1))
    sums3, sums_s = joined[:, :out], joined[:, out:]
    w_rows = w_ireduce.moving_rows(blocks)
    middle, slope3, z4, sums4 = call(
        k_middle, "middle", blocks,
        [column(z3), column(zs), column(sums3), column(sums_s), column(tables[2]),
         column(tables[3]), counts, limits_out, onehot, w_rows],
        [large_out, large_out, small_out, sums_out], [acc], flops=2 * rows_out * mid * out,
    )
    sums4 = sum_everywhere(sums4)
    padded_shape = (half + 2, half + 2, images, mid)
    padded4, slope4, z5, sums5 = call(
        k_inner_spatial, "inner_spatial", 1,
        [fixed(z4), fixed(sums4), fixed(tables[4]), counts, keeps_out, limits_out, onehot,
         w_ispatial.every()],
        [(padded_shape, BF, whole(padded_shape)), small_out, small_out, sums_out], [acc],
        flops=18 * rows_out * mid * mid,
    )
    sums5 = sum_everywhere(sums5)
    a5, slope5, z6, sums6 = call(
        k_expand, "inner_expand", blocks,
        [fixed(z5), fixed(sums5), fixed(tables[5]), counts, keeps_out, onehot,
         w_iexpand.moving()],
        [small_out, small_out, large_out, sums_wide], [acc], flops=2 * rows_out * mid * out,
    )
    sums6 = sum_everywhere(sums6)
    result, du6, back6 = call(
        k_close, "close", blocks,
        [column(z6), column(sums6), column(tables[6]), counts, limits_out, onehot, gate,
         column(middle), column(cot)],
        [large_out, large_out, sums_wide],
    )
    back6 = sum_everywhere(back6)
    dz6, du5, back5 = call(
        k_back_expand, "back_inner_expand", blocks,
        [column(du6), column(z6), column(sums6), column(back6), column(tables[6]), counts,
         limits_out, onehot, w_iexpand.moving(), fixed(slope5), fixed(z5), fixed(sums5)],
        [large_out, (small, F32, whole(small)), sums_out], [acc],
        flops=2 * rows_out * mid * out,
    )
    near, dz6 = after(sum_near(back5), dz6)
    back5 = sum_far(near, LANES)
    inner_grad, inner_rows = grads_into([inner_spatial, inner_expand])
    inner_grad(
        1, k_grad_columns, "inner_expand_grad", blocks, [fixed(a5), column(dz6)],
        2 * rows_out * mid * out, [pltpu.VMEM((mid, rows_out), BF)],
    )
    dz5, du4, back4 = call(
        k_back_inner_spatial, "back_inner_spatial", 1,
        [fixed(du5), fixed(z5), fixed(sums5), fixed(back5), fixed(tables[5]), counts, limits_out,
         onehot, w_ispatial.every(), fixed(slope4), fixed(z4), fixed(sums4)],
        [small_out, (small, F32, whole(small)), sums_out],
        [pltpu.VMEM(padded_shape, BF), acc], flops=18 * rows_out * mid * mid,
    )
    near, dz5 = after(sum_near(back4), dz5)
    inner_grad(
        0, k_taps, "inner_spatial_grad", 9, [fixed(padded4), fixed(dz5)], 18 * rows_out * mid * mid
    )
    late_rows, back4 = after(inner_rows().reshape(-1, LANES), sum_far(near, LANES))
    inner_own = lax.psum_scatter(late_rows, AXES, scatter_dimension=0, tiled=True)
    dz4, du3, back3 = call(
        k_back_middle, "back_middle", blocks,
        [fixed(du4), fixed(z4), fixed(sums4), fixed(back4), fixed(tables[4]), counts, limits_out,
         onehot, w_rows, gate, column(cot), column(du6), column(slope3), column(z3), column(zs),
         column(sums3), column(sums_s)],
        [small_out, large_out, ((16, out), F32, along((16, LANES), 1))], [acc],
        flops=2 * rows_out * mid * out,
    )
    near, dz4 = after(sum_near(back3), dz4)
    back3 = sum_far(near, out)
    middle_grads = [entry_project, inner_reduce, entry_expand]
    middle_grad, middle_rows = grads_into(middle_grads)
    middle_grad(
        1, k_grad, "inner_reduce_grad", blocks, [column(middle), fixed(dz4)],
        2 * rows_out * mid * out,
    )
    dz3, dzs, du2, back2 = call(
        k_back_entry_expand, "back_entry_expand", blocks,
        [column(du3), column(z3), column(zs), column(sums3), column(sums_s), column(back3),
         column(tables[2]), column(tables[3]), counts, limits_out, onehot, w_expand.moving(),
         fixed(slope2), fixed(z2), fixed(sums2)],
        [large_out, large_out, (small, F32, whole(small)), sums_out], [acc],
        flops=2 * rows_out * mid * out,
    )
    near, dz3, dzs = after(sum_near(back2), dz3, dzs)
    back2 = sum_far(near, LANES)
    middle_grad(
        2, k_grad_columns, "expand_grad", blocks, [fixed(a2), column(dz3)],
        2 * rows_out * mid * out, [pltpu.VMEM((mid, rows_out), BF)],
    )
    middle_grad(
        0, k_grad_strided, "project_grad", blocks,
        [(x_split, whole((half, 1, half, 1, images, wide))), column(dzs)],
        2 * rows_out * wide * out, [pltpu.VMEM((wide, rows_out), BF)],
    )
    low, high = cut_rows(halve_bit([[near_shape(middle_rows())]], 0, 3))
    low_sent, high_sent, back2 = after(halve_sent(low, 1, 2), halve_sent(high, 2, 1), back2)
    low, high = halve_end(low, low_sent, 1, 2), halve_end(high, high_sent, 2, 1)
    strided_shape = (half, half, images, wide)
    plane = (half, 1, half, 1, images, LANES)

    def parity(array):
        return (array, pl.BlockSpec(plane, lambda s: (0, s // 2, 0, s % 2, 0, 0)))

    dz2, du1, back1 = call(
        k_back_entry_spatial, "back_entry_spatial", 4,
        [fixed(du2), fixed(z2), fixed(sums2), fixed(back2), fixed(tables[1]), counts, counts_in,
         limits_out, onehot, w_spatial.every(), parity(slope1), parity(z1_split), fixed(sums1)],
        [small_out, (split, BF, parity(z1_split)[1]), sums_out],
        [pltpu.VMEM((half + 1, half + 1, images, mid), BF), pltpu.VMEM((2, images, mid), F32), acc],
        flops=18 * rows_out * mid * mid,
    )
    (g_spatial,) = call(
        k_taps_strided, "entry_spatial_grad", 9, [fixed(planes), fixed(dz2)],
        [grad_out(entry_spatial, 9)],
        flops=18 * rows_out * mid * mid,
    )
    spatial_rows = [[near_shape(grad_rows(g_spatial, entry_spatial))]]
    spatial_sent = halve_sent(spatial_rows, 0, 3)
    back1, low_sent, high_sent, spatial_sent = after(
        back1, halve_sent(low, 2, 1), halve_sent(high, 1, 2), spatial_sent
    )
    near, low_sent, high_sent = after(sum_near(back1), low_sent, high_sent)
    low, high = halve_end(low, low_sent, 2, 1), halve_end(high, high_sent, 1, 2)
    back1 = sum_far(near, LANES)
    spatial_rows = halve_end(spatial_rows, spatial_sent, 0, 3)
    two = (2, full, images, mid)
    taps, q = layout(entry_reduce)
    flat_shape = (devices, q, LANES) if q % 16 == 0 else (devices * q, LANES)
    dz1, g_reduce = call(
        k_back_first, "back_first", half,
        [(du1.reshape(z1.shape), along(two, 0)), (z1, along(two, 0)), fixed(sums1), fixed(back1),
         fixed(tables[0]), counts_in, limits_in, onehot, (x, along((2, full, images, wide), 0))],
        [(z1.shape, BF, along(two, 0)), (flat_shape, BF, whole(flat_shape))],
        [pltpu.VMEM((wide, mid), F32)], flops=2 * rows_in * wide * mid,
    )
    first_rows = [[added(v).astype(BF)] for v in low + high]
    first_rows, g_reduce, dz1, dzs, inner_own = flat_after(
        first_rows, g_reduce, dz1, dzs, inner_own
    )
    reduce_rows = halve_bit([[near_shape(grad_rows(g_reduce, entry_reduce))]], 0, 3)
    low, high = cut_rows(spatial_rows + reduce_rows)
    first_rows, low_sent, high_sent, dz1, dzs = flat_after(
        first_rows, halve_sent(low, 1, 2), halve_sent(high, 2, 1), dz1, dzs
    )
    first_line = LineScatter(first_rows)
    first_line.step(1)
    low, high = halve_end(low, low_sent, 1, 2), halve_end(high, high_sent, 2, 1)
    inner_own = gather_copy(inner_own.reshape(1, 1, -1, LANES), 1)
    (d_strided,) = call(
        k_back_strided, "back_strided", blocks, [column(dzs), w_project.moving()],
        [(strided_shape, F32, whole(strided_shape))], flops=2 * rows_out * wide * out,
    )
    first_state, low_sent, high_sent, d_strided, inner_own = flat_after(
        first_line.state(), halve_sent(low, 2, 1), halve_sent(high, 1, 2), d_strided, inner_own
    )
    first_line.put(first_state)
    first_line.step(2)
    low, high = halve_end(low, low_sent, 2, 1), halve_end(high, high_sent, 1, 2)
    inner_own = gather_copy(inner_own, 0)
    (d_inputs,) = call(
        k_input_grad, "input_grad", half,
        [(dz1, along(two, 0)), w_reduce.moving_all(),
         (d_strided, along((1, half, images, wide), 0))],
        [((full, full, images, wide), F32, along((2, full, images, wide), 0))],
        flops=2 * rows_in * wide * mid,
    )
    last_rows = [[added(v).astype(BF)] for v in low + high]
    first_state, last_rows, d_inputs, inner_own = flat_after(
        first_line.state(), last_rows, d_inputs, inner_own
    )
    first_line.put(first_state)
    first_line.step(3)
    last_line = LineScatter(last_rows)
    last_line.step(1)
    g_ispatial, g_iexpand = shares(inner_own, [inner_spatial, inner_expand])
    first_state, last_state, g_ispatial, g_iexpand = flat_after(
        first_line.state(), last_line.state(), g_ispatial, g_iexpand
    )
    first_line.put(first_state)
    last_line.put(last_state)
    last_line.step(2)
    entry_own = gather_copy(first_line.end().reshape(1, 1, -1, LANES), 1)
    entry_own, last_state = flat_after(entry_own, last_line.state())
    last_line.put(last_state)
    last_line.step(3)
    entry_own = gather_copy(entry_own, 0)
    entry_own, last_state = flat_after(entry_own, last_line.state())
    last_line.put(last_state)
    last_own = gather_copy(last_line.end().reshape(1, 1, -1, LANES), 1)
    g_project, g_ireduce, g_expand = shares(entry_own, middle_grads)
    last_own, g_project, g_ireduce, g_expand = after(last_own, g_project, g_ireduce, g_expand)
    g_spatial, g_reduce = shares(gather_copy(last_own, 0), [entry_spatial, entry_reduce])

    def own_share(back, gain_at=0):
        width = back.shape[1] // shards
        own = lax.dynamic_slice_in_dim(back, position * width, width, 1)
        return jnp.stack([own[gain_at : gain_at + GROUPS], own[GROUPS : 2 * GROUPS]])

    return (
        result.transpose(2, 0, 1, 3),
        d_inputs.transpose(2, 0, 1, 3),
        g_reduce,
        g_spatial,
        g_expand,
        g_project,
        own_share(back1),
        own_share(back2),
        own_share(back3),
        own_share(back3, 2 * GROUPS),
        g_ireduce,
        g_ispatial,
        g_iexpand,
        own_share(back4),
        own_share(back5),
        own_share(back6),
    )


def solution(mesh):
    images = P(("dp", "rep"), None, None, None)
    rows = P("dp", None)
    taps = P(None, "dp", None)
    table = P(None, None, "dp")
    entry = (rows, taps, rows, rows, table, table, table, table)
    inner = (rows, taps, rows, table, table, table)
    return jax.shard_map(
        body,
        mesh=mesh,
        in_specs=(images, images, P(("dp", "rep")), P(), P(), P(), *entry, *inner),
        out_specs=(images, images, *entry, *inner),
        check_vma=False,
    )
```

```python
import functools

import jax
import jax.numpy as jnp
from jax import lax
from jax.experimental import pallas as pl
from jax.experimental.pallas import tpu as pltpu
from jax.sharding import PartitionSpec as P

EPSILON = 1e-05
AXES = ("dp", "rep")
BF = jnp.bfloat16
F32 = jnp.float32
GROUPS = 3
LANES = 512
VMEM = 24 * 1024 * 1024
LARGE = 1700 * 1000
NEAR = ("first",)


def xor_swap(value, distance):
    count = lax.axis_size("dp") * lax.axis_size("rep")
    return lax.ppermute(value, AXES, [(d, d ^ distance) for d in range(count)])


def own_bit(bit):
    me = lax.axis_index("dp") * lax.axis_size("rep") + lax.axis_index("rep")
    return lax.shift_right_logical(me, bit) & 1


def index_bits():
    count = lax.axis_size("dp") * lax.axis_size("rep")
    return count.bit_length() - 1


def sum_stages(value, bits):
    for stage in [bits[i : i + 2] for i in range(0, len(bits), 2)]:
        distances = [0]
        for bit in stage:
            distances = distances + [d | (1 << bit) for d in distances]
        for part in [xor_swap(value, d) for d in distances[1:]]:
            value = value + part
    return value


def sum_near(value):
    if value.size <= 8192:
        return sum_stages(value + xor_swap(value, 1), [1, 2])
    width = value.shape[1] // 2
    own = own_bit(0)
    kept = lax.dynamic_slice_in_dim(value, own * width, width, 1)
    sent = lax.dynamic_slice_in_dim(value, (1 - own) * width, width, 1)
    return sum_stages(kept + xor_swap(sent, 1), [1, 2])


def sum_far(value, columns):
    value = sum_stages(value, list(range(3, index_bits())))
    if value.shape[1] == columns:
        return value
    return pair(value, xor_swap(value, 1), 0, 1)


def sum_everywhere(value):
    return sum_far(sum_near(value), value.shape[1])


def after(*values):
    return lax.optimization_barrier(values)


def pair(value, other, bit, axis):
    own = own_bit(bit)
    return jnp.concatenate(
        [jnp.where(own == 0, value, other), jnp.where(own == 0, other, value)], axis=axis
    )


def gather_bit(value, bit, axis):
    return pair(value, xor_swap(value, 1 << bit), bit, axis)


def gather_rows(part, others):
    count = index_bits()
    value = part.reshape((1,) * count + part.shape)
    for bit in list(range(3, count)) + [2, 1, 0]:
        value = gather_bit(value, bit, count - 1 - bit)
        if bit == 3:
            value, *others = after(value, *others)
    return value.reshape((-1,) + part.shape), others


def split_rows(value):
    total = value.shape[-2]
    cut = total // 32 * 16 or total // 2
    return value[..., :cut, :], value[..., cut:, :]


def is_line():
    return lax.axis_size("dp") == 8 and lax.axis_size("rep") == 4


def line_place():
    return lax.axis_index("dp") // 2


def line_shift(value, step, among=range(4)):
    pairs = [
        (p * 8 + i, (p + step) * 8 + i) for p in among for i in range(8) if 0 <= p + step < 4
    ]
    return lax.ppermute(value, AXES, pairs)


def line_gather_start(part):
    if not is_line():
        return (part,)
    return part, line_shift(part, 1), line_shift(part, -1)


def line_gather_end(parts):
    part = parts[0]
    if not is_line():
        count = index_bits()
        value = part.reshape((1,) * count + part.shape)
        for bit in range(3, count):
            value = gather_bit(value, bit, count - 1 - bit)
        return value.reshape((-1, 1, 1, 1) + part.shape)
    right, left = [parts[1]], [parts[2]]
    for _ in range(2):
        right.append(line_shift(right[-1], 1))
        left.append(line_shift(left[-1], -1))
    row = jnp.stack(right[::-1] + [part] + left)
    row = lax.dynamic_slice_in_dim(row, 3 - line_place(), 4, 0)
    return row.reshape((4, 1, 1, 1) + part.shape)


def added(parts):
    total = parts[0].astype(F32)
    for part in parts[1:]:
        total = total + part.astype(F32)
    return total


def halves(segments, bit, axis, other):
    index = own_bit(bit) ^ other
    return [[lax.dynamic_slice_in_dim(p, index, 1, axis) for p in s] for s in segments]


def halve_sent(segments, bit, axis):
    sent = [added(parts).astype(BF) for parts in halves(segments, bit, axis, 1)]
    return sent[0] if len(sent) == 1 else jnp.concatenate(sent, axis=-2)


def halve_end(segments, sent, bit, axis):
    got = xor_swap(sent, 1 << bit)
    result, at = [], 0
    for parts in halves(segments, bit, axis, 0):
        count = parts[0].shape[-2]
        result.append(parts + [lax.slice_in_dim(got, at, at + count, axis=got.ndim - 2)])
        at += count
    return result


def halve_bit(segments, bit, axis):
    return halve_end(segments, halve_sent(segments, bit, axis), bit, axis)


def cut_rows(segments):
    total = sum(s[0].shape[-2] for s in segments)
    cut = total // 32 * 16 or total // 2
    low, high, at = [], [], 0
    for s in segments:
        count = s[0].shape[-2]
        here = min(max(cut - at, 0), count)
        if here:
            low.append([p[..., :here, :] for p in s])
        if here < count:
            high.append([p[..., here:, :] for p in s])
        at += count
    return low, high


def flat_after(*values):
    leaves, tree = jax.tree.flatten(values)
    return jax.tree.unflatten(tree, lax.optimization_barrier(leaves))


def near_shape(value):
    return value.reshape((-1, 2, 2, 2) + value.shape[1:])


def far_scatter(segments):
    if not is_line():
        count = index_bits() - 3
        values = [[p.reshape((2,) * count + p.shape[-2:]) for p in s] for s in segments]
        for step in range(count):
            values = halve_bit(values, step + 3, count - 1 - step)
        values = [added(s).reshape((-1, LANES)).astype(BF) for s in values]
        return jnp.concatenate(values, axis=0)

    def block(index):
        parts = [
            added([lax.dynamic_index_in_dim(p, index, 0, keepdims=False) for p in s])
            for s in segments
        ]
        return jnp.concatenate(parts, axis=-2) if len(parts) > 1 else parts[0]

    place = line_place()
    parts = [block(place)]
    for k in (1, 2, 3):
        parts.append(xor_swap(block(place ^ k).astype(BF), k << 3))
    return added(parts).reshape((-1, LANES)).astype(BF)


def gather_copy(value, bit):
    return gather_bit(value, bit, 1 - bit)


def gelu_parts(u):
    k = 0.7978845608028654
    square = u * u
    half = 0.5 + 0.5 * jnp.tanh(u * (k + (0.044715 * k) * square))
    slope = half * (1.0 + u * (1.0 - half) * (2 * k + (6 * 0.044715 * k) * square))
    return u * half, slope


def dot(a, b):
    return lax.dot_general(a, b, (((1,), (0,)), ((), ())), preferred_element_type=F32)


def dot_nt(a, b):
    return lax.dot_general(a, b, (((1,), (1,)), ((), ())), preferred_element_type=F32)


def dot_tn(a, b):
    return lax.dot_general(a, b, (((0,), (0,)), ((), ())), preferred_element_type=F32)


def flat(field):
    return field.reshape(-1, field.shape[-1])


def whole(shape):
    return pl.BlockSpec(shape, lambda *_: (0,) * len(shape), pipeline_mode=pl.Buffered(1))


def along(shape, axis):
    return pl.BlockSpec(shape, lambda s: tuple(s if a == axis else 0 for a in range(len(shape))))


class Weight:
    def __init__(self, gathered, at, taps, q):
        if q % 16 == 0:
            self.array, self.at, self.taps, self.q = gathered, at, taps, q
        else:
            devices = gathered.shape[0]
            field = gathered[:, at : at + taps * q].reshape(devices, taps, q, LANES)
            field = field.transpose(1, 0, 2, 3).reshape(1, taps * devices * q, LANES)
            self.array, self.at, self.taps, self.q = field, 0, taps, devices * q

    def held(self):
        return pltpu.with_memory_space_constraint(self.array, pltpu.HBM)

    def spec(self, rows, index, mode=None):
        return pl.BlockSpec((self.array.shape[0], rows, LANES), index, pipeline_mode=mode)

    def chunk(self, at, count):
        rows = count * self.q
        place = at // rows
        return (self.held(), self.spec(rows, lambda *_: (0, place, 0), pl.Buffered(1)))

    def every(self):
        chunks, left, at = [], self.taps, self.at
        while left:
            count = left
            while at % (count * self.q):
                count -= 1
            chunks.append(self.chunk(at, count))
            at += count * self.q
            left -= count
        return chunks

    def moving(self):
        first = self.at // self.q
        return (self.held(), self.spec(self.q, lambda s: (0, first + s, 0)))

    def moving_all(self):
        return self.chunk(self.at, self.taps)

    def moving_rows(self, steps):
        devices = self.array.shape[0]
        if devices > 1:
            place = self.at // self.q
            return (
                self.held(),
                pl.BlockSpec((devices // steps, self.q, LANES), lambda s: (s, place, 0)),
            )
        return (self.held(), pl.BlockSpec((1, self.q // steps, LANES), lambda s: (0, s, 0)))


class Taps:
    def __init__(self, refs, total):
        self.refs = refs
        self.q = sum(r.shape[1] for r in refs) // total

    def __getitem__(self, t):
        row = t * self.q
        for ref in self.refs:
            if row < ref.shape[1]:
                return flat(ref[:, row : row + self.q])
            row -= ref.shape[1]


def call(kernel, name, steps, ins, outs, scratch=(), flops=0, into=None):
    groups = [i if isinstance(i, list) else [i] for i in ins]
    arrays = [a for g in groups for a, _ in g]
    size = sum(a.size * a.dtype.itemsize for a in arrays)

    def body(*refs):
        params, at = [], 0
        for i, g in zip(ins, groups):
            some = refs[at : at + len(g)]
            params.append(Taps(some, 9) if isinstance(i, list) else some[0])
            at += len(g)
        kernel(*params, *refs[at + (into is not None) :])

    given = [] if into is None else [into]
    arrays = [
        pltpu.with_memory_space_constraint(a, pltpu.HBM) if a.nbytes > LARGE and name not in NEAR else a
        for a in arrays
    ]

    def result(shape, dtype):
        size = dtype.dtype.itemsize
        for extent in shape:
            size *= extent
        return (pltpu.HBM if size > LARGE else jax.ShapeDtypeStruct)(shape, dtype)


    return pl.pallas_call(
        body,
        name=name,
        grid=(steps,),
        in_specs=[s for g in groups for _, s in g] + [pl.BlockSpec(memory_space=pl.ANY)] * len(given),
        input_output_aliases={len(arrays): 0} if given else {},
        out_specs=[s for _, _, s in outs],
        out_shape=[result(shape, dtype) for shape, dtype, _ in outs],
        scratch_shapes=list(scratch),
        compiler_params=pltpu.CompilerParams(
            vmem_limit_bytes=VMEM, dimension_semantics=("arbitrary",)
        ),
        cost_estimate=pl.CostEstimate(flops=flops, bytes_accessed=size, transcendentals=0),
    )(*arrays, *given)


def rows3(ref, first):
    return [ref[first + g : first + g + 1, :] for g in range(GROUPS)]


def spread(onehot, rows):
    total = onehot[0] * rows[0]
    for g in range(1, GROUPS):
        total = total + onehot[g] * rows[g]
    return total


def group_rows(onehot, *sums):
    rows = [
        jnp.sum(onehot[g] * image, axis=0, keepdims=True) for image in sums for g in range(GROUPS)
    ]
    return rows


def put_rows(ref, rows):
    for r, row in enumerate(rows):
        ref[r : r + 1, :] = row
    if len(rows) < ref.shape[0]:
        ref[len(rows) :, :] = jnp.zeros((ref.shape[0] - len(rows), ref.shape[1]), F32)


def moments(sums, counts):
    first, second, count = rows3(sums, 0), rows3(sums, GROUPS), rows3(counts, 0)
    center = [a / c for a, c in zip(first, count)]
    inverse = [lax.rsqrt(b / c - m * m + EPSILON) for b, c, m in zip(second, count, center)]
    return center, inverse


def forward_coefs(sums, table, counts, onehot):
    center, inverse = moments(sums, counts)
    scale = [a * i for a, i in zip(rows3(table, 0), inverse)]
    shift = [b - m * s for b, m, s in zip(rows3(table, GROUPS), center, scale)]
    return spread(onehot, scale), spread(onehot, shift)


def backward_coefs(sums, back, table, counts, onehot, gain_at=0):
    center, inverse = moments(sums, counts)
    count = rows3(counts, 0)
    factor = [a * i for a, i in zip(rows3(table, 0), inverse)]
    gain = [g / c for g, c in zip(rows3(back, gain_at), count)]
    bias = [b / c for b, c in zip(rows3(back, GROUPS), count)]
    on_z = [-f * i * g for f, i, g in zip(factor, inverse, gain)]
    on_one = [f * (m * i * g - b) for f, m, i, g, b in zip(factor, center, inverse, gain, bias)]
    return spread(onehot, factor), spread(onehot, on_z), spread(onehot, on_one)


def gain_rows(sums, counts, onehot, with_z, plain):
    center, inverse = moments(sums, counts)
    raw_z, raw = group_rows(onehot, with_z), group_rows(onehot, plain)
    return [i * (e - m * d) for i, e, m, d in zip(inverse, raw_z, center, raw)]


def inside(limits, row, count, step=1, start=0):
    column = lax.broadcasted_iota(jnp.int32, (count,) + limits.shape, 0) * step + start
    return (column < limits[None]) & (row < limits)[None]


def add_stats(values, mask, first, second):
    kept = jnp.where(mask, values, 0.0)
    return first + jnp.sum(kept, axis=0), second + jnp.sum(kept * values, axis=0)


def k_first(x, w, limits, onehot, count_row, z, sums, acc):
    step = pl.program_id(0)

    @pl.when(step == 0)
    def _():
        acc[...] = jnp.zeros_like(acc)

    rows, cols = x.shape[0], x.shape[1]
    values = dot(flat(x[...]), flat(w[...])).reshape(rows, cols, x.shape[2], LANES)
    z[...] = values.astype(BF)
    first, second = acc[0], acc[1]
    for r in range(rows):
        mask = inside(limits[...], step * rows + r, cols)
        first, second = add_stats(values[r], mask, first, second)
    acc[0] = first
    acc[1] = second

    @pl.when(step == pl.num_programs(0) - 1)
    def _():
        put_rows(sums, group_rows(onehot, first, second) + [count_row[0:1, :]])


def stats_of(field, limits, onehot, z, sums):
    side = field.shape[0]
    shape = field.shape[2:]

    def row(i, carry):
        values = field[i]
        z[i] = values.astype(BF)
        if limits is None:
            return carry[0] + jnp.sum(values, axis=0), carry[1] + jnp.sum(values * values, axis=0)
        return add_stats(values, inside(limits[...], i, side), *carry)

    first, second = lax.fori_loop(
        0, side, row, (jnp.zeros(shape, F32), jnp.zeros(shape, F32)), unroll=True
    )
    put_rows(sums, group_rows(onehot, first, second))


def k_strided(x, w, limits, onehot, z, sums, acc):
    side = z.shape[0]
    acc[...] = dot(flat(x[:, 0, :, 0]), flat(w[...])).reshape(acc.shape)
    stats_of(acc, limits, onehot, z, sums)


def k_entry_spatial(
    z1, in_sums, table, counts, counts_out, limits, limits_out, onehot, w,
    planes, slope, z2, sums, acc,
):
    step = pl.program_id(0)
    side = z2.shape[0]

    @pl.when(step == 0)
    def _():
        planes[1, :, 0] = jnp.zeros(planes.shape[1:2] + planes.shape[3:], BF)
        planes[:, 1, :, 0] = jnp.zeros(planes.shape[:1] + planes.shape[2:3] + planes.shape[4:], BF)

    scale, shift = forward_coefs(in_sums, table, counts, onehot)
    for a in range(2):
        for b in range(2):
            u = z1[0, a, :, b].astype(F32) * scale + shift
            act, grad = gelu_parts(u)
            mask = inside(limits[...], 2 * step + a, side, 2, b)
            planes[a, b, step + a, b : b + side] = jnp.where(mask, act, 0.0).astype(BF)
            slope[0, a, :, b] = jnp.where(mask, grad, 0.0).astype(BF)

    @pl.when(step == pl.num_programs(0) - 1)
    def _():
        for t in range(9):
            v, h = t // 3, t % 3
            rows = planes[(v + 1) % 2, (h + 1) % 2, v // 2 : v // 2 + side, h // 2 : h // 2 + side]
            part = dot(flat(rows), w[t]).reshape(acc.shape)
            if t == 0:
                acc[...] = part
            else:
                acc[...] += part
        stats_of(acc, limits_out, onehot, z2, sums)


def activate(z, coefs, limits, store):
    scale, shift = coefs
    side = z.shape[0]

    def row(i, carry):
        act, grad = gelu_parts(z[i].astype(F32) * scale + shift)
        mask = inside(limits[...], i, side)
        store(i, jnp.where(mask, act, 0.0).astype(BF), jnp.where(mask, grad, 0.0).astype(BF))
        return carry

    lax.fori_loop(0, side, row, 0, unroll=True)


def k_expand(z, in_sums, table, counts, keeps, onehot, w, a, slope, z_out, sums, acc):
    @pl.when(pl.program_id(0) == 0)
    def _():
        def store(i, act, grad):
            a[i] = act
            slope[i] = grad

        activate(z, forward_coefs(in_sums, table, counts, onehot), keeps, store)

    acc[...] = dot(flat(a[...]), flat(w[...])).reshape(acc.shape)
    stats_of(acc, None, onehot, z_out, sums)


def k_middle(
    z3, zs, sums3, sums_s, table3, table_s, counts, limits, onehot, w,
    middle, slope, z4, sums, acc,
):
    step = pl.program_id(0)
    side = z3.shape[0]
    scale, shift = forward_coefs(sums3, table3, counts, onehot)
    scale_s, shift_s = forward_coefs(sums_s, table_s, counts, onehot)
    shift = shift + shift_s

    def row(i, carry):
        act, grad = gelu_parts(z3[i].astype(F32) * scale + zs[i].astype(F32) * scale_s + shift)
        mask = inside(limits[...], i, side)
        middle[i] = jnp.where(mask, act, 0.0).astype(BF)
        slope[i] = jnp.where(mask, grad, 0.0).astype(BF)
        return carry

    lax.fori_loop(0, side, row, 0, unroll=True)
    part = dot(flat(middle[...]), flat(w[...])).reshape(acc.shape)

    @pl.when(step == 0)
    def _():
        acc[...] = part

    @pl.when(step > 0)
    def _():
        acc[...] += part

    @pl.when(step == pl.num_programs(0) - 1)
    def _():
        stats_of(acc, None, onehot, z4, sums)


def clear_edges(padded):
    edge = jnp.zeros(padded.shape[1:], BF)
    last = padded.shape[0] - 1
    padded[0] = edge
    padded[last] = edge
    for i in range(1, last):
        padded[i, 0] = edge[0]
        padded[i, last] = edge[0]


def k_inner_spatial(z4, in_sums, table, counts, keeps, limits, onehot, w, padded, slope, z5, sums, acc):
    side = z4.shape[0]
    clear_edges(padded)

    def store(i, act, grad):
        padded[i + 1, 1 : 1 + side] = act
        slope[i] = grad

    activate(z4, forward_coefs(in_sums, table, counts, onehot), keeps, store)
    for t in range(9):
        v, h = t // 3, t % 3
        part = dot(flat(padded[v : v + side, h : h + side]), w[t]).reshape(acc.shape)
        if t == 0:
            acc[...] = part
        else:
            acc[...] += part
    stats_of(acc, limits, onehot, z5, sums)


def k_close(z6, in_sums, table, counts, limits, onehot, gate, middle, cot, result, du6, sums):
    side = z6.shape[0]
    scale, shift = forward_coefs(in_sums, table, counts, onehot)
    opened = gate[...]
    zero = jnp.zeros(opened.shape, F32)

    def row(i, carry):
        plain, with_z = carry
        z = z6[i].astype(F32)
        mid = middle[i].astype(F32)
        act, grad = gelu_parts(z * scale + shift + mid)
        mask = inside(limits[...], i, side)
        closed = jnp.where(mask, act, 0.0)
        result[i] = (mid + opened * (closed - mid)).astype(BF)
        du = jnp.where(mask, grad, 0.0) * opened * cot[i].astype(F32)
        du6[i] = du.astype(BF)
        return plain + jnp.sum(du, axis=0), with_z + jnp.sum(du * z, axis=0)

    plain, with_z = lax.fori_loop(0, side, row, (zero, zero), unroll=True)
    put_rows(
        sums,
        gain_rows(in_sums, counts, onehot, with_z, plain) + group_rows(onehot, plain),
    )


def finish_back(acc, slope, z, in_sums, counts, onehot, du_out, sums):
    zero = jnp.zeros(slope.shape[2:], F32)

    def row(i, carry):
        plain, with_z = carry
        du = acc[i] * slope[i].astype(F32)
        du_out[i] = du.astype(du_out.dtype)
        return plain + jnp.sum(du, axis=0), with_z + jnp.sum(du * z[i].astype(F32), axis=0)

    plain, with_z = lax.fori_loop(0, slope.shape[0], row, (zero, zero), unroll=True)
    put_rows(
        sums,
        gain_rows(in_sums, counts, onehot, with_z, plain) + group_rows(onehot, plain),
    )


def norm_back(du, z, coefs, limits, store):
    factor, on_z, on_one = coefs
    side = z.shape[0]

    def row(i, carry):
        dz = du[i].astype(F32) * factor + z[i].astype(F32) * on_z + on_one
        store(i, jnp.where(inside(limits[...], i, side), dz, 0.0).astype(BF))
        return carry

    lax.fori_loop(0, side, row, 0, unroll=True)


def k_back_expand(
    du6, z6, sums6, back6, table6, counts, limits, onehot, w, slope, z5, sums5,
    dz6, du5, sums, acc,
):
    step = pl.program_id(0)

    def store(i, dz):
        dz6[i] = dz

    norm_back(du6, z6, backward_coefs(sums6, back6, table6, counts, onehot), limits, store)
    part = dot_nt(flat(dz6[...]), flat(w[...])).reshape(acc.shape)

    @pl.when(step == 0)
    def _():
        acc[...] = part

    @pl.when(step > 0)
    def _():
        acc[...] += part

    @pl.when(step == pl.num_programs(0) - 1)
    def _():
        finish_back(acc, slope, z5, sums5, counts, onehot, du5, sums)


def k_back_inner_spatial(
    du5, z5, sums5, back5, table5, counts, limits, onehot, w, slope, z4, sums4,
    dz5, du4, sums, padded, acc,
):
    side = z5.shape[0]
    clear_edges(padded)

    def store(i, dz):
        dz5[i] = dz
        padded[i + 1, 1 : 1 + side] = dz

    norm_back(du5, z5, backward_coefs(sums5, back5, table5, counts, onehot), limits, store)
    for t in range(9):
        v, h = t // 3, t % 3
        rows = padded[2 - v : 2 - v + side, 2 - h : 2 - h + side]
        part = dot_nt(flat(rows), w[t]).reshape(acc.shape)
        if t == 0:
            acc[...] = part
        else:
            acc[...] += part
    finish_back(acc, slope, z4, sums4, counts, onehot, du4, sums)


def k_back_middle(
    du4, z4, sums4, back4, table4, counts, limits, onehot, w, gate, cot, du6, slope3,
    z3, zs, sums3, sums_s, dz4, du3, sums, acc,
):
    side = z4.shape[0]

    @pl.when(pl.program_id(0) == 0)
    def _():
        def store(i, dz):
            dz4[i] = dz

        norm_back(du4, z4, backward_coefs(sums4, back4, table4, counts, onehot), limits, store)

    acc[...] = dot_nt(flat(dz4[...]), flat(w[...])).reshape(acc.shape)
    shut = 1.0 - gate[...]
    zero = jnp.zeros(shut.shape, F32)

    def row(i, carry):
        plain, with_z3, with_zs = carry
        grad = shut * cot[i].astype(F32) + du6[i].astype(F32) + acc[i]
        du = grad * slope3[i].astype(F32)
        du3[i] = du.astype(BF)
        return (
            plain + jnp.sum(du, axis=0),
            with_z3 + jnp.sum(du * z3[i].astype(F32), axis=0),
            with_zs + jnp.sum(du * zs[i].astype(F32), axis=0),
        )

    plain, with_z3, with_zs = lax.fori_loop(0, side, row, (zero, zero, zero), unroll=True)
    put_rows(
        sums,
        gain_rows(sums3, counts, onehot, with_z3, plain)
        + group_rows(onehot, plain)
        + gain_rows(sums_s, counts, onehot, with_zs, plain),
    )


def k_back_entry_expand(
    du3, z3, zs, sums3, sums_s, back3, table3, table_s, counts, limits, onehot, w,
    slope, z2, sums2, dz3, dzs, du2, sums, acc,
):
    step = pl.program_id(0)
    side = z3.shape[0]
    factor, on_z, on_one = backward_coefs(sums3, back3, table3, counts, onehot)
    factor_s, on_zs, on_one_s = backward_coefs(
        sums_s, back3, table_s, counts, onehot, 2 * GROUPS
    )

    def row(i, carry):
        du = du3[i].astype(F32)
        mask = inside(limits[...], i, side)
        dz = du * factor + z3[i].astype(F32) * on_z + on_one
        dz3[i] = jnp.where(mask, dz, 0.0).astype(BF)
        dz = du * factor_s + zs[i].astype(F32) * on_zs + on_one_s
        dzs[i] = jnp.where(mask, dz, 0.0).astype(BF)
        return carry

    lax.fori_loop(0, side, row, 0, unroll=True)
    part = dot_nt(flat(dz3[...]), flat(w[...])).reshape(acc.shape)

    @pl.when(step == 0)
    def _():
        acc[...] = part

    @pl.when(step > 0)
    def _():
        acc[...] += part

    @pl.when(step == pl.num_programs(0) - 1)
    def _():
        finish_back(acc, slope, z2, sums2, counts, onehot, du2, sums)


def k_back_strided(dzs, w, out):
    part = dot_nt(flat(dzs[...]), flat(w[...])).reshape(out.shape)

    @pl.when(pl.program_id(0) == 0)
    def _():
        out[...] = part

    @pl.when(pl.program_id(0) > 0)
    def _():
        out[...] += part


def k_back_entry_spatial(
    du2, z2, sums2, back2, table2, counts, counts_in, limits, onehot, w, slope, z1, sums1,
    dz2, du1, sums, padded, total, acc,
):
    step = pl.program_id(0)
    side = z2.shape[0]

    @pl.when(step == 0)
    def _():
        total[...] = jnp.zeros_like(total)
        padded[...] = jnp.zeros_like(padded)

        def store(i, dz):
            dz2[i] = dz
            padded[i, 0:side] = dz

        norm_back(du2, z2, backward_coefs(sums2, back2, table2, counts, onehot), limits, store)

    steps = {0: [(1, 0)], 1: [(2, 0), (0, 1)]}
    for a in range(2):
        for b in range(2):

            @pl.when(step == 2 * a + b)
            def _():
                started = False
                for v, down in steps[a]:
                    for h, right in steps[b]:
                        rows = padded[down : down + side, right : right + side]
                        part = dot_nt(flat(rows), w[3 * v + h]).reshape(acc.shape)
                        if started:
                            acc[...] += part
                        else:
                            acc[...] = part
                        started = True

    def row(i, carry):
        plain, with_z = carry
        du = acc[i] * slope[i, 0, :, 0].astype(F32)
        du1[i, 0, :, 0] = du.astype(BF)
        z = z1[i, 0, :, 0].astype(F32)
        return plain + jnp.sum(du, axis=0), with_z + jnp.sum(du * z, axis=0)

    plain, with_z = lax.fori_loop(0, side, row, (total[0], total[1]), unroll=True)
    total[0] = plain
    total[1] = with_z

    @pl.when(step == pl.num_programs(0) - 1)
    def _():
        put_rows(
            sums,
            gain_rows(sums1, counts_in, onehot, with_z, plain) + group_rows(onehot, plain),
        )


def k_back_first(du1, z1, sums1, back1, table1, counts, limits, onehot, x, dz1, grad, acc):
    step = pl.program_id(0)
    rows, cols = du1.shape[0], du1.shape[1]
    factor, on_z, on_one = backward_coefs(sums1, back1, table1, counts, onehot)
    for r in range(rows):
        dz = du1[r].astype(F32) * factor + z1[r].astype(F32) * on_z + on_one
        mask = inside(limits[...], rows * step + r, cols)
        dz1[r] = jnp.where(mask, dz, 0.0).astype(BF)
    part = dot_tn(flat(x[...]), flat(dz1[...]))

    @pl.when(step == 0)
    def _():
        acc[...] = part

    @pl.when(step > 0)
    def _():
        acc[...] += part

    @pl.when(step == pl.num_programs(0) - 1)
    def _():
        grad[...] = acc[...].astype(BF).reshape(grad.shape)


def k_input_grad(dz1, w, strided, dx):
    rows, cols = dz1.shape[0], dz1.shape[1]
    weights = flat(w[...])
    for r in range(rows):
        dx[r] = dot_nt(flat(dz1[r]), weights).reshape(dx.shape[1:])
    for j in range(cols // 2):
        dx[0, 2 * j] += strided[0, j]


def k_grad(source, dz, out):
    out[...] = dot_tn(flat(source[...]), flat(dz[...])).astype(BF).reshape(out.shape)


def k_grad_columns(source, dz, out, turned):
    @pl.when(pl.program_id(0) == 0)
    def _():
        turned[...] = flat(source[...]).T

    out[...] = dot(turned[...], flat(dz[...])).astype(BF).reshape(out.shape)


def k_grad_strided(x, dz, out, turned):
    k_grad_columns(x.at[:, 0, :, 0], dz, out, turned)


def k_taps(field, dz, out):
    t = pl.program_id(0)
    v, h = t // 3, t % 3
    side = dz.shape[0]
    rows = field[pl.ds(v, side), pl.ds(h, side)]
    out[...] = dot_tn(flat(rows), flat(dz[...])).astype(BF).reshape(out.shape)


def k_taps_strided(planes, dz, out):
    t = pl.program_id(0)
    v, h = t // 3, t % 3
    side = dz.shape[0]
    rows = planes[(v + 1) % 2, (h + 1) % 2, pl.ds(v // 2, side), pl.ds(h // 2, side)]
    out[...] = dot_tn(flat(rows), flat(dz[...])).astype(BF).reshape(out.shape)


def body(
    inputs,
    cotangent,
    image_group,
    group_side,
    group_width,
    group_depth,
    entry_reduce,
    entry_spatial,
    entry_expand,
    entry_project,
    entry_norm_reduce,
    entry_norm_spatial,
    entry_norm_expand,
    entry_norm_project,
    inner_reduce,
    inner_spatial,
    inner_expand,
    inner_norm_reduce,
    inner_norm_spatial,
    inner_norm_expand,
):
    images, full, _, wide = inputs.shape
    half = full // 2
    mid, out = entry_reduce.shape[1], entry_expand.shape[1]
    blocks = out // LANES
    shards, copies = lax.axis_size("dp"), lax.axis_size("rep")
    devices = shards * copies
    position, copy = lax.axis_index("dp"), lax.axis_index("rep")

    onehot_int = (image_group[None, :] == jnp.arange(GROUPS, dtype=jnp.int32)[:, None]).astype(
        jnp.int32
    )
    own_side = jnp.sum(onehot_int * group_side[:, None], axis=0)
    own_width = jnp.sum(onehot_int * group_width[:, None], axis=0)
    own_gate = jnp.sum(onehot_int * group_depth[:, None], axis=0)

    def lanes(vector):
        return jnp.broadcast_to(vector[:, None], (images, LANES))

    onehot = jnp.broadcast_to(
        onehot_int.astype(F32)[:, :, None], (GROUPS, images, LANES)
    )
    gate = lanes(own_gate).astype(F32)
    limits_in, limits_out = lanes(own_side), lanes(own_side // 2)
    kept = jnp.arange(mid, dtype=jnp.int32)[None, :] < (own_width * mid // 4)[:, None]
    keeps_in = jnp.where(kept, limits_in, 0)
    keeps_out = jnp.where(kept, limits_out, 0)

    def quarter(weights):
        rows = weights.shape[-2] // copies
        part = lax.dynamic_slice_in_dim(weights, copy * rows, rows, weights.ndim - 2)
        part = part.reshape((-1,) + part.shape[-2:])
        return flat(
            jnp.concatenate(
                [part[..., i : i + LANES] for i in range(0, part.shape[-1], LANES)], axis=0
            )
        )

    def layout(weights):
        taps = weights.shape[0] if weights.ndim == 3 else weights.shape[1] // LANES
        return taps, weights.shape[-2] // copies

    def joined(weights):
        parts = [quarter(w) for w in weights]
        return parts[0] if len(parts) == 1 else jnp.concatenate(parts, axis=0)

    def views(gathered, weights):
        result, at = [], 0
        for w in weights:
            taps, q = layout(w)
            result.append(Weight(gathered, at, taps, q))
            at += taps * q
        return result

    def everywhere(weights):
        return views(lax.all_gather(joined(weights), AXES, axis=0, tiled=False), weights)

    def shares(own, weights):
        gathered = own.reshape((copies,) + own.shape[-2:])
        result, at = [], 0
        for w in weights:
            taps, q = layout(w)
            field = gathered[:, at : at + taps * q].reshape(copies, taps, q, LANES)
            if w.ndim == 3:
                field = field.transpose(1, 0, 2, 3)
            else:
                field = field.transpose(0, 2, 1, 3)
            result.append(field.reshape(w.shape).astype(F32))
            at += taps * q
        return result

    def packs(weights):
        return all(layout(w)[1] % 16 == 0 for w in weights)

    def grad_out(weights, steps, at=0, total=None):
        taps, q = layout(weights)
        if q % 16:
            shape = (taps * devices * q, LANES)
            return (shape, BF, pl.BlockSpec((shape[0] // steps, LANES), lambda s: (s, 0)))
        shape = (devices, total or taps * q, LANES)
        first = at // q
        if taps > 1:
            return (shape, BF, pl.BlockSpec((devices, q, LANES), lambda s: (0, first + s, 0)))
        return (shape, BF, pl.BlockSpec((devices // steps, q, LANES), lambda s: (s, first, 0)))

    def grad_rows(grad, weights):
        taps, q = layout(weights)
        if q % 16 == 0:
            return grad
        field = grad.reshape(taps, devices, q, LANES).transpose(1, 0, 2, 3)
        return field.reshape(devices, taps * q, LANES)

    def grads_into(weights):
        total = sum(layout(w)[0] * layout(w)[1] for w in weights)
        results = {}

        def run(index, kernel, name, steps, ins, flops, scratch=()):
            w = weights[index]
            at = sum(layout(v)[0] * layout(v)[1] for v in weights[:index])
            if packs(weights):
                (results["all"],) = call(
                    kernel, name, steps, ins, [grad_out(w, steps, at, total)], scratch, flops,
                    into=results.get("all"),
                )
            else:
                (results[index],) = call(kernel, name, steps, ins, [grad_out(w, steps)], scratch, flops)

        def whole_rows():
            if "all" in results:
                return results["all"]
            return jnp.concatenate(
                [grad_rows(results[i], w) for i, w in enumerate(weights)], axis=1
            )

        return run, whole_rows

    tables_all = (
        entry_norm_reduce,
        entry_norm_spatial,
        entry_norm_expand,
        entry_norm_project,
        inner_norm_reduce,
        inner_norm_spatial,
        inner_norm_expand,
    )
    table_cells = jnp.concatenate([t.reshape(2 * GROUPS, -1) for t in tables_all], axis=1)
    table_rows = -(-table_cells.size // (copies * LANES))
    table_part = jnp.pad(
        table_cells.reshape(-1), (0, copies * table_rows * LANES - table_cells.size)
    ).reshape(copies, table_rows, LANES)
    table_part = lax.dynamic_index_in_dim(table_part, copy, 0, keepdims=False)
    middle_weights = [entry_project, inner_reduce]
    last_weights = [inner_spatial, inner_expand]
    first_weights = [entry_spatial, entry_expand]
    early_array = lax.all_gather(
        jnp.concatenate([joined(first_weights), table_part], axis=0), AXES, axis=0, tiled=False
    )
    w_spatial, w_expand = views(early_array, first_weights)
    first_array, others = gather_rows(quarter(entry_reduce), middle_weights + last_weights)
    w_ispatial, w_iexpand = everywhere(others[2:])
    first_array, part = after(first_array, joined(others[:2]))
    (w_reduce,) = views(first_array, [entry_reduce])
    line = line_gather_start(part)
    x = inputs.transpose(1, 2, 0, 3)
    x_split = x.reshape(half, 2, half, 2, images, wide)
    cot = cotangent.transpose(1, 2, 0, 3)

    small = (half, half, images, LANES)
    large = (half, half, images, out)
    split = (half, 2, half, 2, images, LANES)
    rows_out, rows_in = half * half * images, full * full * images
    six = (2 * GROUPS, LANES)
    sums_block = (8, LANES)

    def fixed(array):
        return (array, whole(array.shape))

    def column(array):
        return (array, along(array.shape[:-1] + (LANES,), array.ndim - 1))

    small_out = (small, BF, whole(small))
    large_out = (large, BF, along(small, 3))
    sums_out = ((8, LANES), F32, whole((8, LANES)))
    sums_wide = ((8, out), F32, along((8, LANES), 1))
    acc = pltpu.VMEM(small, F32)

    count_row = jnp.concatenate(
        [
            jnp.broadcast_to(jnp.sum(onehot_int[g]).astype(F32), (1, 128))
            for g in range(GROUPS)
        ]
        + [jnp.zeros((1, LANES - 128 * GROUPS), F32)],
        axis=1,
    )
    z1, sums1 = call(
        k_first, "first", half,
        [(x, along((2, full, images, wide), 0)), w_reduce.moving_all(), fixed(limits_in), fixed(onehot),
         fixed(count_row)],
        [((full, full, images, mid), BF, along((2, full, images, mid), 0)), sums_out],
        [pltpu.VMEM((2, images, mid), F32)], flops=2 * rows_in * wide * mid,
    )
    sums1, z1, *line = after(sums1, z1, *line)
    sums1, *line = after(sum_everywhere(sums1), *line)
    low, high = split_rows(line_gather_end(line))
    low, high, early_array, z1 = after(low, high, early_array, z1)
    w_spatial, w_expand = views(early_array, first_weights)
    low, high = gather_bit(low, 2, 1), gather_bit(high, 1, 2)
    tables_flat = early_array[:, -table_rows:].reshape(shards, -1)[:, : table_cells.size]
    tables_flat = tables_flat.reshape((shards,) + table_cells.shape)
    tables, at = [], 0
    for t in tables_all:
        width = t.shape[2]
        field = tables_flat[:, :, at : at + width].transpose(1, 0, 2)
        tables.append(field.reshape(2 * GROUPS, shards * width).astype(F32))
        at += width
    totals = sums1[2 * GROUPS, 0 : 128 * GROUPS : 128]
    side_real = group_side.astype(F32)
    half_real = (group_side // 2).astype(F32)
    counts_in = jnp.broadcast_to((totals * side_real * side_real)[:, None], (GROUPS, LANES))
    counts = jnp.broadcast_to((totals * half_real * half_real)[:, None], (GROUPS, LANES))
    counts_in, counts = fixed(counts_in), fixed(counts)
    onehot, gate = fixed(onehot), fixed(gate)
    limits_in, limits_out = fixed(limits_in), fixed(limits_out)
    keeps_in, keeps_out = fixed(keeps_in), fixed(keeps_out)

    z1_split = z1.reshape(split)
    row_split = (1, 2, half, 2, images, LANES)
    planes_shape = (2, 2, half + 1, half + 1, images, mid)
    planes, slope1, z2, sums2 = call(
        k_entry_spatial, "entry_spatial", half,
        [(z1_split, along(row_split, 0)), fixed(sums1), fixed(tables[0]), counts_in, counts,
         keeps_in, limits_out, onehot, w_spatial.every()],
        [(planes_shape, BF, whole(planes_shape)), (split, BF, along(row_split, 0)), small_out,
         sums_out],
        [acc], flops=18 * rows_out * mid * mid,
    )
    sums2, low, high = after(sums2, low, high)
    near, low, high = after(sum_near(sums2), low, high)
    low_other, high_other = xor_swap(low, 1 << 1), xor_swap(high, 1 << 2)
    sums2 = sum_far(near, LANES)
    a2, slope2, z3, sums3 = call(
        k_expand, "expand", blocks,
        [fixed(z2), fixed(sums2), fixed(tables[1]), counts, keeps_out, onehot,
         w_expand.moving()],
        [small_out, small_out, large_out, sums_wide], [acc], flops=2 * rows_out * mid * out,
    )
    z3, sums3, low_other, high_other = after(z3, sums3, low_other, high_other)
    low, high = pair(low, low_other, 1, 2), pair(high, high_other, 2, 1)
    values = [gather_bit(v, 0, 3) for v in (low, high)]
    gathered = jnp.concatenate(values, axis=4).reshape(devices, -1, LANES)
    w_project, w_ireduce = views(gathered, middle_weights)
    zs, sums_s = call(
        k_strided, "strided", blocks,
        [(x_split, whole((half, 1, half, 1, images, wide))), w_project.moving(), limits_out, onehot],
        [large_out, sums_wide], [acc], flops=2 * rows_out * wide * out,
    )
    joined = sum_everywhere(jnp.concatenate([sums3, sums_s], axis=1))
    sums3, sums_s = joined[:, :out], joined[:, out:]
    w_rows = w_ireduce.moving_rows(blocks)
    middle, slope3, z4, sums4 = call(
        k_middle, "middle", blocks,
        [column(z3), column(zs), column(sums3), column(sums_s), column(tables[2]),
         column(tables[3]), counts, limits_out, onehot, w_rows],
        [large_out, large_out, small_out, sums_out], [acc], flops=2 * rows_out * mid * out,
    )
    sums4 = sum_everywhere(sums4)
    padded_shape = (half + 2, half + 2, images, mid)
    padded4, slope4, z5, sums5 = call(
        k_inner_spatial, "inner_spatial", 1,
        [fixed(z4), fixed(sums4), fixed(tables[4]), counts, keeps_out, limits_out, onehot,
         w_ispatial.every()],
        [(padded_shape, BF, whole(padded_shape)), small_out, small_out, sums_out], [acc],
        flops=18 * rows_out * mid * mid,
    )
    sums5 = sum_everywhere(sums5)
    a5, slope5, z6, sums6 = call(
        k_expand, "inner_expand", blocks,
        [fixed(z5), fixed(sums5), fixed(tables[5]), counts, keeps_out, onehot,
         w_iexpand.moving()],
        [small_out, small_out, large_out, sums_wide], [acc], flops=2 * rows_out * mid * out,
    )
    sums6 = sum_everywhere(sums6)
    result, du6, back6 = call(
        k_close, "close", blocks,
        [column(z6), column(sums6), column(tables[6]), counts, limits_out, onehot, gate,
         column(middle), column(cot)],
        [large_out, large_out, sums_wide],
    )
    back6 = sum_everywhere(back6)
    dz6, du5, back5 = call(
        k_back_expand, "back_inner_expand", blocks,
        [column(du6), column(z6), column(sums6), column(back6), column(tables[6]), counts,
         limits_out, onehot, w_iexpand.moving(), fixed(slope5), fixed(z5), fixed(sums5)],
        [large_out, (small, F32, whole(small)), sums_out], [acc],
        flops=2 * rows_out * mid * out,
    )
    near, dz6 = after(sum_near(back5), dz6)
    back5 = sum_far(near, LANES)
    inner_grad, inner_rows = grads_into([inner_spatial, inner_expand])
    inner_grad(
        1, k_grad_columns, "inner_expand_grad", blocks, [fixed(a5), column(dz6)],
        2 * rows_out * mid * out, [pltpu.VMEM((mid, rows_out), BF)],
    )
    dz5, du4, back4 = call(
        k_back_inner_spatial, "back_inner_spatial", 1,
        [fixed(du5), fixed(z5), fixed(sums5), fixed(back5), fixed(tables[5]), counts, limits_out,
         onehot, w_ispatial.every(), fixed(slope4), fixed(z4), fixed(sums4)],
        [small_out, (small, F32, whole(small)), sums_out],
        [pltpu.VMEM(padded_shape, BF), acc], flops=18 * rows_out * mid * mid,
    )
    near, dz5 = after(sum_near(back4), dz5)
    inner_grad(
        0, k_taps, "inner_spatial_grad", 9, [fixed(padded4), fixed(dz5)], 18 * rows_out * mid * mid
    )
    late_rows, back4 = after(inner_rows().reshape(-1, LANES), sum_far(near, LANES))
    inner_own = lax.psum_scatter(late_rows, AXES, scatter_dimension=0, tiled=True)
    dz4, du3, back3 = call(
        k_back_middle, "back_middle", blocks,
        [fixed(du4), fixed(z4), fixed(sums4), fixed(back4), fixed(tables[4]), counts, limits_out,
         onehot, w_rows, gate, column(cot), column(du6), column(slope3), column(z3), column(zs),
         column(sums3), column(sums_s)],
        [small_out, large_out, ((16, out), F32, along((16, LANES), 1))], [acc],
        flops=2 * rows_out * mid * out,
    )
    near, dz4 = after(sum_near(back3), dz4)
    back3 = sum_far(near, out)
    middle_grads = [entry_project, inner_reduce, entry_expand]
    middle_grad, middle_rows = grads_into(middle_grads)
    middle_grad(
        1, k_grad, "inner_reduce_grad", blocks, [column(middle), fixed(dz4)],
        2 * rows_out * mid * out,
    )
    dz3, dzs, du2, back2 = call(
        k_back_entry_expand, "back_entry_expand", blocks,
        [column(du3), column(z3), column(zs), column(sums3), column(sums_s), column(back3),
         column(tables[2]), column(tables[3]), counts, limits_out, onehot, w_expand.moving(),
         fixed(slope2), fixed(z2), fixed(sums2)],
        [large_out, large_out, (small, F32, whole(small)), sums_out], [acc],
        flops=2 * rows_out * mid * out,
    )
    near, dz3, dzs = after(sum_near(back2), dz3, dzs)
    back2 = sum_far(near, LANES)
    middle_grad(
        2, k_grad_columns, "expand_grad", blocks, [fixed(a2), column(dz3)],
        2 * rows_out * mid * out, [pltpu.VMEM((mid, rows_out), BF)],
    )
    middle_grad(
        0, k_grad_strided, "project_grad", blocks,
        [(x_split, whole((half, 1, half, 1, images, wide))), column(dzs)],
        2 * rows_out * wide * out, [pltpu.VMEM((wide, rows_out), BF)],
    )
    low, high = cut_rows(halve_bit([[near_shape(middle_rows())]], 0, 3))
    low_sent, high_sent, back2 = after(halve_sent(low, 1, 2), halve_sent(high, 2, 1), back2)
    low, high = halve_end(low, low_sent, 1, 2), halve_end(high, high_sent, 2, 1)
    strided_shape = (half, half, images, wide)
    (d_strided,) = call(
        k_back_strided, "back_strided", blocks, [column(dzs), w_project.moving()],
        [(strided_shape, F32, whole(strided_shape))], flops=2 * rows_out * wide * out,
    )
    plane = (half, 1, half, 1, images, LANES)

    def parity(array):
        return (array, pl.BlockSpec(plane, lambda s: (0, s // 2, 0, s % 2, 0, 0)))

    dz2, du1, back1 = call(
        k_back_entry_spatial, "back_entry_spatial", 4,
        [fixed(du2), fixed(z2), fixed(sums2), fixed(back2), fixed(tables[1]), counts, counts_in,
         limits_out, onehot, w_spatial.every(), parity(slope1), parity(z1_split), fixed(sums1)],
        [small_out, (split, BF, parity(z1_split)[1]), sums_out],
        [pltpu.VMEM((half + 1, half + 1, images, mid), BF), pltpu.VMEM((2, images, mid), F32), acc],
        flops=18 * rows_out * mid * mid,
    )
    (g_spatial,) = call(
        k_taps_strided, "entry_spatial_grad", 9, [fixed(planes), fixed(dz2)],
        [grad_out(entry_spatial, 9)],
        flops=18 * rows_out * mid * mid,
    )
    spatial_rows = [[near_shape(grad_rows(g_spatial, entry_spatial))]]
    spatial_sent = halve_sent(spatial_rows, 0, 3)
    back1, low_sent, high_sent, spatial_sent, d_strided = after(
        back1, halve_sent(low, 2, 1), halve_sent(high, 1, 2), spatial_sent, d_strided
    )
    near, low_sent, high_sent = after(sum_near(back1), low_sent, high_sent)
    low, high = halve_end(low, low_sent, 2, 1), halve_end(high, high_sent, 1, 2)
    back1 = sum_far(near, LANES)
    spatial_rows = halve_end(spatial_rows, spatial_sent, 0, 3)
    two = (2, full, images, mid)
    taps, q = layout(entry_reduce)
    flat_shape = (devices, q, LANES) if q % 16 == 0 else (devices * q, LANES)
    dz1, g_reduce = call(
        k_back_first, "back_first", half,
        [(du1.reshape(z1.shape), along(two, 0)), (z1, along(two, 0)), fixed(sums1), fixed(back1),
         fixed(tables[0]), counts_in, limits_in, onehot, (x, along((2, full, images, wide), 0))],
        [(z1.shape, BF, along(two, 0)), (flat_shape, BF, whole(flat_shape))],
        [pltpu.VMEM((wide, mid), F32)], flops=2 * rows_in * wide * mid,
    )
    first_rows = [[added(v).astype(BF)] for v in low + high]
    first_rows, g_reduce, dz1, inner_own = flat_after(first_rows, g_reduce, dz1, inner_own)
    reduce_rows = halve_bit([[near_shape(grad_rows(g_reduce, entry_reduce))]], 0, 3)
    low, high = cut_rows(spatial_rows + reduce_rows)
    first_rows, low_sent, high_sent, dz1 = flat_after(
        first_rows, halve_sent(low, 1, 2), halve_sent(high, 2, 1), dz1
    )
    low, high = halve_end(low, low_sent, 1, 2), halve_end(high, high_sent, 2, 1)
    entry_own = far_scatter(first_rows)
    (d_inputs,) = call(
        k_input_grad, "input_grad", half,
        [(dz1, along(two, 0)), w_reduce.moving_all(),
         (d_strided, along((1, half, images, wide), 0))],
        [((full, full, images, wide), F32, along((2, full, images, wide), 0))],
        flops=2 * rows_in * wide * mid,
    )
    entry_own, low_sent, high_sent, d_inputs, inner_own = after(
        entry_own, halve_sent(low, 2, 1), halve_sent(high, 1, 2), d_inputs, inner_own
    )
    low, high = halve_end(low, low_sent, 2, 1), halve_end(high, high_sent, 1, 2)
    early_own = jnp.concatenate([entry_own, inner_own], axis=0).reshape(1, 1, -1, LANES)
    early_own = gather_copy(early_own, 1)
    last_rows = [[added(v).astype(BF)] for v in low + high]
    early_own, last_rows = flat_after(early_own, last_rows)
    last_own = far_scatter(last_rows)
    g_project, g_ireduce, g_expand, g_ispatial, g_iexpand = shares(
        gather_copy(early_own, 0), middle_grads + [inner_spatial, inner_expand]
    )
    last_own, g_project, g_ispatial = after(last_own, g_project, g_ispatial)
    last_own = gather_copy(last_own.reshape(1, 1, -1, LANES), 1)
    g_spatial, g_reduce = shares(gather_copy(last_own, 0), [entry_spatial, entry_reduce])

    def own_share(back, gain_at=0):
        width = back.shape[1] // shards
        own = lax.dynamic_slice_in_dim(back, position * width, width, 1)
        return jnp.stack([own[gain_at : gain_at + GROUPS], own[GROUPS : 2 * GROUPS]])

    return (
        result.transpose(2, 0, 1, 3),
        d_inputs.transpose(2, 0, 1, 3),
        g_reduce,
        g_spatial,
        g_expand,
        g_project,
        own_share(back1),
        own_share(back2),
        own_share(back3),
        own_share(back3, 2 * GROUPS),
        g_ireduce,
        g_ispatial,
        g_iexpand,
        own_share(back4),
        own_share(back5),
        own_share(back6),
    )


def solution(mesh):
    images = P(("dp", "rep"), None, None, None)
    rows = P("dp", None)
    taps = P(None, "dp", None)
    table = P(None, None, "dp")
    entry = (rows, taps, rows, rows, table, table, table, table)
    inner = (rows, taps, rows, table, table, table)
    return jax.shard_map(
        body,
        mesh=mesh,
        in_specs=(images, images, P(("dp", "rep")), P(), P(), P(), *entry, *inner),
        out_specs=(images, images, *entry, *inner),
        check_vma=False,
    )
```

```python
import functools

import jax
import jax.numpy as jnp
from jax import lax
from jax.experimental import pallas as pl
from jax.experimental.pallas import tpu as pltpu
from jax.sharding import PartitionSpec as P

EPSILON = 1e-05
AXES = ("dp", "rep")
BF = jnp.bfloat16
F32 = jnp.float32
GROUPS = 3
LANES = 512
VMEM = 24 * 1024 * 1024
LARGE = 1700 * 1000
NEAR = ("first",)


def xor_swap(value, distance):
    count = lax.axis_size("dp") * lax.axis_size("rep")
    return lax.ppermute(value, AXES, [(d, d ^ distance) for d in range(count)])


def own_bit(bit):
    me = lax.axis_index("dp") * lax.axis_size("rep") + lax.axis_index("rep")
    return lax.shift_right_logical(me, bit) & 1


def index_bits():
    count = lax.axis_size("dp") * lax.axis_size("rep")
    return count.bit_length() - 1


def sum_stages(value, bits):
    for stage in [bits[i : i + 2] for i in range(0, len(bits), 2)]:
        distances = [0]
        for bit in stage:
            distances = distances + [d | (1 << bit) for d in distances]
        for part in [xor_swap(value, d) for d in distances[1:]]:
            value = value + part
    return value


def sum_near(value):
    if value.size <= 8192:
        return sum_stages(value + xor_swap(value, 1), [1, 2])
    width = value.shape[1] // 2
    own = own_bit(0)
    kept = lax.dynamic_slice_in_dim(value, own * width, width, 1)
    sent = lax.dynamic_slice_in_dim(value, (1 - own) * width, width, 1)
    return sum_stages(kept + xor_swap(sent, 1), [1, 2])


def sum_far(value, columns):
    value = sum_stages(value, list(range(3, index_bits())))
    if value.shape[1] == columns:
        return value
    return pair(value, xor_swap(value, 1), 0, 1)


def sum_everywhere(value):
    return sum_far(sum_near(value), value.shape[1])


def after(*values):
    return lax.optimization_barrier(values)


def pair(value, other, bit, axis):
    own = own_bit(bit)
    return jnp.concatenate(
        [jnp.where(own == 0, value, other), jnp.where(own == 0, other, value)], axis=axis
    )


def gather_bit(value, bit, axis):
    return pair(value, xor_swap(value, 1 << bit), bit, axis)


def gather_rows(part, others):
    count = index_bits()
    value = part.reshape((1,) * count + part.shape)
    for bit in list(range(3, count)) + [2, 1, 0]:
        value = gather_bit(value, bit, count - 1 - bit)
        if bit == 3:
            value, *others = after(value, *others)
    return value.reshape((-1,) + part.shape), others


def split_rows(value):
    total = value.shape[-2]
    cut = total // 32 * 16 or total // 2
    return value[..., :cut, :], value[..., cut:, :]


def is_line():
    return lax.axis_size("dp") == 8 and lax.axis_size("rep") == 4


def line_place():
    return lax.axis_index("dp") // 2


def line_shift(value, step, among=range(4)):
    pairs = [
        (p * 8 + i, (p + step) * 8 + i) for p in among for i in range(8) if 0 <= p + step < 4
    ]
    return lax.ppermute(value, AXES, pairs)


def line_gather_start(part):
    if not is_line():
        return (part,)
    return part, line_shift(part, 1), line_shift(part, -1)


def line_gather_end(parts):
    part = parts[0]
    if not is_line():
        count = index_bits()
        value = part.reshape((1,) * count + part.shape)
        for bit in range(3, count):
            value = gather_bit(value, bit, count - 1 - bit)
        return value.reshape((-1, 1, 1, 1) + part.shape)
    right, left = [parts[1]], [parts[2]]
    for _ in range(2):
        right.append(line_shift(right[-1], 1))
        left.append(line_shift(left[-1], -1))
    row = jnp.stack(right[::-1] + [part] + left)
    row = lax.dynamic_slice_in_dim(row, 3 - line_place(), 4, 0)
    return row.reshape((4, 1, 1, 1) + part.shape)


def added(parts):
    total = parts[0].astype(F32)
    for part in parts[1:]:
        total = total + part.astype(F32)
    return total


def halves(segments, bit, axis, other):
    index = own_bit(bit) ^ other
    return [[lax.dynamic_slice_in_dim(p, index, 1, axis) for p in s] for s in segments]


def halve_sent(segments, bit, axis):
    sent = [added(parts).astype(BF) for parts in halves(segments, bit, axis, 1)]
    return sent[0] if len(sent) == 1 else jnp.concatenate(sent, axis=-2)


def halve_end(segments, sent, bit, axis):
    got = xor_swap(sent, 1 << bit)
    result, at = [], 0
    for parts in halves(segments, bit, axis, 0):
        count = parts[0].shape[-2]
        result.append(parts + [lax.slice_in_dim(got, at, at + count, axis=got.ndim - 2)])
        at += count
    return result


def halve_bit(segments, bit, axis):
    return halve_end(segments, halve_sent(segments, bit, axis), bit, axis)


def cut_rows(segments):
    total = sum(s[0].shape[-2] for s in segments)
    cut = total // 32 * 16 or total // 2
    low, high, at = [], [], 0
    for s in segments:
        count = s[0].shape[-2]
        here = min(max(cut - at, 0), count)
        if here:
            low.append([p[..., :here, :] for p in s])
        if here < count:
            high.append([p[..., here:, :] for p in s])
        at += count
    return low, high


def flat_after(*values):
    leaves, tree = jax.tree.flatten(values)
    return jax.tree.unflatten(tree, lax.optimization_barrier(leaves))


def near_shape(value):
    return value.reshape((-1, 2, 2, 2) + value.shape[1:])


def far_scatter(segments):
    if not is_line():
        count = index_bits() - 3
        values = [[p.reshape((2,) * count + p.shape[-2:]) for p in s] for s in segments]
        for step in range(count):
            values = halve_bit(values, step + 3, count - 1 - step)
        values = [added(s).reshape((-1, LANES)).astype(BF) for s in values]
        return jnp.concatenate(values, axis=0)

    def block(index):
        parts = [
            added([lax.dynamic_index_in_dim(p, index, 0, keepdims=False) for p in s])
            for s in segments
        ]
        return jnp.concatenate(parts, axis=-2) if len(parts) > 1 else parts[0]

    place = line_place()
    parts = [block(place)]
    for k in (1, 2, 3):
        parts.append(xor_swap(block(place ^ k).astype(BF), k << 3))
    return added(parts).reshape((-1, LANES)).astype(BF)


def gather_copy(value, bit):
    return gather_bit(value, bit, 1 - bit)


def gelu_parts(u):
    k = 0.7978845608028654
    square = u * u
    half = 0.5 + 0.5 * jnp.tanh(u * (k + (0.044715 * k) * square))
    slope = half * (1.0 + u * (1.0 - half) * (2 * k + (6 * 0.044715 * k) * square))
    return u * half, slope


def dot(a, b):
    return lax.dot_general(a, b, (((1,), (0,)), ((), ())), preferred_element_type=F32)


def dot_nt(a, b):
    return lax.dot_general(a, b, (((1,), (1,)), ((), ())), preferred_element_type=F32)


def dot_tn(a, b):
    return lax.dot_general(a, b, (((0,), (0,)), ((), ())), preferred_element_type=F32)


def flat(field):
    return field.reshape(-1, field.shape[-1])


def whole(shape):
    return pl.BlockSpec(shape, lambda *_: (0,) * len(shape), pipeline_mode=pl.Buffered(1))


def along(shape, axis):
    return pl.BlockSpec(shape, lambda s: tuple(s if a == axis else 0 for a in range(len(shape))))


class Weight:
    def __init__(self, gathered, at, taps, q):
        if q % 16 == 0:
            self.array, self.at, self.taps, self.q = gathered, at, taps, q
        else:
            devices = gathered.shape[0]
            field = gathered[:, at : at + taps * q].reshape(devices, taps, q, LANES)
            field = field.transpose(1, 0, 2, 3).reshape(1, taps * devices * q, LANES)
            self.array, self.at, self.taps, self.q = field, 0, taps, devices * q

    def held(self):
        return pltpu.with_memory_space_constraint(self.array, pltpu.HBM)

    def spec(self, rows, index, mode=None):
        return pl.BlockSpec((self.array.shape[0], rows, LANES), index, pipeline_mode=mode)

    def chunk(self, at, count):
        rows = count * self.q
        place = at // rows
        return (self.held(), self.spec(rows, lambda *_: (0, place, 0), pl.Buffered(1)))

    def every(self):
        chunks, left, at = [], self.taps, self.at
        while left:
            count = left
            while at % (count * self.q):
                count -= 1
            chunks.append(self.chunk(at, count))
            at += count * self.q
            left -= count
        return chunks

    def moving(self):
        first = self.at // self.q
        return (self.held(), self.spec(self.q, lambda s: (0, first + s, 0)))

    def moving_all(self):
        return self.chunk(self.at, self.taps)

    def moving_rows(self, steps):
        devices = self.array.shape[0]
        if devices > 1:
            place = self.at // self.q
            return (
                self.held(),
                pl.BlockSpec((devices // steps, self.q, LANES), lambda s: (s, place, 0)),
            )
        return (self.held(), pl.BlockSpec((1, self.q // steps, LANES), lambda s: (0, s, 0)))


class Taps:
    def __init__(self, refs, total):
        self.refs = refs
        self.q = sum(r.shape[1] for r in refs) // total

    def __getitem__(self, t):
        row = t * self.q
        for ref in self.refs:
            if row < ref.shape[1]:
                return flat(ref[:, row : row + self.q])
            row -= ref.shape[1]


def call(kernel, name, steps, ins, outs, scratch=(), flops=0, into=None):
    groups = [i if isinstance(i, list) else [i] for i in ins]
    arrays = [a for g in groups for a, _ in g]
    size = sum(a.size * a.dtype.itemsize for a in arrays)

    def body(*refs):
        params, at = [], 0
        for i, g in zip(ins, groups):
            some = refs[at : at + len(g)]
            params.append(Taps(some, 9) if isinstance(i, list) else some[0])
            at += len(g)
        kernel(*params, *refs[at + (into is not None) :])

    given = [] if into is None else [into]
    arrays = [
        pltpu.with_memory_space_constraint(a, pltpu.HBM) if a.nbytes > LARGE and name not in NEAR else a
        for a in arrays
    ]

    def result(shape, dtype):
        size = dtype.dtype.itemsize
        for extent in shape:
            size *= extent
        return (pltpu.HBM if size > LARGE else jax.ShapeDtypeStruct)(shape, dtype)


    return pl.pallas_call(
        body,
        name=name,
        grid=(steps,),
        in_specs=[s for g in groups for _, s in g] + [pl.BlockSpec(memory_space=pl.ANY)] * len(given),
        input_output_aliases={len(arrays): 0} if given else {},
        out_specs=[s for _, _, s in outs],
        out_shape=[result(shape, dtype) for shape, dtype, _ in outs],
        scratch_shapes=list(scratch),
        compiler_params=pltpu.CompilerParams(
            vmem_limit_bytes=VMEM, dimension_semantics=("arbitrary",)
        ),
        cost_estimate=pl.CostEstimate(flops=flops, bytes_accessed=size, transcendentals=0),
    )(*arrays, *given)


def rows3(ref, first):
    return [ref[first + g : first + g + 1, :] for g in range(GROUPS)]


def spread(onehot, rows):
    total = onehot[0] * rows[0]
    for g in range(1, GROUPS):
        total = total + onehot[g] * rows[g]
    return total


def group_rows(onehot, *sums):
    rows = [
        jnp.sum(onehot[g] * image, axis=0, keepdims=True) for image in sums for g in range(GROUPS)
    ]
    return rows


def put_rows(ref, rows):
    for r, row in enumerate(rows):
        ref[r : r + 1, :] = row
    if len(rows) < ref.shape[0]:
        ref[len(rows) :, :] = jnp.zeros((ref.shape[0] - len(rows), ref.shape[1]), F32)


def moments(sums, counts):
    first, second, count = rows3(sums, 0), rows3(sums, GROUPS), rows3(counts, 0)
    center = [a / c for a, c in zip(first, count)]
    inverse = [lax.rsqrt(b / c - m * m + EPSILON) for b, c, m in zip(second, count, center)]
    return center, inverse


def forward_coefs(sums, table, counts, onehot):
    center, inverse = moments(sums, counts)
    scale = [a * i for a, i in zip(rows3(table, 0), inverse)]
    shift = [b - m * s for b, m, s in zip(rows3(table, GROUPS), center, scale)]
    return spread(onehot, scale), spread(onehot, shift)


def backward_coefs(sums, back, table, counts, onehot, gain_at=0):
    center, inverse = moments(sums, counts)
    count = rows3(counts, 0)
    factor = [a * i for a, i in zip(rows3(table, 0), inverse)]
    gain = [g / c for g, c in zip(rows3(back, gain_at), count)]
    bias = [b / c for b, c in zip(rows3(back, GROUPS), count)]
    on_z = [-f * i * g for f, i, g in zip(factor, inverse, gain)]
    on_one = [f * (m * i * g - b) for f, m, i, g, b in zip(factor, center, inverse, gain, bias)]
    return spread(onehot, factor), spread(onehot, on_z), spread(onehot, on_one)


def gain_rows(sums, counts, onehot, with_z, plain):
    center, inverse = moments(sums, counts)
    raw_z, raw = group_rows(onehot, with_z), group_rows(onehot, plain)
    return [i * (e - m * d) for i, e, m, d in zip(inverse, raw_z, center, raw)]


def inside(limits, row, count, step=1, start=0):
    column = lax.broadcasted_iota(jnp.int32, (count,) + limits.shape, 0) * step + start
    return (column < limits[None]) & (row < limits)[None]


def add_stats(values, mask, first, second):
    kept = jnp.where(mask, values, 0.0)
    return first + jnp.sum(kept, axis=0), second + jnp.sum(kept * values, axis=0)


def k_first(x, w, limits, onehot, count_row, z, sums, acc):
    step = pl.program_id(0)

    @pl.when(step == 0)
    def _():
        acc[...] = jnp.zeros_like(acc)

    rows, cols = x.shape[0], x.shape[1]
    values = dot(flat(x[...]), flat(w[...])).reshape(rows, cols, x.shape[2], LANES)
    z[...] = values.astype(BF)
    first, second = acc[0], acc[1]
    for r in range(rows):
        mask = inside(limits[...], step * rows + r, cols)
        first, second = add_stats(values[r], mask, first, second)
    acc[0] = first
    acc[1] = second

    @pl.when(step == pl.num_programs(0) - 1)
    def _():
        put_rows(sums, group_rows(onehot, first, second) + [count_row[0:1, :]])


def stats_of(field, limits, onehot, z, sums):
    side = field.shape[0]
    shape = field.shape[2:]

    def row(i, carry):
        values = field[i]
        z[i] = values.astype(BF)
        if limits is None:
            return carry[0] + jnp.sum(values, axis=0), carry[1] + jnp.sum(values * values, axis=0)
        return add_stats(values, inside(limits[...], i, side), *carry)

    first, second = lax.fori_loop(
        0, side, row, (jnp.zeros(shape, F32), jnp.zeros(shape, F32)), unroll=True
    )
    put_rows(sums, group_rows(onehot, first, second))


def k_strided(x, w, limits, onehot, z, sums, acc):
    side = z.shape[0]
    acc[...] = dot(flat(x[:, 0, :, 0]), flat(w[...])).reshape(acc.shape)
    stats_of(acc, limits, onehot, z, sums)


def k_entry_spatial(
    z1, in_sums, table, counts, counts_out, limits, limits_out, onehot, w,
    planes, slope, z2, sums, acc,
):
    step = pl.program_id(0)
    side = z2.shape[0]

    @pl.when(step == 0)
    def _():
        planes[1, :, 0] = jnp.zeros(planes.shape[1:2] + planes.shape[3:], BF)
        planes[:, 1, :, 0] = jnp.zeros(planes.shape[:1] + planes.shape[2:3] + planes.shape[4:], BF)

    scale, shift = forward_coefs(in_sums, table, counts, onehot)
    for a in range(2):
        for b in range(2):
            u = z1[0, a, :, b].astype(F32) * scale + shift
            act, grad = gelu_parts(u)
            mask = inside(limits[...], 2 * step + a, side, 2, b)
            planes[a, b, step + a, b : b + side] = jnp.where(mask, act, 0.0).astype(BF)
            slope[0, a, :, b] = jnp.where(mask, grad, 0.0).astype(BF)

    @pl.when(step == pl.num_programs(0) - 1)
    def _():
        for t in range(9):
            v, h = t // 3, t % 3
            rows = planes[(v + 1) % 2, (h + 1) % 2, v // 2 : v // 2 + side, h // 2 : h // 2 + side]
            part = dot(flat(rows), w[t]).reshape(acc.shape)
            if t == 0:
                acc[...] = part
            else:
                acc[...] += part
        stats_of(acc, limits_out, onehot, z2, sums)


def activate(z, coefs, limits, store):
    scale, shift = coefs
    side = z.shape[0]

    def row(i, carry):
        act, grad = gelu_parts(z[i].astype(F32) * scale + shift)
        mask = inside(limits[...], i, side)
        store(i, jnp.where(mask, act, 0.0).astype(BF), jnp.where(mask, grad, 0.0).astype(BF))
        return carry

    lax.fori_loop(0, side, row, 0, unroll=True)


def k_expand(z, in_sums, table, counts, keeps, onehot, w, a, slope, z_out, sums, acc):
    @pl.when(pl.program_id(0) == 0)
    def _():
        def store(i, act, grad):
            a[i] = act
            slope[i] = grad

        activate(z, forward_coefs(in_sums, table, counts, onehot), keeps, store)

    acc[...] = dot(flat(a[...]), flat(w[...])).reshape(acc.shape)
    stats_of(acc, None, onehot, z_out, sums)


def k_middle(
    z3, zs, sums3, sums_s, table3, table_s, counts, limits, onehot, w,
    middle, slope, z4, sums, acc,
):
    step = pl.program_id(0)
    side = z3.shape[0]
    scale, shift = forward_coefs(sums3, table3, counts, onehot)
    scale_s, shift_s = forward_coefs(sums_s, table_s, counts, onehot)
    shift = shift + shift_s

    def row(i, carry):
        act, grad = gelu_parts(z3[i].astype(F32) * scale + zs[i].astype(F32) * scale_s + shift)
        mask = inside(limits[...], i, side)
        middle[i] = jnp.where(mask, act, 0.0).astype(BF)
        slope[i] = jnp.where(mask, grad, 0.0).astype(BF)
        return carry

    lax.fori_loop(0, side, row, 0, unroll=True)
    part = dot(flat(middle[...]), flat(w[...])).reshape(acc.shape)

    @pl.when(step == 0)
    def _():
        acc[...] = part

    @pl.when(step > 0)
    def _():
        acc[...] += part

    @pl.when(step == pl.num_programs(0) - 1)
    def _():
        stats_of(acc, None, onehot, z4, sums)


def clear_edges(padded):
    edge = jnp.zeros(padded.shape[1:], BF)
    last = padded.shape[0] - 1
    padded[0] = edge
    padded[last] = edge
    for i in range(1, last):
        padded[i, 0] = edge[0]
        padded[i, last] = edge[0]


def k_inner_spatial(z4, in_sums, table, counts, keeps, limits, onehot, w, padded, slope, z5, sums, acc):
    side = z4.shape[0]
    clear_edges(padded)

    def store(i, act, grad):
        padded[i + 1, 1 : 1 + side] = act
        slope[i] = grad

    activate(z4, forward_coefs(in_sums, table, counts, onehot), keeps, store)
    for t in range(9):
        v, h = t // 3, t % 3
        part = dot(flat(padded[v : v + side, h : h + side]), w[t]).reshape(acc.shape)
        if t == 0:
            acc[...] = part
        else:
            acc[...] += part
    stats_of(acc, limits, onehot, z5, sums)


def k_close(z6, in_sums, table, counts, limits, onehot, gate, middle, cot, result, du6, sums):
    side = z6.shape[0]
    scale, shift = forward_coefs(in_sums, table, counts, onehot)
    opened = gate[...]
    zero = jnp.zeros(opened.shape, F32)

    def row(i, carry):
        plain, with_z = carry
        z = z6[i].astype(F32)
        mid = middle[i].astype(F32)
        act, grad = gelu_parts(z * scale + shift + mid)
        mask = inside(limits[...], i, side)
        closed = jnp.where(mask, act, 0.0)
        result[i] = (mid + opened * (closed - mid)).astype(BF)
        du = jnp.where(mask, grad, 0.0) * opened * cot[i].astype(F32)
        du6[i] = du.astype(BF)
        return plain + jnp.sum(du, axis=0), with_z + jnp.sum(du * z, axis=0)

    plain, with_z = lax.fori_loop(0, side, row, (zero, zero), unroll=True)
    put_rows(
        sums,
        gain_rows(in_sums, counts, onehot, with_z, plain) + group_rows(onehot, plain),
    )


def finish_back(acc, slope, z, in_sums, counts, onehot, du_out, sums):
    zero = jnp.zeros(slope.shape[2:], F32)

    def row(i, carry):
        plain, with_z = carry
        du = acc[i] * slope[i].astype(F32)
        du_out[i] = du.astype(du_out.dtype)
        return plain + jnp.sum(du, axis=0), with_z + jnp.sum(du * z[i].astype(F32), axis=0)

    plain, with_z = lax.fori_loop(0, slope.shape[0], row, (zero, zero), unroll=True)
    put_rows(
        sums,
        gain_rows(in_sums, counts, onehot, with_z, plain) + group_rows(onehot, plain),
    )


def norm_back(du, z, coefs, limits, store):
    factor, on_z, on_one = coefs
    side = z.shape[0]

    def row(i, carry):
        dz = du[i].astype(F32) * factor + z[i].astype(F32) * on_z + on_one
        store(i, jnp.where(inside(limits[...], i, side), dz, 0.0).astype(BF))
        return carry

    lax.fori_loop(0, side, row, 0, unroll=True)


def k_back_expand(
    du6, z6, sums6, back6, table6, counts, limits, onehot, w, slope, z5, sums5,
    dz6, du5, sums, acc,
):
    step = pl.program_id(0)

    def store(i, dz):
        dz6[i] = dz

    norm_back(du6, z6, backward_coefs(sums6, back6, table6, counts, onehot), limits, store)
    part = dot_nt(flat(dz6[...]), flat(w[...])).reshape(acc.shape)

    @pl.when(step == 0)
    def _():
        acc[...] = part

    @pl.when(step > 0)
    def _():
        acc[...] += part

    @pl.when(step == pl.num_programs(0) - 1)
    def _():
        finish_back(acc, slope, z5, sums5, counts, onehot, du5, sums)


def k_back_inner_spatial(
    du5, z5, sums5, back5, table5, counts, limits, onehot, w, slope, z4, sums4,
    dz5, du4, sums, padded, acc,
):
    side = z5.shape[0]
    clear_edges(padded)

    def store(i, dz):
        dz5[i] = dz
        padded[i + 1, 1 : 1 + side] = dz

    norm_back(du5, z5, backward_coefs(sums5, back5, table5, counts, onehot), limits, store)
    for t in range(9):
        v, h = t // 3, t % 3
        rows = padded[2 - v : 2 - v + side, 2 - h : 2 - h + side]
        part = dot_nt(flat(rows), w[t]).reshape(acc.shape)
        if t == 0:
            acc[...] = part
        else:
            acc[...] += part
    finish_back(acc, slope, z4, sums4, counts, onehot, du4, sums)


def k_back_middle(
    du4, z4, sums4, back4, table4, counts, limits, onehot, w, gate, cot, du6, slope3,
    z3, zs, sums3, sums_s, dz4, du3, sums, acc,
):
    side = z4.shape[0]

    @pl.when(pl.program_id(0) == 0)
    def _():
        def store(i, dz):
            dz4[i] = dz

        norm_back(du4, z4, backward_coefs(sums4, back4, table4, counts, onehot), limits, store)

    acc[...] = dot_nt(flat(dz4[...]), flat(w[...])).reshape(acc.shape)
    shut = 1.0 - gate[...]
    zero = jnp.zeros(shut.shape, F32)

    def row(i, carry):
        plain, with_z3, with_zs = carry
        grad = shut * cot[i].astype(F32) + du6[i].astype(F32) + acc[i]
        du = grad * slope3[i].astype(F32)
        du3[i] = du.astype(BF)
        return (
            plain + jnp.sum(du, axis=0),
            with_z3 + jnp.sum(du * z3[i].astype(F32), axis=0),
            with_zs + jnp.sum(du * zs[i].astype(F32), axis=0),
        )

    plain, with_z3, with_zs = lax.fori_loop(0, side, row, (zero, zero, zero), unroll=True)
    put_rows(
        sums,
        gain_rows(sums3, counts, onehot, with_z3, plain)
        + group_rows(onehot, plain)
        + gain_rows(sums_s, counts, onehot, with_zs, plain),
    )


def k_back_entry_expand(
    du3, z3, zs, sums3, sums_s, back3, table3, table_s, counts, limits, onehot, w,
    slope, z2, sums2, dz3, dzs, du2, sums, acc,
):
    step = pl.program_id(0)
    side = z3.shape[0]
    factor, on_z, on_one = backward_coefs(sums3, back3, table3, counts, onehot)
    factor_s, on_zs, on_one_s = backward_coefs(
        sums_s, back3, table_s, counts, onehot, 2 * GROUPS
    )

    def row(i, carry):
        du = du3[i].astype(F32)
        mask = inside(limits[...], i, side)
        dz = du * factor + z3[i].astype(F32) * on_z + on_one
        dz3[i] = jnp.where(mask, dz, 0.0).astype(BF)
        dz = du * factor_s + zs[i].astype(F32) * on_zs + on_one_s
        dzs[i] = jnp.where(mask, dz, 0.0).astype(BF)
        return carry

    lax.fori_loop(0, side, row, 0, unroll=True)
    part = dot_nt(flat(dz3[...]), flat(w[...])).reshape(acc.shape)

    @pl.when(step == 0)
    def _():
        acc[...] = part

    @pl.when(step > 0)
    def _():
        acc[...] += part

    @pl.when(step == pl.num_programs(0) - 1)
    def _():
        finish_back(acc, slope, z2, sums2, counts, onehot, du2, sums)


def k_back_strided(dzs, w, out):
    part = dot_nt(flat(dzs[...]), flat(w[...])).reshape(out.shape)

    @pl.when(pl.program_id(0) == 0)
    def _():
        out[...] = part

    @pl.when(pl.program_id(0) > 0)
    def _():
        out[...] += part


def k_back_entry_spatial(
    du2, z2, sums2, back2, table2, counts, counts_in, limits, onehot, w, slope, z1, sums1,
    dz2, du1, sums, padded, total, acc,
):
    step = pl.program_id(0)
    side = z2.shape[0]

    @pl.when(step == 0)
    def _():
        total[...] = jnp.zeros_like(total)
        padded[...] = jnp.zeros_like(padded)

        def store(i, dz):
            dz2[i] = dz
            padded[i, 0:side] = dz

        norm_back(du2, z2, backward_coefs(sums2, back2, table2, counts, onehot), limits, store)

    steps = {0: [(1, 0)], 1: [(2, 0), (0, 1)]}
    for a in range(2):
        for b in range(2):

            @pl.when(step == 2 * a + b)
            def _():
                started = False
                for v, down in steps[a]:
                    for h, right in steps[b]:
                        rows = padded[down : down + side, right : right + side]
                        part = dot_nt(flat(rows), w[3 * v + h]).reshape(acc.shape)
                        if started:
                            acc[...] += part
                        else:
                            acc[...] = part
                        started = True

    def row(i, carry):
        plain, with_z = carry
        du = acc[i] * slope[i, 0, :, 0].astype(F32)
        du1[i, 0, :, 0] = du.astype(BF)
        z = z1[i, 0, :, 0].astype(F32)
        return plain + jnp.sum(du, axis=0), with_z + jnp.sum(du * z, axis=0)

    plain, with_z = lax.fori_loop(0, side, row, (total[0], total[1]), unroll=True)
    total[0] = plain
    total[1] = with_z

    @pl.when(step == pl.num_programs(0) - 1)
    def _():
        put_rows(
            sums,
            gain_rows(sums1, counts_in, onehot, with_z, plain) + group_rows(onehot, plain),
        )


def k_back_first(du1, z1, sums1, back1, table1, counts, limits, onehot, x, dz1, grad, acc):
    step = pl.program_id(0)
    rows, cols = du1.shape[0], du1.shape[1]
    factor, on_z, on_one = backward_coefs(sums1, back1, table1, counts, onehot)
    for r in range(rows):
        dz = du1[r].astype(F32) * factor + z1[r].astype(F32) * on_z + on_one
        mask = inside(limits[...], rows * step + r, cols)
        dz1[r] = jnp.where(mask, dz, 0.0).astype(BF)
    part = dot_tn(flat(x[...]), flat(dz1[...]))

    @pl.when(step == 0)
    def _():
        acc[...] = part

    @pl.when(step > 0)
    def _():
        acc[...] += part

    @pl.when(step == pl.num_programs(0) - 1)
    def _():
        grad[...] = acc[...].astype(BF).reshape(grad.shape)


def k_input_grad(dz1, w, strided, dx):
    rows, cols = dz1.shape[0], dz1.shape[1]
    weights = flat(w[...])
    for r in range(rows):
        dx[r] = dot_nt(flat(dz1[r]), weights).reshape(dx.shape[1:])
    for j in range(cols // 2):
        dx[0, 2 * j] += strided[0, j]


def k_grad(source, dz, out):
    out[...] = dot_tn(flat(source[...]), flat(dz[...])).astype(BF).reshape(out.shape)


def k_grad_columns(source, dz, out, turned):
    @pl.when(pl.program_id(0) == 0)
    def _():
        turned[...] = flat(source[...]).T

    out[...] = dot(turned[...], flat(dz[...])).astype(BF).reshape(out.shape)


def k_grad_strided(x, dz, out, turned):
    k_grad_columns(x.at[:, 0, :, 0], dz, out, turned)


def k_taps(field, dz, out):
    t = pl.program_id(0)
    v, h = t // 3, t % 3
    side = dz.shape[0]
    rows = field[pl.ds(v, side), pl.ds(h, side)]
    out[...] = dot_tn(flat(rows), flat(dz[...])).astype(BF).reshape(out.shape)


def k_taps_strided(planes, dz, out):
    t = pl.program_id(0)
    v, h = t // 3, t % 3
    side = dz.shape[0]
    rows = planes[(v + 1) % 2, (h + 1) % 2, pl.ds(v // 2, side), pl.ds(h // 2, side)]
    out[...] = dot_tn(flat(rows), flat(dz[...])).astype(BF).reshape(out.shape)


def body(
    inputs,
    cotangent,
    image_group,
    group_side,
    group_width,
    group_depth,
    entry_reduce,
    entry_spatial,
    entry_expand,
    entry_project,
    entry_norm_reduce,
    entry_norm_spatial,
    entry_norm_expand,
    entry_norm_project,
    inner_reduce,
    inner_spatial,
    inner_expand,
    inner_norm_reduce,
    inner_norm_spatial,
    inner_norm_expand,
):
    images, full, _, wide = inputs.shape
    half = full // 2
    mid, out = entry_reduce.shape[1], entry_expand.shape[1]
    blocks = out // LANES
    shards, copies = lax.axis_size("dp"), lax.axis_size("rep")
    devices = shards * copies
    position, copy = lax.axis_index("dp"), lax.axis_index("rep")

    onehot_int = (image_group[None, :] == jnp.arange(GROUPS, dtype=jnp.int32)[:, None]).astype(
        jnp.int32
    )
    own_side = jnp.sum(onehot_int * group_side[:, None], axis=0)
    own_width = jnp.sum(onehot_int * group_width[:, None], axis=0)
    own_gate = jnp.sum(onehot_int * group_depth[:, None], axis=0)

    def lanes(vector):
        return jnp.broadcast_to(vector[:, None], (images, LANES))

    onehot = jnp.broadcast_to(
        onehot_int.astype(F32)[:, :, None], (GROUPS, images, LANES)
    )
    gate = lanes(own_gate).astype(F32)
    limits_in, limits_out = lanes(own_side), lanes(own_side // 2)
    kept = jnp.arange(mid, dtype=jnp.int32)[None, :] < (own_width * mid // 4)[:, None]
    keeps_in = jnp.where(kept, limits_in, 0)
    keeps_out = jnp.where(kept, limits_out, 0)

    def quarter(weights):
        rows = weights.shape[-2] // copies
        part = lax.dynamic_slice_in_dim(weights, copy * rows, rows, weights.ndim - 2)
        part = part.reshape((-1,) + part.shape[-2:])
        return flat(
            jnp.concatenate(
                [part[..., i : i + LANES] for i in range(0, part.shape[-1], LANES)], axis=0
            )
        )

    def layout(weights):
        taps = weights.shape[0] if weights.ndim == 3 else weights.shape[1] // LANES
        return taps, weights.shape[-2] // copies

    def joined(weights):
        parts = [quarter(w) for w in weights]
        return parts[0] if len(parts) == 1 else jnp.concatenate(parts, axis=0)

    def views(gathered, weights):
        result, at = [], 0
        for w in weights:
            taps, q = layout(w)
            result.append(Weight(gathered, at, taps, q))
            at += taps * q
        return result

    def everywhere(weights):
        return views(lax.all_gather(joined(weights), AXES, axis=0, tiled=False), weights)

    def shares(own, weights):
        gathered = own.reshape((copies,) + own.shape[-2:])
        result, at = [], 0
        for w in weights:
            taps, q = layout(w)
            field = gathered[:, at : at + taps * q].reshape(copies, taps, q, LANES)
            if w.ndim == 3:
                field = field.transpose(1, 0, 2, 3)
            else:
                field = field.transpose(0, 2, 1, 3)
            result.append(field.reshape(w.shape).astype(F32))
            at += taps * q
        return result

    def packs(weights):
        return all(layout(w)[1] % 16 == 0 for w in weights)

    def grad_out(weights, steps, at=0, total=None):
        taps, q = layout(weights)
        if q % 16:
            shape = (taps * devices * q, LANES)
            return (shape, BF, pl.BlockSpec((shape[0] // steps, LANES), lambda s: (s, 0)))
        shape = (devices, total or taps * q, LANES)
        first = at // q
        if taps > 1:
            return (shape, BF, pl.BlockSpec((devices, q, LANES), lambda s: (0, first + s, 0)))
        return (shape, BF, pl.BlockSpec((devices // steps, q, LANES), lambda s: (s, first, 0)))

    def grad_rows(grad, weights):
        taps, q = layout(weights)
        if q % 16 == 0:
            return grad
        field = grad.reshape(taps, devices, q, LANES).transpose(1, 0, 2, 3)
        return field.reshape(devices, taps * q, LANES)

    def grads_into(weights):
        total = sum(layout(w)[0] * layout(w)[1] for w in weights)
        results = {}

        def run(index, kernel, name, steps, ins, flops, scratch=()):
            w = weights[index]
            at = sum(layout(v)[0] * layout(v)[1] for v in weights[:index])
            if packs(weights):
                (results["all"],) = call(
                    kernel, name, steps, ins, [grad_out(w, steps, at, total)], scratch, flops,
                    into=results.get("all"),
                )
            else:
                (results[index],) = call(kernel, name, steps, ins, [grad_out(w, steps)], scratch, flops)

        def whole_rows():
            if "all" in results:
                return results["all"]
            return jnp.concatenate(
                [grad_rows(results[i], w) for i, w in enumerate(weights)], axis=1
            )

        return run, whole_rows

    tables_all = (
        entry_norm_reduce,
        entry_norm_spatial,
        entry_norm_expand,
        entry_norm_project,
        inner_norm_reduce,
        inner_norm_spatial,
        inner_norm_expand,
    )
    table_cells = jnp.concatenate(tables_all, axis=2).reshape(2 * GROUPS, -1)
    table_rows = -(-table_cells.size // (copies * LANES))
    table_part = jnp.pad(
        table_cells.reshape(-1), (0, copies * table_rows * LANES - table_cells.size)
    ).reshape(copies, table_rows, LANES)
    table_part = lax.dynamic_index_in_dim(table_part, copy, 0, keepdims=False)
    middle_weights = [entry_project, inner_reduce]
    last_weights = [inner_spatial, inner_expand]
    first_weights = [entry_spatial, entry_expand]
    early_array = lax.all_gather(
        jnp.concatenate([joined(first_weights), table_part], axis=0), AXES, axis=0, tiled=False
    )
    w_spatial, w_expand = views(early_array, first_weights)
    first_array, others = gather_rows(quarter(entry_reduce), middle_weights + last_weights)
    w_ispatial, w_iexpand = everywhere(others[2:])
    first_array, part = after(first_array, joined(others[:2]))
    (w_reduce,) = views(first_array, [entry_reduce])
    line = line_gather_start(part)
    x = inputs.transpose(1, 2, 0, 3)
    x_split = x.reshape(half, 2, half, 2, images, wide)
    cot = cotangent.transpose(1, 2, 0, 3)

    small = (half, half, images, LANES)
    large = (half, half, images, out)
    split = (half, 2, half, 2, images, LANES)
    rows_out, rows_in = half * half * images, full * full * images
    six = (2 * GROUPS, LANES)
    sums_block = (8, LANES)

    def fixed(array):
        return (array, whole(array.shape))

    def column(array):
        return (array, along(array.shape[:-1] + (LANES,), array.ndim - 1))

    small_out = (small, BF, whole(small))
    large_out = (large, BF, along(small, 3))
    sums_out = ((8, LANES), F32, whole((8, LANES)))
    sums_wide = ((8, out), F32, along((8, LANES), 1))
    acc = pltpu.VMEM(small, F32)

    count_row = jnp.concatenate(
        [
            jnp.broadcast_to(jnp.sum(onehot_int[g]).astype(F32), (1, 128))
            for g in range(GROUPS)
        ]
        + [jnp.zeros((1, LANES - 128 * GROUPS), F32)],
        axis=1,
    )
    z1, sums1 = call(
        k_first, "first", half,
        [(x, along((2, full, images, wide), 0)), w_reduce.moving_all(), fixed(limits_in), fixed(onehot),
         fixed(count_row)],
        [((full, full, images, mid), BF, along((2, full, images, mid), 0)), sums_out],
        [pltpu.VMEM((2, images, mid), F32)], flops=2 * rows_in * wide * mid,
    )
    sums1, z1, *line = after(sums1, z1, *line)
    sums1, *line = after(sum_everywhere(sums1), *line)
    low, high = split_rows(line_gather_end(line))
    low, high, early_array, z1 = after(low, high, early_array, z1)
    w_spatial, w_expand = views(early_array, first_weights)
    low, high = gather_bit(low, 2, 1), gather_bit(high, 1, 2)
    tables_flat = early_array[:, -table_rows:].reshape(shards, -1)[:, : table_cells.size]
    tables_flat = tables_flat.reshape((shards,) + table_cells.shape)
    tables, at = [], 0
    for t in tables_all:
        width = t.shape[2]
        field = tables_flat[:, :, at : at + width].transpose(1, 0, 2)
        tables.append(field.reshape(2 * GROUPS, shards * width).astype(F32))
        at += width
    totals = sums1[2 * GROUPS, 0 : 128 * GROUPS : 128]
    side_real = group_side.astype(F32)
    half_real = (group_side // 2).astype(F32)
    counts_in = jnp.broadcast_to((totals * side_real * side_real)[:, None], (GROUPS, LANES))
    counts = jnp.broadcast_to((totals * half_real * half_real)[:, None], (GROUPS, LANES))
    counts_in, counts = fixed(counts_in), fixed(counts)
    onehot, gate = fixed(onehot), fixed(gate)
    limits_in, limits_out = fixed(limits_in), fixed(limits_out)
    keeps_in, keeps_out = fixed(keeps_in), fixed(keeps_out)

    z1_split = z1.reshape(split)
    row_split = (1, 2, half, 2, images, LANES)
    planes_shape = (2, 2, half + 1, half + 1, images, mid)
    planes, slope1, z2, sums2 = call(
        k_entry_spatial, "entry_spatial", half,
        [(z1_split, along(row_split, 0)), fixed(sums1), fixed(tables[0]), counts_in, counts,
         keeps_in, limits_out, onehot, w_spatial.every()],
        [(planes_shape, BF, whole(planes_shape)), (split, BF, along(row_split, 0)), small_out,
         sums_out],
        [acc], flops=18 * rows_out * mid * mid,
    )
    sums2, low, high = after(sums2, low, high)
    near, low, high = after(sum_near(sums2), low, high)
    low_other, high_other = xor_swap(low, 1 << 1), xor_swap(high, 1 << 2)
    sums2 = sum_far(near, LANES)
    a2, slope2, z3, sums3 = call(
        k_expand, "expand", blocks,
        [fixed(z2), fixed(sums2), fixed(tables[1]), counts, keeps_out, onehot,
         w_expand.moving()],
        [small_out, small_out, large_out, sums_wide], [acc], flops=2 * rows_out * mid * out,
    )
    z3, sums3, low_other, high_other = after(z3, sums3, low_other, high_other)
    low, high = pair(low, low_other, 1, 2), pair(high, high_other, 2, 1)
    values = [gather_bit(v, 0, 3) for v in (low, high)]
    gathered = jnp.concatenate(values, axis=4).reshape(devices, -1, LANES)
    w_project, w_ireduce = views(gathered, middle_weights)
    zs, sums_s = call(
        k_strided, "strided", blocks,
        [(x_split, whole((half, 1, half, 1, images, wide))), w_project.moving(), limits_out, onehot],
        [large_out, sums_wide], [acc], flops=2 * rows_out * wide * out,
    )
    joined = sum_everywhere(jnp.concatenate([sums3, sums_s], axis=1))
    sums3, sums_s = joined[:, :out], joined[:, out:]
    w_rows = w_ireduce.moving_rows(blocks)
    middle, slope3, z4, sums4 = call(
        k_middle, "middle", blocks,
        [column(z3), column(zs), column(sums3), column(sums_s), column(tables[2]),
         column(tables[3]), counts, limits_out, onehot, w_rows],
        [large_out, large_out, small_out, sums_out], [acc], flops=2 * rows_out * mid * out,
    )
    sums4 = sum_everywhere(sums4)
    padded_shape = (half + 2, half + 2, images, mid)
    padded4, slope4, z5, sums5 = call(
        k_inner_spatial, "inner_spatial", 1,
        [fixed(z4), fixed(sums4), fixed(tables[4]), counts, keeps_out, limits_out, onehot,
         w_ispatial.every()],
        [(padded_shape, BF, whole(padded_shape)), small_out, small_out, sums_out], [acc],
        flops=18 * rows_out * mid * mid,
    )
    sums5 = sum_everywhere(sums5)
    a5, slope5, z6, sums6 = call(
        k_expand, "inner_expand", blocks,
        [fixed(z5), fixed(sums5), fixed(tables[5]), counts, keeps_out, onehot,
         w_iexpand.moving()],
        [small_out, small_out, large_out, sums_wide], [acc], flops=2 * rows_out * mid * out,
    )
    sums6 = sum_everywhere(sums6)
    result, du6, back6 = call(
        k_close, "close", blocks,
        [column(z6), column(sums6), column(tables[6]), counts, limits_out, onehot, gate,
         column(middle), column(cot)],
        [large_out, large_out, sums_wide],
    )
    back6 = sum_everywhere(back6)
    dz6, du5, back5 = call(
        k_back_expand, "back_inner_expand", blocks,
        [column(du6), column(z6), column(sums6), column(back6), column(tables[6]), counts,
         limits_out, onehot, w_iexpand.moving(), fixed(slope5), fixed(z5), fixed(sums5)],
        [large_out, (small, F32, whole(small)), sums_out], [acc],
        flops=2 * rows_out * mid * out,
    )
    near, dz6 = after(sum_near(back5), dz6)
    back5 = sum_far(near, LANES)
    inner_grad, inner_rows = grads_into([inner_spatial, inner_expand])
    inner_grad(
        1, k_grad_columns, "inner_expand_grad", blocks, [fixed(a5), column(dz6)],
        2 * rows_out * mid * out, [pltpu.VMEM((mid, rows_out), BF)],
    )
    dz5, du4, back4 = call(
        k_back_inner_spatial, "back_inner_spatial", 1,
        [fixed(du5), fixed(z5), fixed(sums5), fixed(back5), fixed(tables[5]), counts, limits_out,
         onehot, w_ispatial.every(), fixed(slope4), fixed(z4), fixed(sums4)],
        [small_out, (small, F32, whole(small)), sums_out],
        [pltpu.VMEM(padded_shape, BF), acc], flops=18 * rows_out * mid * mid,
    )
    near, dz5 = after(sum_near(back4), dz5)
    inner_grad(
        0, k_taps, "inner_spatial_grad", 9, [fixed(padded4), fixed(dz5)], 18 * rows_out * mid * mid
    )
    late_rows, back4 = after(inner_rows().reshape(-1, LANES), sum_far(near, LANES))
    inner_own = lax.psum_scatter(late_rows, AXES, scatter_dimension=0, tiled=True)
    dz4, du3, back3 = call(
        k_back_middle, "back_middle", blocks,
        [fixed(du4), fixed(z4), fixed(sums4), fixed(back4), fixed(tables[4]), counts, limits_out,
         onehot, w_rows, gate, column(cot), column(du6), column(slope3), column(z3), column(zs),
         column(sums3), column(sums_s)],
        [small_out, large_out, ((16, out), F32, along((16, LANES), 1))], [acc],
        flops=2 * rows_out * mid * out,
    )
    near, dz4 = after(sum_near(back3), dz4)
    back3 = sum_far(near, out)
    middle_grads = [entry_project, inner_reduce, entry_expand]
    middle_grad, middle_rows = grads_into(middle_grads)
    middle_grad(
        1, k_grad, "inner_reduce_grad", blocks, [column(middle), fixed(dz4)],
        2 * rows_out * mid * out,
    )
    dz3, dzs, du2, back2 = call(
        k_back_entry_expand, "back_entry_expand", blocks,
        [column(du3), column(z3), column(zs), column(sums3), column(sums_s), column(back3),
         column(tables[2]), column(tables[3]), counts, limits_out, onehot, w_expand.moving(),
         fixed(slope2), fixed(z2), fixed(sums2)],
        [large_out, large_out, (small, F32, whole(small)), sums_out], [acc],
        flops=2 * rows_out * mid * out,
    )
    near, dz3, dzs = after(sum_near(back2), dz3, dzs)
    back2 = sum_far(near, LANES)
    middle_grad(
        2, k_grad_columns, "expand_grad", blocks, [fixed(a2), column(dz3)],
        2 * rows_out * mid * out, [pltpu.VMEM((mid, rows_out), BF)],
    )
    middle_grad(
        0, k_grad_strided, "project_grad", blocks,
        [(x_split, whole((half, 1, half, 1, images, wide))), column(dzs)],
        2 * rows_out * wide * out, [pltpu.VMEM((wide, rows_out), BF)],
    )
    low, high = cut_rows(halve_bit([[near_shape(middle_rows())]], 0, 3))
    low_sent, high_sent, back2 = after(halve_sent(low, 1, 2), halve_sent(high, 2, 1), back2)
    low, high = halve_end(low, low_sent, 1, 2), halve_end(high, high_sent, 2, 1)
    strided_shape = (half, half, images, wide)
    (d_strided,) = call(
        k_back_strided, "back_strided", blocks, [column(dzs), w_project.moving()],
        [(strided_shape, F32, whole(strided_shape))], flops=2 * rows_out * wide * out,
    )
    plane = (half, 1, half, 1, images, LANES)

    def parity(array):
        return (array, pl.BlockSpec(plane, lambda s: (0, s // 2, 0, s % 2, 0, 0)))

    dz2, du1, back1 = call(
        k_back_entry_spatial, "back_entry_spatial", 4,
        [fixed(du2), fixed(z2), fixed(sums2), fixed(back2), fixed(tables[1]), counts, counts_in,
         limits_out, onehot, w_spatial.every(), parity(slope1), parity(z1_split), fixed(sums1)],
        [small_out, (split, BF, parity(z1_split)[1]), sums_out],
        [pltpu.VMEM((half + 1, half + 1, images, mid), BF), pltpu.VMEM((2, images, mid), F32), acc],
        flops=18 * rows_out * mid * mid,
    )
    (g_spatial,) = call(
        k_taps_strided, "entry_spatial_grad", 9, [fixed(planes), fixed(dz2)],
        [grad_out(entry_spatial, 9)],
        flops=18 * rows_out * mid * mid,
    )
    spatial_rows = [[near_shape(grad_rows(g_spatial, entry_spatial))]]
    spatial_sent = halve_sent(spatial_rows, 0, 3)
    back1, low_sent, high_sent, spatial_sent, d_strided = after(
        back1, halve_sent(low, 2, 1), halve_sent(high, 1, 2), spatial_sent, d_strided
    )
    near, low_sent, high_sent = after(sum_near(back1), low_sent, high_sent)
    low, high = halve_end(low, low_sent, 2, 1), halve_end(high, high_sent, 1, 2)
    back1 = sum_far(near, LANES)
    spatial_rows = halve_end(spatial_rows, spatial_sent, 0, 3)
    two = (2, full, images, mid)
    taps, q = layout(entry_reduce)
    flat_shape = (devices, q, LANES) if q % 16 == 0 else (devices * q, LANES)
    dz1, g_reduce = call(
        k_back_first, "back_first", half,
        [(du1.reshape(z1.shape), along(two, 0)), (z1, along(two, 0)), fixed(sums1), fixed(back1),
         fixed(tables[0]), counts_in, limits_in, onehot, (x, along((2, full, images, wide), 0))],
        [(z1.shape, BF, along(two, 0)), (flat_shape, BF, whole(flat_shape))],
        [pltpu.VMEM((wide, mid), F32)], flops=2 * rows_in * wide * mid,
    )
    first_rows = [[added(v).astype(BF)] for v in low + high]
    first_rows, g_reduce, dz1, inner_own = flat_after(first_rows, g_reduce, dz1, inner_own)
    reduce_rows = halve_bit([[near_shape(grad_rows(g_reduce, entry_reduce))]], 0, 3)
    low, high = cut_rows(spatial_rows + reduce_rows)
    first_rows, low_sent, high_sent, dz1 = flat_after(
        first_rows, halve_sent(low, 1, 2), halve_sent(high, 2, 1), dz1
    )
    low, high = halve_end(low, low_sent, 1, 2), halve_end(high, high_sent, 2, 1)
    entry_own = far_scatter(first_rows)
    (d_inputs,) = call(
        k_input_grad, "input_grad", half,
        [(dz1, along(two, 0)), w_reduce.moving_all(),
         (d_strided, along((1, half, images, wide), 0))],
        [((full, full, images, wide), F32, along((2, full, images, wide), 0))],
        flops=2 * rows_in * wide * mid,
    )
    entry_own, low_sent, high_sent, d_inputs, inner_own = after(
        entry_own, halve_sent(low, 2, 1), halve_sent(high, 1, 2), d_inputs, inner_own
    )
    low, high = halve_end(low, low_sent, 2, 1), halve_end(high, high_sent, 1, 2)
    early_own = jnp.concatenate([entry_own, inner_own], axis=0).reshape(1, 1, -1, LANES)
    early_own = gather_copy(early_own, 1)
    last_rows = [[added(v).astype(BF)] for v in low + high]
    early_own, last_rows = flat_after(early_own, last_rows)
    last_own = far_scatter(last_rows)
    g_project, g_ireduce, g_expand, g_ispatial, g_iexpand = shares(
        gather_copy(early_own, 0), middle_grads + [inner_spatial, inner_expand]
    )
    last_own, g_project, g_ireduce, g_expand, g_ispatial, g_iexpand = after(
        last_own, g_project, g_ireduce, g_expand, g_ispatial, g_iexpand
    )
    last_own = gather_copy(last_own.reshape(1, 1, -1, LANES), 1)
    g_spatial, g_reduce = shares(gather_copy(last_own, 0), [entry_spatial, entry_reduce])

    def own_share(back, gain_at=0):
        width = back.shape[1] // shards
        own = lax.dynamic_slice_in_dim(back, position * width, width, 1)
        return jnp.stack([own[gain_at : gain_at + GROUPS], own[GROUPS : 2 * GROUPS]])

    return (
        result.transpose(2, 0, 1, 3),
        d_inputs.transpose(2, 0, 1, 3),
        g_reduce,
        g_spatial,
        g_expand,
        g_project,
        own_share(back1),
        own_share(back2),
        own_share(back3),
        own_share(back3, 2 * GROUPS),
        g_ireduce,
        g_ispatial,
        g_iexpand,
        own_share(back4),
        own_share(back5),
        own_share(back6),
    )


def solution(mesh):
    images = P(("dp", "rep"), None, None, None)
    rows = P("dp", None)
    taps = P(None, "dp", None)
    table = P(None, None, "dp")
    entry = (rows, taps, rows, rows, table, table, table, table)
    inner = (rows, taps, rows, table, table, table)
    return jax.shard_map(
        body,
        mesh=mesh,
        in_specs=(images, images, P(("dp", "rep")), P(), P(), P(), *entry, *inner),
        out_specs=(images, images, *entry, *inner),
        check_vma=False,
    )
```
